128 devices in a mesh: dp: 2 (over z_lo), seq: 8 (over z_hi, x), col: 8 (over y, core).
Axes of the slice: x: 4, y: 4, z: 4 (z_hi: 2, z_lo: 2; z = z_hi * 2 + z_lo), core: 2. Of those that a mesh axis runs over, the one named last changes fastest.
Arguments:
- inputs: bfloat16 [2, 4096, 1024], P('dp', 'seq'), may hold values from -6 to 6
- cotangent: bfloat16 [2, 4096, 1024], P('dp', 'seq'), may hold values from -6 to 6
- norm_gain: float32 [1024], replicated, may hold values from 0.1 to 1.9
- proj_in: bfloat16 [4, 1024, 1024], P(None, None, 'col'), may hold values from -0.1875 to 0.1875
- proj_out: bfloat16 [1024, 1024], P('col'), may hold values from -0.1875 to 0.1875
- item_ids: int32 [2, 4096], P('dp', 'seq'), may hold values from 0 to 16383
- lengths: int32 [2], P('dp'), may hold values from 128 to 4096, as said below
- tile_mask: int32 [2, 32, 32], P('dp'), may hold values from 0 to 1, as said below
Outputs:
- grad_proj_in: float32 [4, 1024, 1024], P(None, None, 'col')
- grad_proj_out: float32 [1024, 1024], P('col')
- grad_gain: float32 [1024], P('col')
- table_grad: float32 [16384, 1024], P(('dp', 'seq'), 'col')
The draws below stay inside these ranges and needn't reach their ends.
Inputs may be any that keep to these rules, and one draw needn't show every extreme that they name: `lengths`: each length is a multiple of 128; some user has exactly 4096. `tile_mask`: tiles above the diagonal are 0, diagonal tiles are 1, tiles below the diagonal are 0 or 1.
All inputs are finite; a program needn't handle non-finite values.
Results may differ from the reference program's by a relative error of at most 0.006.
Values may be sent and summed in bfloat16 or wider, within the bound.
No kernel may reach another device: no remote copies, remote signals or barrier semaphores. Data moves between devices by JAX's collectives and lax.ppermute only.
A program may use at most 64 MiB of HBM per device.

```python
import math
import jax
import jax.numpy as jnp
import numpy as np
from jax import lax

D = 1024
HEADS = 8
BLOCK = 128
TOK_DEV = 512
USERS = 2
LEN = 4096
NBLK = 32
VOCAB = 16384


def draw_lengths(key, part):
    key = jax.random.fold_in(key, 11)
    pick_key, size_key = jax.random.split(key)
    blocks = jax.random.randint(size_key, (USERS,), 1, NBLK + 1)
    full_user = jax.random.randint(pick_key, (), 0, USERS)
    blocks = jnp.where(jnp.arange(USERS) == full_user, NBLK, blocks)
    return (blocks * BLOCK).astype(jnp.int32)


def draw_tile_mask(key, part):
    key = jax.random.fold_in(key, 23)
    coin_flips = jax.random.randint(key, (USERS, NBLK, NBLK), 0, 2)
    row_pos = jnp.arange(NBLK)[:, None]
    col_pos = jnp.arange(NBLK)[None, :]
    below = (col_pos < row_pos).astype(jnp.int32)
    on_diag = (col_pos == row_pos).astype(jnp.int32)
    return (coin_flips * below[None] + on_diag[None]).astype(jnp.int32)


def touch_ends(drawn, key, smallest, top_value):
    spot = [jax.random.randint(jax.random.fold_in(key, axis), (), 0, length) for axis, length in enumerate(drawn.shape)]
    main_axis = drawn.shape.index(max(drawn.shape))
    neighbour = spot[:main_axis] + [(spot[main_axis] + 1) % drawn.shape[main_axis]] + spot[main_axis + 1:]
    return drawn.at[tuple(spot)].set(smallest).at[tuple(neighbour)].set(top_value)


def levels(rng, dims, cuts, least, high):
    factor_of = 1.0
    for dim, blocks in cuts:
        steps = jax.random.uniform(jax.random.fold_in(jax.random.fold_in(rng, 6), dim), (blocks,), jnp.float32, least / len(cuts), high / len(cuts))
        factor_of = factor_of * jnp.repeat(jnp.exp(steps), dims[dim] // blocks).reshape((-1,) + (1,) * (len(dims) - 1 - dim))
    return factor_of


def cumulative_ranks(amount, slope):
    weights = [(1 << 20) // math.isqrt(standing ** slope) + 1 for standing in range(1, amount + 1)]
    width = 1 + sum(weights) // (1 << 30)
    return np.cumsum(np.array([max(1, weight // width) for weight in weights]))


def ranked_ids(stream_key, shape, count, lean):
    listing = cumulative_ranks(count, lean)
    ticket = jax.random.randint(jax.random.fold_in(stream_key, 1), shape, 0, int(listing[count - 1]))
    rank = jnp.searchsorted(jnp.asarray(listing, jnp.int32), ticket, side="right")
    return jax.random.permutation(jax.random.fold_in(stream_key, 2), count)[rank].astype(jnp.int32)


def gaussian(stream_key, dims, scale, reach, cuts=(), kind=jnp.bfloat16):
    factor_of = levels(stream_key, dims, cuts, -0.22, 0.18) if cuts else 1.0
    result = jax.random.normal(stream_key, dims, jnp.float32) * scale * factor_of
    return jnp.minimum(jnp.maximum(result, -reach), reach).astype(kind)


def setup_inputs(seed: int = 0) -> dict:
    key_of = jax.random.split(jax.random.key(seed), 9)
    inputs = gaussian(key_of[0], (USERS, LEN, D), 1.0, 6.0, ((0, 2), (1, 8)))
    cotangent = gaussian(key_of[1], (USERS, LEN, D), 1.0, 6.0, ((0, 2), (1, 8)))
    norm_gain = jnp.clip(1.0 + 0.18 * jax.random.normal(key_of[2], (D,), jnp.float32), 0.1, 1.9)
    proj_in = gaussian(key_of[3], (4, D, D), D ** -0.5, 0.1875, ((2, 8),))
    proj_out = gaussian(key_of[4], (D, D), D ** -0.5, 0.1875, ((0, 8),))
    item_ids = touch_ends(ranked_ids(key_of[5], (USERS, LEN), VOCAB, 2), jax.random.fold_in(key_of[5], 3), 0, VOCAB - 1).astype(jnp.int32)
    lengths = draw_lengths(jax.random.fold_in(key_of[8], 71), 0)
    tile_mask = draw_tile_mask(jax.random.fold_in(key_of[8], 71), 0)
    return {"inputs": inputs, "cotangent": cotangent, "norm_gain": norm_gain, "proj_in": proj_in, "proj_out": proj_out, "item_ids": item_ids, "lengths": lengths, "tile_mask": tile_mask}


EPSILON = 1e-06

def block_counts(tile_grid, length, q_first, row_count):
    nblocks = tile_grid.shape[1]
    tile_part = lax.dynamic_slice_in_dim(tile_grid, q_first // BLOCK, row_count // BLOCK, 0).astype(jnp.float32)
    blocks = jnp.arange(nblocks, dtype=jnp.int32)
    filled = jnp.clip(length - BLOCK * blocks, 0, BLOCK).astype(jnp.float32)
    own_block = q_first // BLOCK + jnp.arange(row_count // BLOCK, dtype=jnp.int32)
    earlier_mask = (blocks[None, :] < own_block[:, None]).astype(jnp.float32)
    earlier = lax.optimization_barrier(jnp.sum(tile_part * earlier_mask * filled[None, :], axis=1))
    positions = q_first + jnp.arange(row_count, dtype=jnp.int32)
    diagonal = jnp.minimum(positions % BLOCK + 1, jnp.clip(length - BLOCK * (positions // BLOCK), 0, BLOCK))
    return jnp.maximum(jnp.repeat(earlier, BLOCK) + diagonal.astype(jnp.float32), 1.0)

def tile_weights(tile_grid, length, counts, q_first, row_count, key_first, col_count):
    key_first = jnp.asarray(key_first, jnp.int32)
    tile_part = lax.dynamic_slice(tile_grid, (q_first // BLOCK, key_first // BLOCK), (row_count // BLOCK, col_count // BLOCK)).astype(jnp.float32)
    expanded = jnp.repeat(jnp.repeat(tile_part, BLOCK, axis=0), BLOCK, axis=1)
    query_pos = q_first + jnp.arange(row_count, dtype=jnp.int32)
    key_pos = key_first + jnp.arange(col_count, dtype=jnp.int32)
    allowed = (key_pos[None, :] <= query_pos[:, None]) & (key_pos[None, :] < length)
    return jnp.where(allowed, expanded, 0.0) / counts[:, None]

def user_grads(rows_in, incoming, norm_gain, proj_in, proj_out, length, tile_grid, score_scale):
    full_len, model_width = rows_in.shape
    head_size = model_width // HEADS
    rows_f32 = rows_in.astype(jnp.float32)
    inv_rms = lax.rsqrt(lax.optimization_barrier(jnp.mean(rows_f32 * rows_f32, axis=1, keepdims=True)) + EPSILON)
    normed = (rows_f32 * inv_rms * norm_gain).astype(jnp.bfloat16)
    pre_acts = jnp.einsum('td,cde->cte', normed.astype(jnp.float32), proj_in.astype(jnp.float32))
    activated = (pre_acts * jax.nn.sigmoid(pre_acts)).astype(jnp.bfloat16)
    is_valid = jnp.arange(full_len, dtype=jnp.int32) < length
    grad_out = jnp.where(is_valid[:, None], incoming, jnp.zeros_like(incoming))
    shaped = activated.reshape(4, full_len, HEADS, head_size)
    query_act = shaped[1].astype(jnp.float32)
    key_act = shaped[2].astype(jnp.float32)
    value_act = shaped[3].astype(jnp.float32)
    nblocks = full_len // TOK_DEV

    def forward(block_index):
        q_first = block_index * TOK_DEV
        query_here = lax.dynamic_slice_in_dim(query_act, q_first, TOK_DEV, 0)
        counts = block_counts(tile_grid, length, q_first, TOK_DEV)
        weights = tile_weights(tile_grid, length, counts, q_first, TOK_DEV, 0, full_len)
        logits = jnp.einsum('thd,jhd->htj', query_here, key_act) * score_scale
        probs = (logits * jax.nn.sigmoid(logits) * weights[None]).astype(jnp.bfloat16)
        return jnp.einsum('htj,jhd->thd', probs.astype(jnp.float32), value_act)
    attended = lax.map(forward, jnp.arange(nblocks, dtype=jnp.int32)).reshape(full_len, model_width)
    update_act = activated[0].astype(jnp.float32)
    mixed_out = (attended * update_act).astype(jnp.bfloat16)
    d_mixed = jnp.dot(grad_out, proj_out.T, preferred_element_type=jnp.float32)
    grad_out_w = jnp.dot(mixed_out.T, grad_out, preferred_element_type=jnp.float32)
    d_attended = (d_mixed * update_act).astype(jnp.bfloat16).reshape(full_len, HEADS, head_size).astype(jnp.float32)
    d_update = d_mixed * attended

    def backward(state_now, block_index):
        d_key, d_value = state_now
        q_first = block_index * TOK_DEV
        query_here = lax.dynamic_slice_in_dim(query_act, q_first, TOK_DEV, 0)
        d_att_here = lax.dynamic_slice_in_dim(d_attended, q_first, TOK_DEV, 0)
        counts = block_counts(tile_grid, length, q_first, TOK_DEV)
        weights = tile_weights(tile_grid, length, counts, q_first, TOK_DEV, 0, full_len)
        logits = jnp.einsum('thd,jhd->htj', query_here, key_act) * score_scale
        sigmoid_s = jax.nn.sigmoid(logits)
        probs = (logits * sigmoid_s * weights[None]).astype(jnp.bfloat16).astype(jnp.float32)
        d_probs = jnp.einsum('thd,jhd->htj', d_att_here, value_act)
        d_logits = (d_probs * weights[None] * sigmoid_s * (1.0 + logits * (1.0 - sigmoid_s)) * score_scale).astype(jnp.bfloat16).astype(jnp.float32)
        d_query = jnp.einsum('htj,jhd->thd', d_logits, key_act)
        d_key = d_key + jnp.einsum('htj,thd->jhd', d_logits, query_here)
        d_value = d_value + jnp.einsum('htj,thd->jhd', probs, d_att_here)
        return ((d_key, d_value), d_query)
    blank_acc = jnp.zeros((full_len, HEADS, head_size), jnp.float32)
    (d_key, d_value), d_query = lax.scan(backward, (blank_acc, blank_acc), jnp.arange(nblocks, dtype=jnp.int32))
    d_acts = jnp.stack([d_update, d_query.reshape(full_len, model_width), d_key.reshape(full_len, model_width), d_value.reshape(full_len, model_width)])
    sigmoid_p = jax.nn.sigmoid(pre_acts)
    d_pre = (d_acts * sigmoid_p * (1.0 + pre_acts * (1.0 - sigmoid_p))).astype(jnp.bfloat16).astype(jnp.float32)
    grad_in_w = jnp.einsum('td,cte->cde', normed.astype(jnp.float32), d_pre)
    d_normed = jnp.einsum('cte,cde->td', d_pre, proj_in.astype(jnp.float32))
    grad_gain = lax.optimization_barrier(jnp.sum(d_normed * rows_f32 * inv_rms, axis=0))
    scaled = d_normed * norm_gain
    d_inputs = inv_rms * (scaled - rows_f32 * inv_rms * inv_rms * lax.optimization_barrier(jnp.mean(scaled * rows_f32, axis=1, keepdims=True))) + grad_out.astype(jnp.float32)
    return (grad_in_w, grad_out_w, grad_gain, d_inputs.astype(jnp.bfloat16))

def reference(inputs, cotangent, norm_gain, proj_in, proj_out, item_ids, lengths, tile_mask):
    model_width = inputs.shape[2]
    score_scale = 1.0 / (model_width // HEADS) ** 0.5
    total_in = jnp.zeros(proj_in.shape, jnp.float32)
    total_out = jnp.zeros(proj_out.shape, jnp.float32)
    total_gain = jnp.zeros((model_width,), jnp.float32)
    table_grad = jnp.zeros((VOCAB, model_width), jnp.float32)
    for user in range(inputs.shape[0]):
        grad_in_w, grad_out_w, grad_gain, d_inputs = user_grads(inputs[user], cotangent[user], norm_gain, proj_in, proj_out, lengths[user], tile_mask[user], score_scale)
        total_in = total_in + grad_in_w
        total_out = total_out + grad_out_w
        total_gain = total_gain + grad_gain
        table_grad = table_grad + jax.ops.segment_sum(d_inputs.astype(jnp.float32), item_ids[user], num_segments=VOCAB)
    return (total_in, total_out, total_gain, table_grad)
```

```python
import functools
import math

import jax
import jax.numpy as jnp
from jax import lax
from jax.experimental import pallas as pl
from jax.experimental.pallas import tpu as pltpu
from jax.sharding import PartitionSpec as P

BLOCK = 128
EPSILON = 1e-06
BF16 = jnp.bfloat16
F32 = jnp.float32
VMEM_LIMIT = 48 * 1024 * 1024
EXTRA = 16
NT = (((1,), (1,)), ((), ()))
TN = (((0,), (0,)), ((), ()))


def kernel_call(body, out_shape, name, flops=0, bytes_accessed=0, **kwargs):
    return pl.pallas_call(
        body,
        out_shape=out_shape,
        name=name,
        compiler_params=pltpu.CompilerParams(vmem_limit_bytes=VMEM_LIMIT),
        cost_estimate=pl.CostEstimate(flops=flops, bytes_accessed=bytes_accessed, transcendentals=0),
        **kwargs,
    )


def shape_of(shape, dtype):
    return jax.ShapeDtypeStruct(shape, dtype)


def plane_perm(dz, dx):
    pairs = []
    for z in range(4):
        for x in range(4):
            z2, x2 = (z + dz) % 4, (x + dx) % 4
            source = (z % 2) * 8 + (z // 2) * 4 + x
            target = (z2 % 2) * 8 + (z2 // 2) * 4 + x2
            pairs.append((source, target))
    return pairs


def move_plane(value, dz, dx):
    return lax.ppermute(value, ("dp", "seq"), plane_perm(dz, dx))


def move_seq(value, dz_hi, dx):
    pairs = [(i, ((i // 4 + dz_hi) % 2) * 4 + (i % 4 + dx) % 4) for i in range(8)]
    return lax.ppermute(value, "seq", pairs)


def move_y(value, dy):
    return lax.ppermute(value, "col", [(i, ((i // 2 + dy) % 4) * 2 + i % 2) for i in range(8)])


def move_core(value):
    return lax.ppermute(value, "col", [(i, i ^ 1) for i in range(8)])


def gather_plane(value):
    line = jnp.concatenate([value] + [move_plane(value, 0, k) for k in (1, 3, 2)], axis=0)
    return [line] + [move_plane(line, k, 0) for k in (1, 3, 2)]


def project_body(where, x_ref, cot_ref, gain_ref, proj_ref, out_ref, mask_ref,
                 qd_ref, kv_ref, pre_ref, normed_ref, grad_ref, dmix_ref, upd_ref, inv_cnt_ref, inv_rms_ref):
    first_tile, length = where[0], where[1]
    tile = first_tile + pl.program_id(0)
    x = x_ref[...].astype(F32)
    inv_rms = lax.rsqrt(jnp.mean(x * x, axis=1, keepdims=True) + EPSILON)
    normed = (x * inv_rms * gain_ref[...]).astype(BF16)
    normed_ref[...] = normed
    inv_rms_ref[...] = jnp.broadcast_to(inv_rms, inv_rms_ref.shape)
    acts = []
    for c in range(4):
        pre = jnp.dot(normed, proj_ref[c], preferred_element_type=F32)
        pre_ref[c] = pre
        acts.append((pre * jax.nn.sigmoid(pre)).astype(BF16))
    local = lax.broadcasted_iota(jnp.int32, (BLOCK, 1), 0)
    valid = (tile * BLOCK + local) < length
    grad = jnp.where(valid, cot_ref[...].astype(F32), 0.0).astype(BF16)
    grad_ref[...] = grad
    d_mixed = lax.dot_general(grad, out_ref[...], NT, preferred_element_type=F32)
    dmix_ref[...] = d_mixed
    upd_ref[...] = acts[0]
    tiles = mask_ref.shape[0]
    rows = lax.broadcasted_iota(jnp.int32, (tiles, tiles), 0)
    cols = lax.broadcasted_iota(jnp.int32, (tiles, tiles), 1)
    filled = jnp.clip(length - BLOCK * cols, 0, BLOCK)
    picked = jnp.where((rows == tile) & (cols < tile), mask_ref[...] * filled, 0).astype(F32)
    earlier = jnp.sum(jnp.sum(picked, axis=1, keepdims=True), axis=0, keepdims=True)
    diagonal = jnp.minimum(local + 1, jnp.clip(length - BLOCK * tile, 0, BLOCK)).astype(F32)
    inv_cnt = 1.0 / jnp.maximum(earlier + diagonal, 1.0)
    inv_cnt_ref[...] = jnp.broadcast_to(inv_cnt, inv_cnt_ref.shape)
    qd_ref[0] = acts[1]
    qd_ref[1] = (d_mixed * acts[0].astype(F32) * inv_cnt).astype(BF16)
    kv_ref[0] = acts[2]
    kv_ref[1] = acts[3]


def project(where, x, cot, gain, proj_in, proj_out, mask):
    tok, width = x.shape
    col = proj_in.shape[2]
    steps = tok // BLOCK
    row = lambda i, w: (i, 0)
    side = lambda i, w: (0, i, 0)
    fixed2 = lambda i, w: (0, 0)
    return kernel_call(
        project_body,
        (
            shape_of((2, tok, col), BF16),
            shape_of((2, tok, col), BF16),
            shape_of((4, tok, col), F32),
            shape_of((tok, width), BF16),
            shape_of((tok, width), BF16),
            shape_of((tok, col), F32),
            shape_of((tok, col), BF16),
            shape_of((tok, col), F32),
            shape_of((tok, col), F32),
        ),
        "project",
        grid_spec=pltpu.PrefetchScalarGridSpec(
            num_scalar_prefetch=1,
            grid=(steps,),
            in_specs=[
                pl.BlockSpec((BLOCK, width), row),
                pl.BlockSpec((BLOCK, width), row),
                pl.BlockSpec((1, width), fixed2),
                pl.BlockSpec((4, width, col), lambda i, w: (0, 0, 0)),
                pl.BlockSpec((col, width), fixed2),
                pl.BlockSpec(mask.shape, fixed2),
            ],
            out_specs=[
                pl.BlockSpec((2, BLOCK, col), side),
                pl.BlockSpec((2, BLOCK, col), side),
                pl.BlockSpec((4, BLOCK, col), side),
                pl.BlockSpec((BLOCK, width), row),
                pl.BlockSpec((BLOCK, width), row),
                pl.BlockSpec((BLOCK, col), row),
                pl.BlockSpec((BLOCK, col), row),
                pl.BlockSpec((BLOCK, col), row),
                pl.BlockSpec((BLOCK, col), row),
            ],
        ),
    )(where, x, cot, gain.reshape(1, -1), proj_in, proj_out, mask)


def block_terms(a1, a2, b1, b2, keep, scale):
    half = lax.dot_general(a1, b1, NT, preferred_element_type=F32) * (keep * (0.5 * scale))
    other = lax.dot_general(a2, b2, NT, preferred_element_type=F32) * keep
    tanh = jnp.tanh(half)
    twice = 1.0 + tanh
    probs = half * twice
    slope = (other * (twice + probs * (1.0 - tanh))).astype(BF16)
    first = jnp.dot(probs.astype(BF16), b2, preferred_element_type=F32)
    second = jnp.dot(slope, b1, preferred_element_type=F32)
    return first, second


def own_body(qd_ref, kv_ref, keep_ref, acc_ref, *, scale):
    tok = qd_ref.shape[1]
    for side in range(2):
        a, b = (qd_ref, kv_ref) if side == 0 else (kv_ref, qd_ref)
        for tile in range(tok // BLOCK):
            rows = pl.ds(tile * BLOCK, BLOCK)
            keep = jnp.broadcast_to(keep_ref[side, pl.ds(tile, 1), :], (BLOCK, tok))
            row = lax.broadcasted_iota(jnp.int32, (BLOCK, tok), 0) + tile * BLOCK
            col = lax.broadcasted_iota(jnp.int32, (BLOCK, tok), 1)
            ordered = (col <= row) if side == 0 else (row <= col)
            keep = jnp.where(ordered, keep, 0.0)
            first, second = block_terms(a[0, rows], a[1, rows], b[0], b[1], keep, scale)
            acc_ref[side, 0, rows] = first
            acc_ref[side, 1, rows] = second


def own_terms(qd, kv, keep, scale):
    _, tok, col = qd.shape
    return kernel_call(
        functools.partial(own_body, scale=scale),
        shape_of((2, 2, tok, col), F32),
        "own_terms",
        flops=2 * 8 * tok * tok * col,
        bytes_accessed=4 * tok * col * 8,
    )(qd, kv, keep)


def far_body(side_ref, qd_ref, kv_ref, keep_ref, *refs, count, scale):
    others, acc_in, acc_ref = refs[:count], refs[count], refs[count + 1]
    tok = qd_ref.shape[1]
    acc_ref[...] = acc_in[...]
    for index in range(count):
        other = others[index]
        for side in range(2):
            own = qd_ref if side == 0 else kv_ref

            @pl.when(side_ref[index] == side)
            def _():
                for tile in range(tok // BLOCK):
                    rows = pl.ds(tile * BLOCK, BLOCK)
                    keep = keep_ref[index, pl.ds(tile, 1), :]
                    first, second = block_terms(own[0, rows], own[1, rows], other[0], other[1], keep, scale)
                    acc_ref[side, 0, rows] += first
                    acc_ref[side, 1, rows] += second


def far_terms(sides, qd, kv, keep, others, acc, scale, name):
    _, tok, col = qd.shape
    count = len(others)
    whole = pl.BlockSpec(memory_space=pltpu.VMEM)
    return kernel_call(
        functools.partial(far_body, count=count, scale=scale),
        shape_of(acc.shape, F32),
        name,
        flops=2 * 4 * tok * tok * col * count,
        bytes_accessed=4 * tok * col * 8,
        in_specs=[pl.BlockSpec(memory_space=pltpu.SMEM)] + [whole] * (4 + count),
        out_specs=whole,
        input_output_aliases={4 + count: 0},
    )(sides, qd, kv, keep, *others, acc)


def pre_grad_body(acc_ref, pre_ref, dmix_ref, upd_ref, inv_cnt_ref, inv_rms_ref, d_ref, mixed_ref, *, scale):
    tok, col = dmix_ref.shape
    stat = jnp.zeros((tok, col), F32)
    attended = acc_ref[0, 0] * inv_cnt_ref[...]
    mixed_ref[...] = (attended * upd_ref[...].astype(F32)).astype(BF16)
    grads = (
        dmix_ref[...] * attended,
        acc_ref[0, 1] * (0.5 * scale),
        acc_ref[1, 1] * (0.5 * scale),
        acc_ref[1, 0],
    )
    for c in range(4):
        pre = pre_ref[c]
        sig = jax.nn.sigmoid(pre)
        d_pre = (grads[c] * sig * (1.0 + pre * (1.0 - sig))).astype(BF16)
        d_ref[pl.ds(0, tok), pl.ds(c * col, col)] = d_pre
        stat = stat + d_pre.astype(F32) * pre
    stat = stat / inv_rms_ref[...]
    high = stat.astype(BF16)
    low = (stat - high.astype(F32)).astype(BF16)
    ones = jnp.ones((8, col), BF16)
    sums = lax.dot_general(ones, high, NT, preferred_element_type=F32)
    sums = sums + lax.dot_general(ones, low, NT, preferred_element_type=F32)
    d_ref[pl.ds(tok, EXTRA), :] = two_rows(sums[0:1])


def two_rows(value):
    high = value.astype(BF16).astype(F32)
    low = value - high
    row = lax.broadcasted_iota(jnp.int32, (EXTRA, value.shape[1]), 0)
    both = jnp.where(row == 0, jnp.broadcast_to(high, row.shape), jnp.where(row == 1, jnp.broadcast_to(low, row.shape), 0.0))
    return both.astype(BF16)


def pre_grads(acc, pre, dmix, upd, inv_cnt, inv_rms, scale):
    tok, col = dmix.shape
    return kernel_call(
        functools.partial(pre_grad_body, scale=scale),
        (shape_of((tok + EXTRA, 4 * col), BF16), shape_of((tok, col), BF16)),
        "pre_grads",
        bytes_accessed=tok * col * 48,
    )(acc, pre, dmix, upd, inv_cnt, inv_rms)


def back_body(own_ref, peer_ref, w_own_ref, w_peer_ref, *outs):
    tok = own_ref.shape[0] - EXTRA
    part = lax.dot_general(own_ref[pl.ds(0, tok), :], w_own_ref[...], NT, preferred_element_type=F32)
    part = part + lax.dot_general(peer_ref[pl.ds(0, tok), :], w_peer_ref[...], NT, preferred_element_type=F32)
    sums = jnp.sum(
        own_ref[pl.ds(tok, EXTRA), :].astype(F32) + peer_ref[pl.ds(tok, EXTRA), :].astype(F32), axis=0, keepdims=True
    )
    high = sums.astype(BF16).astype(F32)
    low = sums - high
    col = outs[0].shape[1]
    row = lax.broadcasted_iota(jnp.int32, (EXTRA, col), 0)
    extra = jnp.zeros((EXTRA, col), F32)
    for tile in range(tok // BLOCK):
        span = slice(tile * BLOCK, (tile + 1) * BLOCK)
        extra = jnp.where(row == 4 * tile, jnp.broadcast_to(high[:, span], row.shape), extra)
        extra = jnp.where(row == 4 * tile + 1, jnp.broadcast_to(low[:, span], row.shape), extra)
    extra = extra.astype(BF16)
    for k, out in enumerate(outs):
        out[pl.ds(0, tok), :] = part[:, k * col:(k + 1) * col].astype(BF16)
        out[pl.ds(tok, EXTRA), :] = extra


def back_project(own, peer, w_own, w_peer, col):
    rows, depth = own.shape
    return kernel_call(
        back_body,
        tuple(shape_of((rows, col), BF16) for _ in range(4)),
        "back_project",
        flops=4 * rows * depth * w_own.shape[0],
        bytes_accessed=rows * depth * 8,
    )(own, peer, w_own, w_peer)


def weight_body(where, normed_t_ref, grad_t_ref, d_ref, mixed_ref, *outs):
    quarter, width = outs[0].shape
    tok, col = mixed_ref.shape
    for k, out in enumerate(outs):
        first = pl.multiple_of(lax.rem(where[0] + k, 4) * quarter, quarter)
        rows = pl.ds(first, quarter)
        out[:, pl.ds(0, width - col)] = jnp.dot(
            normed_t_ref[rows, :], d_ref[pl.ds(0, tok), :], preferred_element_type=F32
        ).astype(BF16)
        out[:, pl.ds(width - col, col)] = jnp.dot(
            grad_t_ref[rows, :], mixed_ref[...], preferred_element_type=F32
        ).astype(BF16)


def weight_parts(where, normed_t, grad_t, d, mixed):
    width, tok = normed_t.shape
    col = mixed.shape[1]
    whole = pl.BlockSpec(memory_space=pltpu.VMEM)
    return kernel_call(
        weight_body,
        tuple(shape_of((width // 4, 5 * col), BF16) for _ in range(4)),
        "weight_parts",
        flops=2 * width * tok * 5 * col,
        bytes_accessed=width * tok * 6,
        in_specs=[pl.BlockSpec(memory_space=pltpu.SMEM)] + [whole] * 4,
        out_specs=[whole] * 4,
    )(where, normed_t, grad_t, d, mixed)


def input_grad_body(*refs):
    parts, (x_ref, gain_ref, inv_rms_ref, grad_ref, out_ref) = refs[:4], refs[4:]
    tok, col = x_ref.shape
    d_normed = parts[0][pl.ds(0, tok), :].astype(F32)
    for part in parts[1:]:
        d_normed = d_normed + part[pl.ds(0, tok), :].astype(F32)
    x = x_ref[...].astype(F32)
    inv_rms = inv_rms_ref[...]
    gain_sum = jnp.sum(d_normed * x * inv_rms, axis=0, keepdims=True)
    out_ref[pl.ds(tok, EXTRA), :] = two_rows(gain_sum)
    extra = [part[pl.ds(tok, EXTRA), :] for part in parts]
    row = lax.broadcasted_iota(jnp.int32, (EXTRA, col), 0)
    for tile in range(tok // BLOCK):
        rows = pl.ds(tile * BLOCK, BLOCK)
        pick = jnp.where((row >= 4 * tile) & (row < 4 * tile + 4), 1.0, 0.0).astype(BF16)
        mean = jnp.zeros((BLOCK, col), F32)
        for piece in extra:
            mean = mean + lax.dot_general(piece, pick, TN, preferred_element_type=F32)
        mean = mean * (1.0 / (8 * col))
        x_t, inv = x_ref[rows, :].astype(F32), inv_rms_ref[rows, :]
        d_t = d_normed[tile * BLOCK:(tile + 1) * BLOCK]
        value = inv * (d_t * gain_ref[...] - x_t * inv * inv * mean) + grad_ref[rows, :].astype(F32)
        out_ref[rows, :] = value.astype(BF16)


def input_grads(parts, x_cols, gain_cols, inv_rms, grad_cols):
    tok, col = x_cols.shape
    return kernel_call(
        input_grad_body,
        shape_of((tok + EXTRA, col), BF16),
        "input_grads",
        bytes_accessed=tok * col * 24,
    )(*parts, x_cols, gain_cols.reshape(1, -1), inv_rms, grad_cols)


def table_body(first_ref, *refs, lines):
    grads, ids_ref, out_ref, gain_ref = refs[:lines], refs[lines], refs[lines + 1], refs[lines + 2]
    items, col = out_ref.shape
    tok = ids_ref.shape[2]
    gain = jnp.zeros((EXTRA, col), F32)
    step = 256
    for line in range(lines):
        for part in range(4):
            gain = gain + grads[line][pl.ds(part * (tok + EXTRA) + tok, EXTRA), :].astype(F32)
    gain_ref[...] = jnp.sum(gain, axis=0, keepdims=True)

    def body(index, carry):
        start = pl.multiple_of(index * step, step)
        row = lax.broadcasted_iota(jnp.int32, (step, tok), 0) + (first_ref[0] + start)
        total = jnp.zeros((step, col), F32)
        for line in range(lines):
            for part in range(4):
                ids = ids_ref[line * 4 + part]
                hot = jnp.where(ids == row, 1.0, 0.0).astype(BF16)
                total = total + jnp.dot(
                    hot, grads[line][pl.ds(part * (tok + EXTRA), tok), :], preferred_element_type=F32
                )
        out_ref[pl.ds(start, step), :] = total
        return carry

    lax.fori_loop(0, items // step, body, 0)


def table_grads(first, grads, ids, items, col):
    whole = pl.BlockSpec(memory_space=pltpu.VMEM)
    lines = len(grads)
    return kernel_call(
        functools.partial(table_body, lines=lines),
        (shape_of((items, col), F32), shape_of((1, col), F32)),
        "table_grads",
        flops=2 * items * ids.shape[0] * ids.shape[2] * col,
        bytes_accessed=items * col * 8,
        in_specs=[pl.BlockSpec(memory_space=pltpu.SMEM)] + [whole] * (lines + 1),
        out_specs=[whole] * 2,
    )(first, *grads, ids)


def per_device(inputs, cotangent, norm_gain, proj_in, proj_out, item_ids, lengths, tile_mask):
    x_rows, cot_rows = inputs[0], cotangent[0]
    length, mask = lengths[0], tile_mask[0]
    tok, width = x_rows.shape
    col = proj_in.shape[2]
    scale = 1.0 / math.sqrt(col)
    tiles = tok // BLOCK
    dp, seq, cols = lax.axis_index("dp"), lax.axis_index("seq"), lax.axis_index("col")
    z_hi, x_pos = seq // 4, seq % 4
    z_pos = z_hi * 2 + dp
    y_pos, core = cols // 2, cols % 2

    where = jnp.stack([seq * tiles, length]).astype(jnp.int32)
    qd, kv, pre, normed, grad, dmix, upd, inv_cnt, inv_rms = project(
        where, x_rows, cot_rows, norm_gain, proj_in, proj_out, mask
    )

    zero, one = jnp.int32(0), jnp.int32(1)
    far_rank = (1 - z_hi) * 4 + x_pos
    across = move_seq(jnp.where(z_hi == 0, kv, qd), 1, 0)
    near, near_rank = [], []
    for k in (1, 3, 2):
        near.append(move_seq(jnp.where(x_pos + k < 4, kv, qd), 0, k))
        near_rank.append(z_hi * 4 + (x_pos - k) % 4)
    far, far_ranks = [], []
    for k in (1, 3, 2):
        far.append(move_seq(across, 0, k))
        far_ranks.append((1 - z_hi) * 4 + (x_pos - k) % 4)

    filled = (BLOCK * jnp.arange(mask.shape[0], dtype=jnp.int32) < length).astype(F32)
    kept = mask.astype(F32) * filled[None, :]
    as_query = lax.dynamic_slice_in_dim(kept, seq * tiles, tiles, 0)
    as_key = lax.dynamic_slice_in_dim(kept, seq * tiles, tiles, 1).T

    def keep_of(rows, rank):
        return jnp.repeat(lax.dynamic_slice_in_dim(rows, rank * tiles, tiles, 1), BLOCK, axis=1)

    def keep_side(ranks):
        sides = [jnp.where(rank > seq, one, zero) for rank in ranks]
        keeps = [keep_of(jnp.where(rank > seq, as_key, as_query), rank) for rank in ranks]
        return jnp.stack(sides), jnp.stack(keeps)

    acc = own_terms(qd, kv, jnp.stack([keep_of(as_query, seq), keep_of(as_key, seq)]), scale)
    sides, keeps = keep_side([far_rank] + near_rank)
    acc = far_terms(sides, qd, kv, keeps, [across] + near, acc, scale, "near_terms")
    sides, keeps = keep_side(far_ranks)
    acc = far_terms(sides, qd, kv, keeps, far, acc, scale, "far_terms")

    by_row = proj_in.transpose(1, 0, 2).reshape(4, 2, col, 4 * col)
    by_row = jnp.roll(by_row, -y_pos, axis=0)
    w_own = lax.dynamic_index_in_dim(by_row, core, 1, keepdims=False).reshape(4 * col, 4 * col)
    w_peer = move_core(lax.dynamic_index_in_dim(by_row, 1 - core, 1, keepdims=False).reshape(4 * col, 4 * col))
    normed_t, grad_t = normed.T, grad.T
    ids_all = jnp.stack(gather_plane(item_ids)).reshape(16, 1, tok)

    d_own, mixed = pre_grads(acc, pre, dmix, upd, inv_cnt, inv_rms, scale)
    d_peer = move_core(d_own)
    parts = back_project(d_own, d_peer, w_own, w_peer, col)
    parts = [parts[0]] + [move_y(parts[k], k) for k in (1, 3, 2)]
    weights = weight_parts(x_pos.reshape(1).astype(jnp.int32), normed_t, grad_t, d_own, mixed)

    quarter = weights[0]
    moved = [move_plane(weights[k], 0, k) for k in (1, 3, 2)]
    quarter = functools.reduce(lambda a, b: a + b.astype(F32), moved, quarter.astype(F32)).astype(BF16)
    pieces = quarter.reshape(4, width // 16, 5 * col)
    pieces = [lax.dynamic_index_in_dim(pieces, (z_pos + k) % 4, 0, keepdims=False) for k in range(4)]
    moved = [move_plane(pieces[k], k, 0) for k in (1, 3, 2)]
    share = functools.reduce(lambda a, b: a + b.astype(F32), moved, pieces[0].astype(F32)).astype(BF16)

    col_first = cols * col
    x_cols = lax.dynamic_slice_in_dim(x_rows, col_first, col, 1)
    grad_cols = lax.dynamic_slice_in_dim(grad, col_first, col, 1)
    gain_cols = lax.dynamic_slice_in_dim(norm_gain, col_first, col)
    d_inputs = input_grads(parts, x_cols, gain_cols, inv_rms, grad_cols)
    lines = gather_plane(d_inputs)
    items = 1024
    first = ((dp * 8 + seq) * items).reshape(1).astype(jnp.int32)
    table, gain = table_grads(first, lines, ids_all, items, col)

    column = jnp.stack([share, *(move_plane(share, k, 0) for k in (1, 2, 3))])
    column = jnp.roll(column[::-1], z_pos + 1, axis=0).reshape(width // 4, 5 * col)
    whole = jnp.stack([column, *(move_plane(column, 0, k) for k in (1, 2, 3))])
    whole = jnp.roll(whole[::-1], x_pos + 1, axis=0).reshape(width, 5, col)
    grad_in_w = whole[:, :4].transpose(1, 0, 2).astype(F32)
    grad_out_w = whole[:, 4].T.astype(F32)
    return (grad_in_w, grad_out_w, gain[0], table)


def solution(mesh):
    placed = (
        P("dp", "seq", None),
        P("dp", "seq", None),
        P(),
        P(None, None, "col"),
        P("col", None),
        P("dp", "seq"),
        P("dp"),
        P("dp", None, None),
    )
    return jax.shard_map(
        per_device,
        mesh=mesh,
        in_specs=placed,
        out_specs=(P(None, None, "col"), P("col", None), P("col"), P(("dp", "seq"), "col")),
        check_vma=False,
    )
```

```python
import functools
import math

import jax
import jax.numpy as jnp
from jax import lax
from jax.experimental import pallas as pl
from jax.experimental.pallas import tpu as pltpu
from jax.sharding import PartitionSpec as P

BLOCK = 128
EPSILON = 1e-06
BF16 = jnp.bfloat16
F32 = jnp.float32
MIB = 1024 * 1024
EXTRA = 16
NT = (((1,), (1,)), ((), ()))
TN = (((0,), (0,)), ((), ()))


def kernel_call(body, out_shape, name, flops=1000, bytes_accessed=1000, vmem=24, **kwargs):
    return pl.pallas_call(
        body,
        out_shape=out_shape,
        name=name,
        compiler_params=pltpu.CompilerParams(vmem_limit_bytes=vmem * MIB),
        cost_estimate=pl.CostEstimate(flops=flops, bytes_accessed=bytes_accessed, transcendentals=0),
        **kwargs,
    )


def shape_of(shape, dtype):
    return jax.ShapeDtypeStruct(shape, dtype)


def swap_plane(value):
    return lax.all_to_all(value, ("dp", "seq"), 0, 0, tiled=True)


def move_seq(value, dz_hi, dx):
    pairs = [(i, ((i // 4 + dz_hi) % 2) * 4 + (i % 4 + dx) % 4) for i in range(8)]
    return lax.ppermute(value, "seq", pairs)


def move_y(value, dy):
    return lax.ppermute(value, "col", [(i, ((i // 2 + dy) % 4) * 2 + i % 2) for i in range(8)])


def move_core(value):
    return lax.ppermute(value, "col", [(i, i ^ 1) for i in range(8)])


def project_body(length_ref, x_ref, cot_ref, gain_ref, proj_ref, out_ref, mask_ref,
                 own_ref, cross_ref, near1_ref, near2_ref, near3_ref, pre_ref, normed_ref, grad_ref, dmix_ref, upd_ref, inv_cnt_ref, inv_rms_ref, both_ref):
    length, rank = length_ref[0], lax.axis_index("seq")
    step, col = dmix_ref.shape

    @pl.when(pl.program_id(0) == 0)
    def _():
        for c in range(4):
            both_ref[:, pl.ds(c * col, col)] = proj_ref[c]

    x = x_ref[...].astype(F32)
    inv_rms = lax.rsqrt(jnp.mean(x * x, axis=1, keepdims=True) + EPSILON)
    normed = (x * inv_rms * gain_ref[...]).astype(BF16)
    normed_ref[...] = normed
    inv_rms_ref[...] = jnp.broadcast_to(inv_rms, inv_rms_ref.shape)
    pre = jnp.dot(normed, both_ref[...], preferred_element_type=F32)
    act = (pre * jax.nn.sigmoid(pre)).astype(BF16)
    for c in range(4):
        pre_ref[c] = pre[:, c * col:(c + 1) * col]
    tile = (rank * pl.num_programs(0) + pl.program_id(0)) * (step // BLOCK)
    local = lax.broadcasted_iota(jnp.int32, (step, 1), 0)
    position = tile * BLOCK + local
    grad = jnp.where(position < length, cot_ref[...].astype(F32), 0.0).astype(BF16)
    grad_ref[...] = grad
    d_mixed = lax.dot_general(grad, out_ref[...], NT, preferred_element_type=F32)
    dmix_ref[...] = d_mixed
    update = act[:, :col]
    upd_ref[...] = update
    tiles = mask_ref.shape[0]
    rows = lax.broadcasted_iota(jnp.int32, (tiles, tiles), 0)
    cols = lax.broadcasted_iota(jnp.int32, (tiles, tiles), 1)
    filled = jnp.clip(length - BLOCK * cols, 0, BLOCK)
    counted = jnp.where(cols < rows, mask_ref[...] * filled, 0)
    earlier = jnp.zeros((step, 1), F32)
    for index in range(step // BLOCK):
        picked = jnp.where(rows == tile + index, counted, 0).astype(F32)
        total = jnp.sum(jnp.sum(picked, axis=1, keepdims=True), axis=0, keepdims=True)
        earlier = jnp.where(local // BLOCK == index, total, earlier)
    own_first = tile * BLOCK + local // BLOCK * BLOCK
    diagonal = jnp.minimum(local % BLOCK + 1, jnp.clip(length - own_first, 0, BLOCK)).astype(F32)
    inv_cnt = 1.0 / jnp.maximum(earlier + diagonal, 1.0)
    inv_cnt_ref[...] = jnp.broadcast_to(inv_cnt, inv_cnt_ref.shape)
    qd = (act[:, col:2 * col], (d_mixed * update.astype(F32) * inv_cnt).astype(BF16))
    kv = (act[:, 2 * col:3 * col], act[:, 3 * col:])
    for index in range(2):
        own_ref[0, index], own_ref[1, index] = qd[index], kv[index]
    x_pos = lax.rem(rank, 4)
    later = [rank < 4] + [x_pos + k < 4 for k in (1, 2, 3)]
    for ref, is_later in zip((cross_ref, near1_ref, near2_ref, near3_ref), later):

        @pl.when(is_later)
        def _():
            ref[0], ref[1] = kv

        @pl.when(jnp.logical_not(is_later))
        def _():
            ref[0], ref[1] = qd


def project(lengths, x, cot, gain, proj_in, proj_out, mask):
    tok, width = x.shape
    col = proj_in.shape[2]
    step = 2 * BLOCK
    row = lambda i, w: (i, 0)
    side = lambda i, w: (0, i, 0)
    pair = lambda i, w: (0, 0, i, 0)
    fixed2 = lambda i, w: (0, 0)
    return kernel_call(
        project_body,
        (
            shape_of((2, 2, tok, col), BF16),
            *(shape_of((2, tok, col), BF16) for _ in range(4)),
            shape_of((4, tok, col), F32),
            shape_of((tok, width), BF16),
            shape_of((tok, width), BF16),
            shape_of((tok, col), F32),
            shape_of((tok, col), BF16),
            shape_of((tok, col), F32),
            shape_of((tok, col), F32),
        ),
        "project",
        vmem=63,
        grid_spec=pltpu.PrefetchScalarGridSpec(
            num_scalar_prefetch=1,
            grid=(tok // step,),
            in_specs=[
                pl.BlockSpec((step, width), row),
                pl.BlockSpec((step, width), row),
                pl.BlockSpec((1, width), fixed2),
                pl.BlockSpec((4, width, col), lambda i, w: (0, 0, 0)),
                pl.BlockSpec((col, width), fixed2),
                pl.BlockSpec(mask.shape, fixed2),
            ],
            out_specs=[
                pl.BlockSpec((2, 2, step, col), pair),
                *(pl.BlockSpec((2, step, col), side) for _ in range(4)),
                pl.BlockSpec((4, step, col), side),
                pl.BlockSpec((step, width), row),
                pl.BlockSpec((step, width), row),
                pl.BlockSpec((step, col), row),
                pl.BlockSpec((step, col), row),
                pl.BlockSpec((step, col), row),
                pl.BlockSpec((step, col), row),
            ],
            scratch_shapes=[pltpu.VMEM((width, 4 * col), BF16)],
        ),
    )(lengths, x, cot, gain.reshape(1, -1), proj_in, proj_out, mask)


def block_terms(a1, a2, b1, b2, keep, scale):
    half = lax.dot_general(a1, b1, NT, preferred_element_type=F32) * (keep * (0.5 * scale))
    other = lax.dot_general(a2, b2, NT, preferred_element_type=F32) * keep
    tanh = jnp.tanh(half)
    twice = 1.0 + tanh
    probs = half * twice
    slope = (other * (twice + probs * (1.0 - tanh))).astype(BF16)
    first = jnp.dot(probs.astype(BF16), b2, preferred_element_type=F32)
    second = jnp.dot(slope, b1, preferred_element_type=F32)
    return first, second


def block_sums(side, own_ref, other, keep_of, scale):
    tok, col = own_ref.shape[2:]
    part = 2 * BLOCK
    first, second = jnp.zeros((tok, col), F32), jnp.zeros((tok, col), F32)
    for start in range(0, tok, part):
        span = pl.ds(start, part)
        terms = block_terms(
            own_ref[side, 0], own_ref[side, 1], other[0][span, :], other[1][span, :], keep_of(start, part), scale
        )
        first, second = first + terms[0], second + terms[1]
    return first, second


def far_sums(index, side_ref, own_ref, other_ref, keep_ref, scale):
    def keep_of(start, part):
        return by_tile(keep_ref[index, :, pl.ds(start, part)], own_ref.shape[2])

    return block_sums(side_ref[index], own_ref, (other_ref.at[0], other_ref.at[1]), keep_of, scale)


def by_tile(rows, tok):
    tiles, part = rows.shape
    return jnp.broadcast_to(rows[:, None, :], (tiles, tok // tiles, part)).reshape(tok, part)


def near_body(side_ref, own_ref, keep_own_ref, keep_ref, *refs, scale):
    others, acc_ref = refs[:-1], refs[-1]
    tok = own_ref.shape[2]
    for side in range(2):
        other = own_ref.at[1 - side, 0], own_ref.at[1 - side, 1]

        def keep_of(start, part):
            keep = by_tile(keep_own_ref[side, :, pl.ds(start, part)], tok)
            row = lax.broadcasted_iota(jnp.int32, (tok, part), 0)
            column = lax.broadcasted_iota(jnp.int32, (tok, part), 1) + start
            ordered = (column <= row) if side == 0 else (row <= column)
            return jnp.where(ordered, keep, 0.0)

        acc_ref[side, 0], acc_ref[side, 1] = block_sums(side, own_ref, other, keep_of, scale)
    for index, other in enumerate(others):
        first, second = far_sums(index, side_ref, own_ref, other, keep_ref, scale)
        acc_ref[side_ref[index], 0] += first
        acc_ref[side_ref[index], 1] += second


def near_terms(sides, own, keep_own, keep, others, scale):
    whole = pl.BlockSpec(memory_space=pltpu.VMEM)
    return kernel_call(
        functools.partial(near_body, scale=scale),
        shape_of(own.shape, F32),
        "near_terms",
        vmem=63,
        in_specs=[pl.BlockSpec(memory_space=pltpu.SMEM)] + [whole] * (3 + len(others)),
        out_specs=whole,
    )(sides, own, keep_own, keep, *others)


FAR_INPUTS = 13


def far_body(side_ref, *refs, scale):
    sources, d_ref, parts_ref = refs[:FAR_INPUTS], refs[FAR_INPUTS], refs[FAR_INPUTS + 1]
    held, mixed_ref, sems = refs[FAR_INPUTS + 2:2 * FAR_INPUTS + 2], refs[-2], refs[-1]
    copies = [pltpu.make_async_copy(source, place, sems.at[n]) for n, (source, place) in enumerate(zip(sources, held))]
    for copy in copies:
        copy.start()
    own_ref, keep_ref = held[:2]
    others, acc_ref = held[2:5], held[5]
    pre_ref, inv_rms_ref, dmix_ref, upd_ref, inv_cnt_ref, normed_t_ref, grad_t_ref = held[6:]
    copies[0].wait()
    copies[1].wait()
    for index, other in enumerate(others):
        copies[2 + index].wait()
        first, second = far_sums(index, side_ref, own_ref, other, keep_ref, scale)
        if index == 0:
            copies[5].wait()
        acc_ref[side_ref[index], 0] += first
        acc_ref[side_ref[index], 1] += second
    for copy in copies[6:11]:
        copy.wait()
    pre_grad_body(acc_ref, pre_ref, inv_rms_ref, dmix_ref, upd_ref, inv_cnt_ref, d_ref, mixed_ref, scale=scale)
    for copy in copies[11:]:
        copy.wait()
    weight_body(normed_t_ref, grad_t_ref, d_ref, mixed_ref, parts_ref)


def far_terms(sides, own, keep, others, acc, pre, inv_rms, dmix, upd, inv_cnt, normed_t, grad_t, owners, scale):
    _, _, tok, col = own.shape
    width = normed_t.shape[0]
    sources = (own, keep, *others, acc, pre, inv_rms, dmix, upd, inv_cnt, normed_t, grad_t)
    return kernel_call(
        functools.partial(far_body, scale=scale),
        (shape_of((tok + EXTRA, 4 * col), BF16), shape_of((owners, 5 * width // owners, col), BF16)),
        "far_terms",
        vmem=63,
        in_specs=[pl.BlockSpec(memory_space=pltpu.SMEM)] + [pl.BlockSpec(memory_space=pl.ANY)] * len(sources),
        scratch_shapes=[
            *(pltpu.VMEM(source.shape, source.dtype) for source in sources),
            pltpu.VMEM((tok, col), BF16),
            pltpu.SemaphoreType.DMA((len(sources),)),
        ],
    )(sides, *sources)


def pre_grad_body(acc_ref, pre_ref, inv_rms_ref, dmix_ref, upd_ref, inv_cnt_ref, d_ref, mixed_ref, *, scale):
    tok, col = dmix_ref.shape
    stat = jnp.zeros((tok, col), F32)
    attended = acc_ref[0, 0] * inv_cnt_ref[...]
    mixed_ref[...] = (attended * upd_ref[...].astype(F32)).astype(BF16)
    grads = (
        dmix_ref[...] * attended,
        acc_ref[0, 1] * (0.5 * scale),
        acc_ref[1, 1] * (0.5 * scale),
        acc_ref[1, 0],
    )
    for c in range(4):
        pre = pre_ref[c]
        sig = jax.nn.sigmoid(pre)
        d_pre = (grads[c] * (sig * (1.0 + pre * (1.0 - sig)))).astype(BF16)
        d_ref[pl.ds(0, tok), pl.ds(c * col, col)] = d_pre
        stat = stat + d_pre.astype(F32) * pre
    stat = stat / inv_rms_ref[...]
    high = stat.astype(BF16)
    low = (stat - high.astype(F32)).astype(BF16)
    ones = jnp.ones((8, col), BF16)
    sums = lax.dot_general(ones, high, NT, preferred_element_type=F32)
    sums = sums + lax.dot_general(ones, low, NT, preferred_element_type=F32)
    d_ref[pl.ds(tok, EXTRA), :] = two_rows(sums[0:1])


def two_rows(value):
    high = value.astype(BF16).astype(F32)
    low = value - high
    row = lax.broadcasted_iota(jnp.int32, (EXTRA, value.shape[1]), 0)
    both = jnp.where(row == 0, jnp.broadcast_to(high, row.shape), jnp.where(row == 1, jnp.broadcast_to(low, row.shape), 0.0))
    return both.astype(BF16)


def back_body(own_ref, peer_ref, w_own_ref, w_peer_ref, *outs):
    tok = own_ref.shape[0] - EXTRA
    part = lax.dot_general(own_ref[pl.ds(0, tok), :], w_own_ref[...], NT, preferred_element_type=F32)
    part = part + lax.dot_general(peer_ref[pl.ds(0, tok), :], w_peer_ref[...], NT, preferred_element_type=F32)
    sums = jnp.sum(
        own_ref[pl.ds(tok, EXTRA), :].astype(F32) + peer_ref[pl.ds(tok, EXTRA), :].astype(F32), axis=0, keepdims=True
    )
    high = sums.astype(BF16).astype(F32)
    low = sums - high
    col = outs[0].shape[1]
    row = lax.broadcasted_iota(jnp.int32, (EXTRA, col), 0)
    extra = jnp.zeros((EXTRA, col), F32)
    for tile in range(tok // BLOCK):
        span = slice(tile * BLOCK, (tile + 1) * BLOCK)
        extra = jnp.where(row == 4 * tile, jnp.broadcast_to(high[:, span], row.shape), extra)
        extra = jnp.where(row == 4 * tile + 1, jnp.broadcast_to(low[:, span], row.shape), extra)
    extra = extra.astype(BF16)
    for k, out in enumerate(outs):
        out[pl.ds(0, tok), :] = part[:, k * col:(k + 1) * col].astype(BF16)
        out[pl.ds(tok, EXTRA), :] = extra


def back_project(own, peer, w_own, w_peer, col):
    rows, depth = own.shape
    return kernel_call(
        back_body,
        tuple(shape_of((rows, col), BF16) for _ in range(4)),
        "back_project",
    )(own, peer, w_own, w_peer)


def weight_body(normed_t_ref, grad_t_ref, d_ref, mixed_ref, out_ref):
    tok, col = mixed_ref.shape
    share = out_ref.shape[1] // 5
    step = 8 * share
    for part in range(2):
        rows = pl.ds(part * step, step)
        value = jnp.dot(normed_t_ref[rows, :], d_ref[pl.ds(0, tok), :], preferred_element_type=F32)
        last = jnp.dot(grad_t_ref[rows, :], mixed_ref[...], preferred_element_type=F32)
        for c in range(5):
            piece = value[:, c * col:(c + 1) * col] if c < 4 else last
            out_ref[pl.ds(part * 8, 8), pl.ds(c * share, share), :] = piece.astype(BF16).reshape(8, share, col)


def join_body(parts_ref, block_ref, out_ref, total_ref):
    held = parts_ref.shape[1]

    @pl.when(pl.program_id(0) == 0)
    def _():
        total = parts_ref[0].astype(F32)
        for index in range(1, parts_ref.shape[0]):
            total = total + parts_ref[index].astype(F32)
        total_ref[...] = total.astype(BF16)

    for index in range(out_ref.shape[0]):
        out_ref[index, pl.ds(0, held), :] = total_ref[...]
        out_ref[index, pl.ds(held, block_ref.shape[1]), :] = block_ref[index]


def join_sums(parts, blocks):
    owners, held, col = parts.shape
    rows = blocks.shape[1]
    step = 4
    return kernel_call(
        join_body,
        shape_of((owners, held + rows, col), BF16),
        "join_sums",
        grid=(owners // step,),
        in_specs=[
            pl.BlockSpec(parts.shape, lambda i: (0, 0, 0)),
            pl.BlockSpec((step, rows, col), lambda i: (i, 0, 0)),
        ],
        out_specs=pl.BlockSpec((step, held + rows, col), lambda i: (i, 0, 0)),
        scratch_shapes=[pltpu.VMEM((held, col), BF16)],
    )(parts, blocks)


def prepare_body(place_ref, normed_ref, grad_ref, proj_ref, x_ref, inv_rms_ref,
                 normed_t_ref, grad_t_ref, own_ref, peer_ref, x_cols_ref, grad_cols_ref):
    place = place_ref[0]
    y_pos, core = place // 2, lax.rem(place, 2)
    col = proj_ref.shape[2]
    normed_t_ref[...] = normed_ref[...].T
    grad_t_ref[...] = grad_ref[...].T
    pair = lax.rem(y_pos + pl.program_id(0), 4) * 2
    for c in range(4):
        span = pl.ds(c * col, col)
        own_ref[:, span] = proj_ref[c, pl.ds(pl.multiple_of((pair + core) * col, col), col), :]
        peer_ref[:, span] = proj_ref[c, pl.ds(pl.multiple_of((pair + 1 - core) * col, col), col), :]
    mine = pl.ds(pl.multiple_of(place * col, col), col)
    x_cols_ref[...] = x_ref[...].astype(F32) * inv_rms_ref[...]
    grad_cols_ref[...] = grad_ref[:, mine].astype(F32)


def prepare(place, normed, grad, proj_in, x, inv_rms):
    tok, width = normed.shape
    col = proj_in.shape[2]
    step = tok // 4
    row = lambda i, w: (i, 0)
    column = lambda i, w: (0, i)
    return kernel_call(
        prepare_body,
        (
            shape_of((width, tok), BF16),
            shape_of((width, tok), BF16),
            shape_of((4 * col, 4 * col), BF16),
            shape_of((4 * col, 4 * col), BF16),
            shape_of((tok, col), F32),
            shape_of((tok, col), F32),
        ),
        "prepare",
        vmem=63,
        grid_spec=pltpu.PrefetchScalarGridSpec(
            num_scalar_prefetch=1,
            grid=(4,),
            in_specs=[
                pl.BlockSpec((step, width), row),
                pl.BlockSpec((step, width), row),
                pl.BlockSpec(proj_in.shape, lambda i, w: (0, 0, 0)),
                pl.BlockSpec((step, col), lambda i, w: (i, w[0])),
                pl.BlockSpec((step, col), row),
            ],
            out_specs=[
                pl.BlockSpec((width, step), column),
                pl.BlockSpec((width, step), column),
                pl.BlockSpec((col, 4 * col), row),
                pl.BlockSpec((col, 4 * col), row),
                pl.BlockSpec((step, col), row),
                pl.BlockSpec((step, col), row),
            ],
        ),
    )(place, normed, grad, proj_in, x, inv_rms)


def fill_slots(slot_ref, item_ref, value_ref, blocks, owners, extra):
    room = blocks[0].shape[0] - EXTRA
    tok = slot_ref.shape[1]
    group = 4
    local = lax.broadcasted_iota(jnp.int32, (room, tok), 0)
    for first in range(0, len(blocks), group):
        hots = [jnp.where(slot_ref[...] == local + owner * room, 1.0, 0.0) for owner in owners[first:first + group]]
        hot = jnp.concatenate(hots, axis=0).astype(BF16)
        moved = jnp.dot(hot, value_ref[...], preferred_element_type=F32).astype(BF16)
        items = lax.dot_general(item_ref[...], hot, NT, preferred_element_type=F32)
        for index in range(group):
            span = slice(index * room, (index + 1) * room)
            block = blocks[first + index]
            block[pl.ds(0, room), :] = moved[span]
            block[pl.ds(room, EXTRA), :] = (extra + items[:, span]).astype(BF16)


def fill_all(slot_ref, item_ref, value_ref, out_ref, extra):
    owners = list(range(out_ref.shape[0]))
    fill_slots(slot_ref, item_ref, value_ref, [out_ref.at[owner] for owner in owners], owners, extra)


def input_grad_body(*refs):
    parts = refs[:4]
    x_ref, gain_ref, inv_rms_ref, grad_ref, slot_ref, item_ref, value_ref = refs[4:11]
    out_ref = refs[11]
    tok, col = x_ref.shape
    d_normed = parts[0][pl.ds(0, tok), :].astype(F32)
    for part in parts[1:]:
        d_normed = d_normed + part[pl.ds(0, tok), :].astype(F32)
    gain_sum = two_rows(jnp.sum(d_normed * x_ref[...], axis=0, keepdims=True)).astype(F32)
    extra = [part[pl.ds(tok, EXTRA), :] for part in parts]
    row = lax.broadcasted_iota(jnp.int32, (EXTRA, col), 0)
    for tile in range(tok // BLOCK):
        rows = pl.ds(tile * BLOCK, BLOCK)
        pick = jnp.where((row >= 4 * tile) & (row < 4 * tile + 4), 1.0, 0.0).astype(BF16)
        mean = jnp.zeros((BLOCK, col), F32)
        for piece in extra:
            mean = mean + lax.dot_general(piece, pick, TN, preferred_element_type=F32)
        inv = inv_rms_ref[rows, :]
        d_t = d_normed[tile * BLOCK:(tile + 1) * BLOCK]
        mean = mean * inv * (1.0 / (8 * col))
        value = inv * (d_t * gain_ref[...] - x_ref[rows, :] * mean) + grad_ref[rows, :]
        value_ref[rows, :] = value.astype(BF16)
    rounds = jnp.max(item_ref[pl.ds(5, 1), :].astype(F32), axis=1, keepdims=True)
    fill_all(slot_ref, item_ref, value_ref, out_ref, gain_sum + jnp.where(row == 4, rounds, 0.0))


def input_grads(parts, x_cols, gain_cols, inv_rms, grad_cols, slots, items, owners, room):
    tok, col = x_cols.shape
    return kernel_call(
        input_grad_body,
        (shape_of((tok, col), BF16), shape_of((owners, room + EXTRA, col), BF16)),
        "input_grads",
    )(*parts, x_cols, gain_cols.reshape(1, -1), inv_rms, grad_cols, slots, items)


def more_body(slot_ref, item_ref, value_ref, out_ref):
    fill_all(slot_ref, item_ref, value_ref, out_ref, 0.0)


def more_slots(slots, items, values, owners, room):
    col = values.shape[1]
    return kernel_call(more_body, shape_of((owners, room + EXTRA, col), BF16), "more_slots")(slots, items, values)


def rows_total(blocks, first, count):
    room = blocks[0].shape[0] - EXTRA
    total = jnp.zeros((count, blocks[0].shape[1]), F32)
    row = lax.broadcasted_iota(jnp.int32, (count, room), 0) + first
    for pair in range(0, len(blocks), 2):
        hots, data = [], []
        for block in blocks[pair:pair + 2]:
            extra = block[pl.ds(room, EXTRA), :].astype(F32)
            item = ((extra[2:3] - 1.0) * 32.0 + extra[3:4]).astype(jnp.int32)
            hots.append(jnp.where(item == row, 1.0, 0.0).astype(BF16))
            data.append(block[pl.ds(0, room), :])
        total = total + jnp.dot(
            jnp.concatenate(hots, axis=1), jnp.concatenate(data, axis=0), preferred_element_type=F32
        )
    return total


def finish_body(got_ref, in_ref, out_ref, table_ref, gain_ref, rounds_ref):
    step = pl.program_id(0)
    count, col = table_ref.shape
    at = got_ref.shape[1] - BLOCK - EXTRA
    share = at // 5
    lasts = []
    for index in range(4):
        owner = step * 4 + index
        for c in range(4):
            in_ref[c, pl.ds(index * share, share), :] = got_ref[owner, pl.ds(c * share, share), :].astype(F32)
        lasts.append(got_ref[owner, pl.ds(4 * share, share), :].astype(F32))
    out_ref[...] = jnp.concatenate(lasts, axis=0).T
    blocks = [got_ref.at[index, pl.ds(at, BLOCK + EXTRA)] for index in range(got_ref.shape[0])]
    table_ref[...] = rows_total(blocks, step * count, count)
    extra = [block[pl.ds(BLOCK, EXTRA), :].astype(F32) for block in blocks]
    total = functools.reduce(lambda a, b: a + b, extra)
    gain_ref[...] = total[0:1] + total[1:2]
    rounds_ref[0] = jnp.max(functools.reduce(jnp.maximum, extra)[4:5]).astype(jnp.int32)


def finish(got, items):
    owners, _, col = got.shape
    width = 8 * col
    steps = owners // 4
    return kernel_call(
        finish_body,
        (
            shape_of((4, width, col), F32),
            shape_of((col, width), F32),
            shape_of((items, col), F32),
            shape_of((1, col), F32),
            shape_of((1,), jnp.int32),
        ),
        "finish",
        grid=(steps,),
        in_specs=[pl.BlockSpec(got.shape, lambda i: (0, 0, 0))],
        out_specs=[
            pl.BlockSpec((4, width // steps, col), lambda i: (0, i, 0)),
            pl.BlockSpec((col, width // steps), lambda i: (0, i)),
            pl.BlockSpec((items // steps, col), lambda i: (i, 0)),
            pl.BlockSpec((1, col), lambda i: (0, 0)),
            pl.BlockSpec(memory_space=pltpu.SMEM),
        ],
    )(got)


def more_table_body(got_ref, table_ref, out_ref):
    count = 2 * BLOCK
    blocks = [got_ref.at[index] for index in range(got_ref.shape[0])]
    for first in range(0, table_ref.shape[0], count):
        rows = pl.ds(first, count)
        out_ref[rows, :] = table_ref[rows, :] + rows_total(blocks, first, count)


def more_table(got, table):
    return kernel_call(more_table_body, shape_of(table.shape, F32), "more_table")(got, table)


def per_device(inputs, cotangent, norm_gain, proj_in, proj_out, item_ids, lengths, tile_mask):
    x_rows, cot_rows = inputs[0], cotangent[0]
    length, mask = lengths[0], tile_mask[0]
    tok, width = x_rows.shape
    col = proj_in.shape[2]
    scale = 1.0 / math.sqrt(col)
    tiles = tok // BLOCK
    seq, cols = lax.axis_index("seq"), lax.axis_index("col")
    z_hi, x_pos = seq // 4, seq % 4

    own, cross, near1, near2, near3, pre, normed, grad, dmix, upd, inv_cnt, inv_rms = project(
        lengths, x_rows, cot_rows, norm_gain, proj_in, proj_out, mask
    )

    across = move_seq(cross, 1, 0)
    near = [move_seq(block, 0, k) for block, k in ((near1, 1), (near3, 3), (near2, 2))]
    far = [move_seq(across, 0, k) for k in (1, 3, 2)]

    filled = (BLOCK * jnp.arange(mask.shape[0], dtype=jnp.int32) < length).astype(F32)
    kept = mask.astype(F32) * filled[None, :]
    as_query = lax.dynamic_slice_in_dim(kept, seq * tiles, tiles, 0)
    as_key = lax.dynamic_slice_in_dim(kept, seq * tiles, tiles, 1).T
    later = jnp.arange(mask.shape[0], dtype=jnp.int32) // tiles > seq
    keep = jnp.where(later[None, :], as_key, as_query)

    def keep_of(rows, rank):
        return jnp.repeat(lax.dynamic_slice_in_dim(rows, rank * tiles, tiles, 1), BLOCK, axis=1)

    def keep_side(dz):
        ranks = [(z_hi + dz) % 2 * 4 + (x_pos - k) % 4 for k in (1, 3, 2)]
        return [(rank > seq).astype(jnp.int32) for rank in ranks], [keep_of(keep, rank) for rank in ranks]

    cross_rank = (1 - z_hi) * 4 + x_pos
    near_side, near_keep = keep_side(0)
    far_side, far_keep = keep_side(1)
    near_side = jnp.stack([(cross_rank > seq).astype(jnp.int32)] + near_side)
    near_keep = jnp.stack([keep_of(keep, cross_rank)] + near_keep)
    far_side, far_keep = jnp.stack(far_side), jnp.stack(far_keep)
    keep_own = jnp.stack([keep_of(as_query, seq), keep_of(as_key, seq)])

    owners, items, room = 16, 1024, BLOCK
    ids = item_ids[0]
    owner = ids // items
    order = jnp.arange(tok, dtype=jnp.int32)
    ahead = (owner[:, None] == owner[None, :]) & (order[:, None] < order[None, :])
    rank = jnp.sum(ahead.astype(jnp.int32), axis=0)
    rounds_here = rank // room + 1
    offset = ids % items
    nothing = jnp.zeros_like(ids)
    rows = [nothing, nothing, offset // 32 + 1, offset % 32, nothing, rounds_here] + [nothing] * (EXTRA - 6)
    item_rows = jnp.stack(rows).astype(BF16)

    def slots_of(turn):
        place = rank - turn * room
        return jnp.where((place >= 0) & (place < room), owner * room + place, -1).reshape(1, tok)

    slots = slots_of(0)

    normed, grad, proj_now, x_now, inv_rms_now, across = lax.optimization_barrier(
        (normed, grad, proj_in, x_rows, inv_rms, across)
    )
    normed_t, grad_t, w_own, w_peer, x_cols, grad_cols = prepare(
        cols.reshape(1).astype(jnp.int32), normed, grad, proj_now, x_now, inv_rms_now
    )
    w_peer = move_core(w_peer)
    gain_cols = lax.dynamic_slice_in_dim(norm_gain, cols * col, col)
    acc = near_terms(near_side, own, keep_own, near_keep, [across] + near, scale)
    far_side, far_keep, w_peer, slots, item_rows, gain_cols = lax.optimization_barrier(
        (far_side, far_keep, w_peer, slots, item_rows, gain_cols)
    )
    d_own, shares = far_terms(
        far_side, own, far_keep, far, acc, pre, inv_rms, dmix, upd, inv_cnt, normed_t, grad_t, owners, scale
    )
    d_peer = move_core(d_own)
    shares = swap_plane(shares)
    parts = back_project(d_own, d_peer, w_own, w_peer, col)
    parts = [parts[0]] + [move_y(parts[k], k) for k in (1, 3, 2)]

    d_inputs, blocks = input_grads(parts, x_cols, gain_cols, inv_rms, grad_cols, slots, item_rows, owners, room)
    grad_in_w, grad_out_w, table, gain, rounds = finish(swap_plane(join_sums(shares, blocks)), items)

    def another(state):
        turn, total = state
        got = swap_plane(more_slots(slots_of(turn), item_rows, d_inputs, owners, room))
        return turn + 1, more_table(got, total)

    _, table = lax.while_loop(lambda state: state[0] < rounds[0], another, (jnp.int32(1), table))

    return (grad_in_w, grad_out_w, gain[0], table)


def solution(mesh):
    placed = (
        P("dp", "seq", None),
        P("dp", "seq", None),
        P(),
        P(None, None, "col"),
        P("col", None),
        P("dp", "seq"),
        P("dp"),
        P("dp", None, None),
    )
    return jax.shard_map(
        per_device,
        mesh=mesh,
        in_specs=placed,
        out_specs=(P(None, None, "col"), P("col", None), P("col"), P(("dp", "seq"), "col")),
        check_vma=False,
    )
```

```python
import functools
import math

import jax
import jax.numpy as jnp
from jax import lax
from jax.experimental import pallas as pl
from jax.experimental.pallas import tpu as pltpu
from jax.sharding import PartitionSpec as P

BLOCK = 128
EPSILON = 1e-06
BF16 = jnp.bfloat16
F32 = jnp.float32
MIB = 1024 * 1024
EXTRA = 16
NT = (((1,), (1,)), ((), ()))
TN = (((0,), (0,)), ((), ()))


def kernel_call(body, out_shape, name, flops=1000, bytes_accessed=1000, vmem=24, **kwargs):
    return pl.pallas_call(
        body,
        out_shape=out_shape,
        name=name,
        compiler_params=pltpu.CompilerParams(vmem_limit_bytes=vmem * MIB),
        cost_estimate=pl.CostEstimate(flops=flops, bytes_accessed=bytes_accessed, transcendentals=0),
        **kwargs,
    )


def shape_of(shape, dtype):
    return jax.ShapeDtypeStruct(shape, dtype)


def swap_plane(value):
    return lax.all_to_all(value, ("dp", "seq"), 0, 0, tiled=True)


def plane_rank(z, x):
    return (z % 2) * 8 + (z // 2) * 4 + x


def move_plane(value, dz, dx):
    pairs = []
    for z in range(4):
        for x in range(4):
            pairs.append((plane_rank(z, x), plane_rank((z + dz) % 4, (x + dx) % 4)))
    return lax.ppermute(value, ("dp", "seq"), pairs)


def move_seq(value, dz_hi, dx):
    pairs = [(i, ((i // 4 + dz_hi) % 2) * 4 + (i % 4 + dx) % 4) for i in range(8)]
    return lax.ppermute(value, "seq", pairs)


def move_y(value, dy):
    return lax.ppermute(value, "col", [(i, ((i // 2 + dy) % 4) * 2 + i % 2) for i in range(8)])


def move_core(value):
    return lax.ppermute(value, "col", [(i, i ^ 1) for i in range(8)])


def project_body(length_ref, x_ref, cot_ref, gain_ref, proj_ref, out_ref, mask_ref,
                 own_ref, cross_ref, near1_ref, near2_ref, near3_ref, pre_ref, dmix_ref, upd_ref, inv_cnt_ref, inv_rms_ref, both_ref):
    length, rank = length_ref[0], lax.axis_index("seq")
    step, col = dmix_ref.shape

    @pl.when(pl.program_id(0) == 0)
    def _():
        for c in range(4):
            both_ref[:, pl.ds(c * col, col)] = proj_ref[c]

    x = x_ref[...].astype(F32)
    inv_rms = lax.rsqrt(jnp.mean(x * x, axis=1, keepdims=True) + EPSILON)
    normed = (x * inv_rms * gain_ref[...]).astype(BF16)
    inv_rms_ref[...] = jnp.broadcast_to(inv_rms, inv_rms_ref.shape)
    pre = jnp.dot(normed, both_ref[...], preferred_element_type=F32)
    act = (pre * jax.nn.sigmoid(pre)).astype(BF16)
    for c in range(4):
        pre_ref[c] = pre[:, c * col:(c + 1) * col]
    tile = (rank * pl.num_programs(0) + pl.program_id(0)) * (step // BLOCK)
    local = lax.broadcasted_iota(jnp.int32, (step, 1), 0)
    position = tile * BLOCK + local
    grad = jnp.where(position < length, cot_ref[...].astype(F32), 0.0).astype(BF16)
    d_mixed = lax.dot_general(grad, out_ref[...], NT, preferred_element_type=F32)
    dmix_ref[...] = d_mixed
    update = act[:, :col]
    upd_ref[...] = update
    tiles = mask_ref.shape[0]
    rows = lax.broadcasted_iota(jnp.int32, (tiles, tiles), 0)
    cols = lax.broadcasted_iota(jnp.int32, (tiles, tiles), 1)
    filled = jnp.clip(length - BLOCK * cols, 0, BLOCK)
    counted = jnp.where(cols < rows, mask_ref[...] * filled, 0)
    earlier = jnp.zeros((step, 1), F32)
    for index in range(step // BLOCK):
        picked = jnp.where(rows == tile + index, counted, 0).astype(F32)
        total = jnp.sum(jnp.sum(picked, axis=1, keepdims=True), axis=0, keepdims=True)
        earlier = jnp.where(local // BLOCK == index, total, earlier)
    own_first = tile * BLOCK + local // BLOCK * BLOCK
    diagonal = jnp.minimum(local % BLOCK + 1, jnp.clip(length - own_first, 0, BLOCK)).astype(F32)
    inv_cnt = 1.0 / jnp.maximum(earlier + diagonal, 1.0)
    inv_cnt_ref[...] = jnp.broadcast_to(inv_cnt, inv_cnt_ref.shape)
    qd = (act[:, col:2 * col], (d_mixed * update.astype(F32) * inv_cnt).astype(BF16))
    kv = (act[:, 2 * col:3 * col], act[:, 3 * col:])
    for index in range(2):
        own_ref[0, index], own_ref[1, index] = qd[index], kv[index]
    x_pos = lax.rem(rank, 4)
    later = [rank < 4] + [x_pos + k < 4 for k in (1, 2, 3)]
    for ref, is_later in zip((cross_ref, near1_ref, near2_ref, near3_ref), later):

        @pl.when(is_later)
        def _():
            ref[0], ref[1] = kv

        @pl.when(jnp.logical_not(is_later))
        def _():
            ref[0], ref[1] = qd


def project(lengths, x, cot, gain, proj_in, proj_out, mask):
    tok, width = x.shape
    col = proj_in.shape[2]
    step = 2 * BLOCK
    row = lambda i, w: (i, 0)
    side = lambda i, w: (0, i, 0)
    pair = lambda i, w: (0, 0, i, 0)
    fixed2 = lambda i, w: (0, 0)
    return kernel_call(
        project_body,
        (
            shape_of((2, 2, tok, col), BF16),
            *(shape_of((2, tok, col), BF16) for _ in range(4)),
            shape_of((4, tok, col), F32),
            shape_of((tok, col), F32),
            shape_of((tok, col), BF16),
            shape_of((tok, col), F32),
            shape_of((tok, col), F32),
        ),
        "project",
        vmem=63,
        grid_spec=pltpu.PrefetchScalarGridSpec(
            num_scalar_prefetch=1,
            grid=(tok // step,),
            in_specs=[
                pl.BlockSpec((step, width), row),
                pl.BlockSpec((step, width), row),
                pl.BlockSpec((1, width), fixed2),
                pl.BlockSpec((4, width, col), lambda i, w: (0, 0, 0)),
                pl.BlockSpec((col, width), fixed2),
                pl.BlockSpec(mask.shape, fixed2),
            ],
            out_specs=[
                pl.BlockSpec((2, 2, step, col), pair),
                *(pl.BlockSpec((2, step, col), side) for _ in range(4)),
                pl.BlockSpec((4, step, col), side),
                pl.BlockSpec((step, col), row),
                pl.BlockSpec((step, col), row),
                pl.BlockSpec((step, col), row),
                pl.BlockSpec((step, col), row),
            ],
            scratch_shapes=[pltpu.VMEM((width, 4 * col), BF16)],
        ),
    )(lengths, x, cot, gain.reshape(1, -1), proj_in, proj_out, mask)


def block_terms(a1, a2, b1, b2, keep, scale):
    half = lax.dot_general(a1, b1, NT, preferred_element_type=F32) * (keep * (0.5 * scale))
    other = lax.dot_general(a2, b2, NT, preferred_element_type=F32) * keep
    tanh = jnp.tanh(half)
    twice = 1.0 + tanh
    probs = half * twice
    slope = (other * (twice + probs * (1.0 - tanh))).astype(BF16)
    first = jnp.dot(probs.astype(BF16), b2, preferred_element_type=F32)
    second = jnp.dot(slope, b1, preferred_element_type=F32)
    return first, second


def block_sums(side, own_ref, other, keep_of, scale):
    tok, col = own_ref.shape[2:]
    part = 2 * BLOCK
    first, second = jnp.zeros((tok, col), F32), jnp.zeros((tok, col), F32)
    for start in range(0, tok, part):
        span = pl.ds(start, part)
        terms = block_terms(
            own_ref[side, 0], own_ref[side, 1], other[0][span, :], other[1][span, :], keep_of(start, part), scale
        )
        first, second = first + terms[0], second + terms[1]
    return first, second


def kept_tiles(mask_ref, length_ref, rank, tiles):
    count = mask_ref.shape[0]
    row = lax.broadcasted_iota(jnp.int32, (count, count), 0)
    column = lax.broadcasted_iota(jnp.int32, (count, count), 1)
    kept = jnp.where(column * BLOCK < length_ref[0], mask_ref[...].astype(F32), 0.0).astype(BF16)
    own = jnp.where(row + rank * tiles == column, 1.0, 0.0).astype(BF16)
    as_query = jnp.dot(own, kept, preferred_element_type=F32)
    as_key = lax.dot_general(own, kept, NT, preferred_element_type=F32)
    return as_query.astype(BF16), as_key.astype(BF16)


def keep_rows(kept, other, tiles, tok):
    count = kept.shape[0]
    row = lax.broadcasted_iota(jnp.int32, (count, tok), 0)
    column = lax.broadcasted_iota(jnp.int32, (count, tok), 1)
    spread = jnp.where(row == other * tiles + column // BLOCK, 1.0, 0.0).astype(BF16)
    return jnp.dot(kept, spread, preferred_element_type=F32)[:tiles]


def far_sums(other, rank, kept, own_ref, other_ref, scale):
    tok = own_ref.shape[2]
    tiles = tok // BLOCK
    side = jnp.where(other > rank, 1, 0)
    rows = jnp.where(other > rank, kept[1].astype(F32), kept[0].astype(F32)).astype(BF16)
    keep = keep_rows(rows, other, tiles, tok)

    def keep_of(start, part):
        return by_tile(keep[:, start:start + part], tok)

    return side, block_sums(side, own_ref, (other_ref.at[0], other_ref.at[1]), keep_of, scale)


def rank_at(rank, dz, dx):
    return lax.rem(rank // 4 + dz, 2) * 4 + lax.rem(rank + 4 - dx, 4)


def by_tile(rows, tok):
    tiles, part = rows.shape
    return jnp.broadcast_to(rows[:, None, :], (tiles, tok // tiles, part)).reshape(tok, part)


def near_body(length_ref, own_ref, mask_ref, proj_own_ref, proj_peer_ref, *refs, scale):
    others, (acc_ref, w_own_ref, w_peer_ref, sems) = refs[:-4], refs[-4:]
    tok, col = own_ref.shape[2:]
    place = lax.axis_index("col")
    picks = []
    for proj_ref, w_ref in ((proj_own_ref, w_own_ref), (proj_peer_ref, w_peer_ref)):
        for k in range(4):
            first = (lax.rem(place // 2 + k, 4) * 2 + lax.rem(place, 2)) * col
            rows = pl.ds(pl.multiple_of(first, col), col)
            for c in range(4):
                spot = w_ref.at[pl.ds(k * col, col), pl.ds(c * col, col)]
                picks.append(pltpu.make_async_copy(proj_ref.at[c, rows], spot, sems.at[len(picks)]))
    for pick in picks:
        pick.start()
    tiles = tok // BLOCK
    rank = lax.axis_index("seq")
    kept = kept_tiles(mask_ref, length_ref, rank, tiles)
    for side in range(2):
        other = own_ref.at[1 - side, 0], own_ref.at[1 - side, 1]
        rows = keep_rows(kept[side], rank, tiles, tok)

        def keep_of(start, part):
            row = lax.broadcasted_iota(jnp.int32, (tok, part), 0)
            column = lax.broadcasted_iota(jnp.int32, (tok, part), 1) + start
            ordered = (column <= row) if side == 0 else (row <= column)
            return jnp.where(ordered, by_tile(rows[:, start:start + part], tok), 0.0)

        acc_ref[side, 0], acc_ref[side, 1] = block_sums(side, own_ref, other, keep_of, scale)
    places = [(1, 0), (0, 1), (0, 3), (0, 2)]
    for (dz, dx), other in zip(places, others):
        side, sums = far_sums(rank_at(rank, dz, dx), rank, kept, own_ref, other, scale)
        acc_ref[side, 0] += sums[0]
        acc_ref[side, 1] += sums[1]
    for pick in picks:
        pick.wait()


def near_terms(lengths, own, mask, proj_own, proj_peer, others, scale):
    whole, anywhere = pl.BlockSpec(memory_space=pltpu.VMEM), pl.BlockSpec(memory_space=pl.ANY)
    depth = 4 * proj_own.shape[2]
    return kernel_call(
        functools.partial(near_body, scale=scale),
        (shape_of(own.shape, F32), shape_of((depth, depth), BF16), shape_of((depth, depth), BF16)),
        "near_terms",
        vmem=63,
        in_specs=[pl.BlockSpec(memory_space=pltpu.SMEM)] + [whole] * 2 + [anywhere] * 2 + [whole] * len(others),
        out_specs=[whole] * 3,
        scratch_shapes=[pltpu.SemaphoreType.DMA((32,))],
    )(lengths, own, mask, proj_own, proj_peer, *others)


FAR_INPUTS = 13


def far_body(length_ref, *refs, scale):
    sources, d_out, parts_out = refs[:FAR_INPUTS], refs[FAR_INPUTS], refs[FAR_INPUTS + 1]
    held = refs[FAR_INPUTS + 2:2 * FAR_INPUTS + 2]
    mixed_ref, d_ref, parts_ref, sems, out_sems = refs[2 * FAR_INPUTS + 2:]
    copies = [pltpu.make_async_copy(source, place, sems.at[n]) for n, (source, place) in enumerate(zip(sources, held))]
    for copy in copies:
        copy.start()
    own_ref, mask_ref = held[:2]
    rank = lax.axis_index("seq")
    others, acc_ref = held[2:5], held[5]
    pre_ref, inv_rms_ref, dmix_ref, upd_ref, inv_cnt_ref, normed_t_ref, grad_t_ref = held[6:]
    copies[0].wait()
    copies[1].wait()
    kept = kept_tiles(mask_ref, length_ref, rank, own_ref.shape[2] // BLOCK)
    for index, (dx, other) in enumerate(zip((1, 3, 2), others)):
        copies[2 + index].wait()
        side, sums = far_sums(rank_at(rank, 1, dx), rank, kept, own_ref, other, scale)
        if index == 0:
            copies[5].wait()
        acc_ref[side, 0] += sums[0]
        acc_ref[side, 1] += sums[1]
    for copy in copies[6:11]:
        copy.wait()
    pre_grad_body(acc_ref, pre_ref, inv_rms_ref, dmix_ref, upd_ref, inv_cnt_ref, d_ref, mixed_ref, scale=scale)
    leaving = [pltpu.make_async_copy(d_ref, d_out, out_sems.at[0])]
    leaving[0].start()
    for copy in copies[11:]:
        copy.wait()
    half = parts_ref.shape[0] // 2
    for part in range(2):
        weight_body(part, normed_t_ref, grad_t_ref, d_ref, mixed_ref, parts_ref)
        owners = pl.ds(part * half, half)
        leaving.append(pltpu.make_async_copy(parts_ref.at[owners], parts_out.at[owners], out_sems.at[part + 1]))
        leaving[-1].start()
    for copy in leaving:
        copy.wait()


def far_terms(lengths, own, mask, others, acc, pre, inv_rms, dmix, upd, inv_cnt, normed_t, grad_t, owners, scale):
    _, _, tok, col = own.shape
    width = normed_t.shape[0]
    sources = (own, mask, *others, acc, pre, inv_rms, dmix, upd, inv_cnt, normed_t, grad_t)
    return kernel_call(
        functools.partial(far_body, scale=scale),
        (shape_of((tok + EXTRA, 4 * col), BF16), shape_of((owners, 5 * width // owners, col), BF16)),
        "far_terms",
        vmem=63,
        in_specs=[pl.BlockSpec(memory_space=pltpu.SMEM)] + [pl.BlockSpec(memory_space=pl.ANY)] * len(sources),
        out_specs=[pl.BlockSpec(memory_space=pl.ANY)] * 2,
        scratch_shapes=[
            *(pltpu.VMEM(source.shape, source.dtype) for source in sources),
            pltpu.VMEM((tok, col), BF16),
            pltpu.VMEM((tok + EXTRA, 4 * col), BF16),
            pltpu.VMEM((owners, 5 * width // owners, col), BF16),
            pltpu.SemaphoreType.DMA((len(sources),)),
            pltpu.SemaphoreType.DMA((3,)),
        ],
    )(lengths, *sources)


def pre_grad_body(acc_ref, pre_ref, inv_rms_ref, dmix_ref, upd_ref, inv_cnt_ref, d_ref, mixed_ref, *, scale):
    tok, col = dmix_ref.shape
    stat = jnp.zeros((tok, col), F32)
    attended = acc_ref[0, 0] * inv_cnt_ref[...]
    mixed_ref[...] = (attended * upd_ref[...].astype(F32)).astype(BF16)
    grads = (
        dmix_ref[...] * attended,
        acc_ref[0, 1] * (0.5 * scale),
        acc_ref[1, 1] * (0.5 * scale),
        acc_ref[1, 0],
    )
    for c in range(4):
        pre = pre_ref[c]
        sig = jax.nn.sigmoid(pre)
        d_pre = (grads[c] * (sig * (1.0 + pre * (1.0 - sig)))).astype(BF16)
        d_ref[pl.ds(0, tok), pl.ds(c * col, col)] = d_pre
        stat = stat + d_pre.astype(F32) * pre
    stat = stat / inv_rms_ref[...]
    high = stat.astype(BF16)
    low = (stat - high.astype(F32)).astype(BF16)
    ones = jnp.ones((8, col), BF16)
    sums = lax.dot_general(ones, high, NT, preferred_element_type=F32)
    sums = sums + lax.dot_general(ones, low, NT, preferred_element_type=F32)
    d_ref[pl.ds(tok, EXTRA), :] = two_rows(sums[0:1])


def two_rows(value):
    high = value.astype(BF16).astype(F32)
    low = value - high
    row = lax.broadcasted_iota(jnp.int32, (EXTRA, value.shape[1]), 0)
    both = jnp.where(row == 0, jnp.broadcast_to(high, row.shape), jnp.where(row == 1, jnp.broadcast_to(low, row.shape), 0.0))
    return both.astype(BF16)


def back_body(own_ref, peer_ref, w_own_ref, w_peer_ref, *outs):
    tok = own_ref.shape[0] - EXTRA
    part = lax.dot_general(own_ref[pl.ds(0, tok), :], w_own_ref[...], NT, preferred_element_type=F32)
    part = part + lax.dot_general(peer_ref[pl.ds(0, tok), :], w_peer_ref[...], NT, preferred_element_type=F32)
    sums = jnp.sum(
        own_ref[pl.ds(tok, EXTRA), :].astype(F32) + peer_ref[pl.ds(tok, EXTRA), :].astype(F32), axis=0, keepdims=True
    )
    high = sums.astype(BF16).astype(F32)
    low = sums - high
    col = outs[0].shape[1]
    row = lax.broadcasted_iota(jnp.int32, (EXTRA, col), 0)
    extra = jnp.zeros((EXTRA, col), F32)
    for tile in range(tok // BLOCK):
        span = slice(tile * BLOCK, (tile + 1) * BLOCK)
        extra = jnp.where(row == 4 * tile, jnp.broadcast_to(high[:, span], row.shape), extra)
        extra = jnp.where(row == 4 * tile + 1, jnp.broadcast_to(low[:, span], row.shape), extra)
    extra = extra.astype(BF16)
    for k, out in enumerate(outs):
        out[pl.ds(0, tok), :] = part[:, k * col:(k + 1) * col].astype(BF16)
        out[pl.ds(tok, EXTRA), :] = extra


def back_project(own, peer, w_own, w_peer, col):
    rows, depth = own.shape
    return kernel_call(
        back_body,
        tuple(shape_of((rows, col), BF16) for _ in range(4)),
        "back_project",
    )(own, peer, w_own, w_peer)


def weight_body(part, normed_t_ref, grad_t_ref, d_ref, mixed_ref, out_ref):
    tok, col = mixed_ref.shape
    owners, share = out_ref.shape[0], out_ref.shape[1] // 5
    half = owners // 2
    rows = pl.ds(part * half * share, half * share)
    value = jnp.dot(normed_t_ref[rows, :], d_ref[pl.ds(0, tok), :], preferred_element_type=F32)
    last = jnp.dot(grad_t_ref[rows, :], mixed_ref[...], preferred_element_type=F32)
    for c in range(5):
        piece = value[:, c * col:(c + 1) * col] if c < 4 else last
        out_ref[pl.ds(part * half, half), pl.ds(c * share, share), :] = piece.astype(BF16).reshape(half, share, col)


def weight_sum_body(parts_ref, out_ref):
    total = parts_ref[0].astype(F32)
    for index in range(1, parts_ref.shape[0]):
        total = total + parts_ref[index].astype(F32)
    out_ref[...] = jnp.broadcast_to(total.astype(BF16)[None], out_ref.shape)


def weight_sum(parts):
    return kernel_call(weight_sum_body, shape_of(parts.shape, BF16), "weight_sum")(parts)


def prepare_body(length_ref, x_ref, cot_ref, gain_ref, inv_rms_ref, normed_t_ref, grad_t_ref):
    step = x_ref.shape[0]
    normed = (x_ref[...].astype(F32) * inv_rms_ref[:, :1] * gain_ref[...]).astype(BF16)
    normed_t_ref[...] = normed.T
    first = (lax.axis_index("seq") * pl.num_programs(0) + pl.program_id(0)) * step
    valid = lax.broadcasted_iota(jnp.int32, (step, 1), 0) + first < length_ref[0]
    grad_t_ref[...] = jnp.where(valid, cot_ref[...].astype(F32), 0.0).astype(BF16).T


def prepare(lengths, x, cot, gain, inv_rms):
    tok, width = x.shape
    col = inv_rms.shape[1]
    step = tok // 4
    row = lambda i, n: (i, 0)
    column = lambda i, n: (0, i)
    return kernel_call(
        prepare_body,
        (shape_of((width, tok), BF16), shape_of((width, tok), BF16)),
        "prepare",
        vmem=63,
        grid_spec=pltpu.PrefetchScalarGridSpec(
            num_scalar_prefetch=1,
            grid=(4,),
            in_specs=[
                pl.BlockSpec((step, width), row),
                pl.BlockSpec((step, width), row),
                pl.BlockSpec((1, width), lambda i, n: (0, 0)),
                pl.BlockSpec((step, col), row),
            ],
            out_specs=[pl.BlockSpec((width, step), column), pl.BlockSpec((width, step), column)],
        ),
    )(lengths, x, cot, gain.reshape(1, -1), inv_rms)


def fill_slots(slot_ref, item_ref, value_ref, blocks, owners, extra):
    room = blocks[0].shape[0] - EXTRA
    tok = slot_ref.shape[1]
    group = 4
    local = lax.broadcasted_iota(jnp.int32, (room, tok), 0)
    for first in range(0, len(blocks), group):
        hots = [jnp.where(slot_ref[...] == local + owner * room, 1.0, 0.0) for owner in owners[first:first + group]]
        hot = jnp.concatenate(hots, axis=0).astype(BF16)
        moved = jnp.dot(hot, value_ref[...], preferred_element_type=F32).astype(BF16)
        items = lax.dot_general(item_ref[...], hot, NT, preferred_element_type=F32)
        for index in range(group):
            span = slice(index * room, (index + 1) * room)
            block = blocks[first + index]
            block[pl.ds(0, room), :] = moved[span]
            block[pl.ds(room, EXTRA), :] = (extra + items[:, span]).astype(BF16)


def fill_all(slot_ref, item_ref, value_ref, out_ref, extra):
    owners = list(range(out_ref.shape[0]))
    fill_slots(slot_ref, item_ref, value_ref, [out_ref.at[owner] for owner in owners], owners, extra)


def slots_for(id_ref, rank_ref, slot_ref, item_ref, items, room):
    tok = id_ref.shape[1]
    ids = id_ref[...]
    owner = ids // items
    offset = ids - owner * items
    across = jnp.broadcast_to(owner.astype(F32), (8, tok)).T[:, :1]
    before = lax.broadcasted_iota(jnp.int32, (tok, tok), 0) < lax.broadcasted_iota(jnp.int32, (tok, tok), 1)
    same = jnp.where(before & (across == owner.astype(F32)), 1.0, 0.0)
    rank = jnp.sum(same, axis=0, keepdims=True).astype(jnp.int32)
    rank_ref[...] = rank
    slot_ref[...] = jnp.where(rank < room, owner * room + rank, -1)
    high = offset // 32
    row = lax.broadcasted_iota(jnp.int32, item_ref.shape, 0)
    rows = jnp.zeros(item_ref.shape, F32)
    for index, value in ((2, high + 1), (3, offset - high * 32), (5, rank // room + 1)):
        rows = jnp.where(row == index, jnp.broadcast_to(value.astype(F32), rows.shape), rows)
    item_ref[...] = rows.astype(BF16)


def input_grad_body(length_ref, *refs, items):
    parts = refs[:4]
    x_any, cot_any, gain_any, inv_rms_ref, id_ref, value_ref = refs[4:10]
    outs, (rank_ref, item_ref) = refs[10:14], refs[14:16]
    x_bf_ref, cot_ref, gain_ref, x_ref, slot_ref, sems = refs[16:]
    tok, col = x_ref.shape
    room = outs[0].shape[1] - EXTRA
    mine = pl.ds(pl.multiple_of(lax.axis_index("col") * col, col), col)
    copies = [
        pltpu.make_async_copy(source.at[:, mine], place, sems.at[n])
        for n, (source, place) in enumerate(((x_any, x_bf_ref), (cot_any, cot_ref), (gain_any, gain_ref)))
    ]
    for copy in copies:
        copy.start()
    slots_for(id_ref, rank_ref, slot_ref, item_ref, items, room)
    for copy in copies:
        copy.wait()
    x_ref[...] = x_bf_ref[...].astype(F32) * inv_rms_ref[...]
    first = lax.axis_index("seq") * tok
    d_normed = parts[0][pl.ds(0, tok), :].astype(F32)
    for part in parts[1:]:
        d_normed = d_normed + part[pl.ds(0, tok), :].astype(F32)
    gain_sum = two_rows(jnp.sum(d_normed * x_ref[...], axis=0, keepdims=True)).astype(F32)
    extra = [part[pl.ds(tok, EXTRA), :] for part in parts]
    row = lax.broadcasted_iota(jnp.int32, (EXTRA, col), 0)
    for tile in range(tok // BLOCK):
        rows = pl.ds(tile * BLOCK, BLOCK)
        pick = jnp.where((row >= 4 * tile) & (row < 4 * tile + 4), 1.0, 0.0).astype(BF16)
        mean = jnp.zeros((BLOCK, col), F32)
        for piece in extra:
            mean = mean + lax.dot_general(piece, pick, TN, preferred_element_type=F32)
        inv = inv_rms_ref[rows, :]
        d_t = d_normed[tile * BLOCK:(tile + 1) * BLOCK]
        mean = mean * inv * (1.0 / (8 * col))
        valid = lax.broadcasted_iota(jnp.int32, (BLOCK, 1), 0) + (first + tile * BLOCK) < length_ref[0]
        grad = jnp.where(valid, cot_ref[rows, :].astype(F32), 0.0)
        value = inv * (d_t * gain_ref[...] - x_ref[rows, :] * mean) + grad
        value_ref[rows, :] = value.astype(BF16)
    rounds = jnp.max(item_ref[pl.ds(5, 1), :].astype(F32), axis=1, keepdims=True)
    seq = lax.axis_index("seq")
    z_pos, x_pos = seq // 4 * 2 + lax.axis_index("dp"), lax.rem(seq, 4)
    spots = [(dx, dz) for dx in range(4) for dz in range(4)]
    owners = [plane_rank(lax.rem(z_pos + dz, 4), lax.rem(x_pos + dx, 4)) for dx, dz in spots]
    places = [outs[dx].at[dz] for dx, dz in spots]
    fill_slots(slot_ref, item_ref, value_ref, places, owners, gain_sum + jnp.where(row == 4, rounds, 0.0))


def input_grads(lengths, parts, x, cot, gain, inv_rms, ids, items, room):
    tok, col = inv_rms.shape
    whole, anywhere = pl.BlockSpec(memory_space=pltpu.VMEM), pl.BlockSpec(memory_space=pl.ANY)
    return kernel_call(
        functools.partial(input_grad_body, items=items),
        (
            shape_of((tok, col), BF16),
            *(shape_of((4, room + EXTRA, col), BF16) for _ in range(4)),
            shape_of((1, tok), jnp.int32),
            shape_of((EXTRA, tok), BF16),
        ),
        "input_grads",
        in_specs=[pl.BlockSpec(memory_space=pltpu.SMEM)] + [whole] * 4 + [anywhere] * 3 + [whole] * 2,
        scratch_shapes=[
            pltpu.VMEM((tok, col), BF16),
            pltpu.VMEM((tok, col), BF16),
            pltpu.VMEM((1, col), F32),
            pltpu.VMEM((tok, col), F32),
            pltpu.VMEM((1, tok), jnp.int32),
            pltpu.SemaphoreType.DMA((3,)),
        ],
    )(lengths, *parts, x, cot, gain.reshape(1, -1), inv_rms, ids)


def more_body(slot_ref, item_ref, value_ref, out_ref):
    fill_all(slot_ref, item_ref, value_ref, out_ref, 0.0)


def more_slots(slots, items, values, owners, room):
    col = values.shape[1]
    return kernel_call(more_body, shape_of((owners, room + EXTRA, col), BF16), "more_slots", vmem=63)(slots, items, values)


def rows_total(blocks, first, count):
    room = blocks[0].shape[0] - EXTRA
    total = jnp.zeros((count, blocks[0].shape[1]), F32)
    row = lax.broadcasted_iota(jnp.int32, (count, room), 0) + first
    for pair in range(0, len(blocks), 2):
        hots, data = [], []
        for block in blocks[pair:pair + 2]:
            extra = block[pl.ds(room, EXTRA), :].astype(F32)
            item = ((extra[2:3] - 1.0) * 32.0 + extra[3:4]).astype(jnp.int32)
            hots.append(jnp.where(item == row, 1.0, 0.0).astype(BF16))
            data.append(block[pl.ds(0, room), :])
        total = total + jnp.dot(
            jnp.concatenate(hots, axis=1), jnp.concatenate(data, axis=0), preferred_element_type=F32
        )
    return total


def finish_body(*refs):
    gots, whole_ref, (in_ref, out_ref, table_out, gain_ref, rounds_ref, table_ref, sems) = refs[:4], refs[4], refs[5:]
    step = pl.program_id(0)
    count, (_, rows, col) = table_ref.shape[1], whole_ref.shape
    share = rows // 5
    lasts = []
    for index in range(whole_ref.shape[0]):
        for c in range(4):
            in_ref[c, pl.ds(index * share, share), :] = whole_ref[index, pl.ds(c * share, share), :].astype(F32)
        lasts.append(whole_ref[index, pl.ds(4 * share, share), :].astype(F32))
    out_ref[...] = jnp.concatenate(lasts, axis=0).T
    blocks = [got.at[index] for got in gots for index in range(got.shape[0])]
    table_ref[step] = rows_total(blocks, step * count, count)

    def leaving(index):
        return pltpu.make_async_copy(table_ref.at[index], table_out.at[pl.ds(index * count, count)], sems.at[index])

    leaving(step).start()
    extra = [block[pl.ds(BLOCK, EXTRA), :].astype(F32) for block in blocks]
    total = functools.reduce(lambda a, b: a + b, extra)
    gain_ref[...] = total[0:1] + total[1:2]
    rounds_ref[0] = jnp.max(functools.reduce(jnp.maximum, extra)[4:5]).astype(jnp.int32)

    @pl.when(step == pl.num_programs(0) - 1)
    def _():
        for index in range(table_ref.shape[0]):
            leaving(index).wait()


def finish(gots, whole, items):
    owners, rows, col = whole.shape
    width, steps = 8 * col, 4
    return kernel_call(
        finish_body,
        (
            shape_of((4, width, col), F32),
            shape_of((col, width), F32),
            shape_of((items, col), F32),
            shape_of((1, col), F32),
            shape_of((1,), jnp.int32),
        ),
        "finish",
        grid=(steps,),
        in_specs=[pl.BlockSpec(got.shape, lambda i: (0, 0, 0)) for got in gots]
        + [pl.BlockSpec((owners // steps, rows, col), lambda i: (i, 0, 0))],
        out_specs=[
            pl.BlockSpec((4, width // steps, col), lambda i: (0, i, 0)),
            pl.BlockSpec((col, width // steps), lambda i: (0, i)),
            pl.BlockSpec(memory_space=pltpu.HBM),
            pl.BlockSpec((1, col), lambda i: (0, 0)),
            pl.BlockSpec(memory_space=pltpu.SMEM),
        ],
        scratch_shapes=[pltpu.VMEM((steps, items // steps, col), F32), pltpu.SemaphoreType.DMA((steps,))],
    )(*gots, whole)


def more_table_body(got_ref, table_ref, out_ref):
    count = 2 * BLOCK
    blocks = [got_ref.at[index] for index in range(got_ref.shape[0])]
    for first in range(0, table_ref.shape[0], count):
        rows = pl.ds(first, count)
        out_ref[rows, :] = table_ref[rows, :] + rows_total(blocks, first, count)


def more_table(got, table):
    return kernel_call(more_table_body, shape_of(table.shape, F32), "more_table", vmem=63)(got, table)


def per_device(inputs, cotangent, norm_gain, proj_in, proj_out, item_ids, lengths, tile_mask):
    x_rows, cot_rows = inputs[0], cotangent[0]
    mask = tile_mask[0]
    tok = x_rows.shape[0]
    col = proj_in.shape[2]
    scale = 1.0 / math.sqrt(col)
    owners, items, room = 16, 1024, BLOCK
    seq = lax.axis_index("seq")
    own, cross, near1, near2, near3, pre, dmix, upd, inv_cnt, inv_rms = project(
        lengths, x_rows, cot_rows, norm_gain, proj_in, proj_out, mask
    )

    across = move_seq(cross, 1, 0)
    near = [move_seq(block, 0, k) for block, k in ((near1, 1), (near3, 3), (near2, 2))]
    far = [move_seq(across, 0, k) for k in (1, 3, 2)]

    proj_peer = move_core(proj_in)
    x_now, cot_now, across = lax.optimization_barrier((x_rows, cot_rows, across))
    normed_t, grad_t = prepare(lengths, x_now, cot_now, norm_gain, inv_rms)
    acc, w_own, w_peer = near_terms(lengths, own, mask, proj_in, proj_peer, [across] + near, scale)
    d_own, shares = far_terms(
        lengths, own, mask, far, acc, pre, inv_rms, dmix, upd, inv_cnt, normed_t, grad_t, owners, scale
    )
    d_peer = move_core(d_own)
    shares = swap_plane(shares)
    parts = back_project(d_own, d_peer, w_own, w_peer, col)
    parts = [parts[0]] + [move_y(parts[k], k) for k in (1, 3, 2)]

    d_inputs, *sends, rank, item_rows = input_grads(
        lengths, parts, x_rows, cot_rows, norm_gain, inv_rms, item_ids, items, room
    )
    line = [sends[0]] + [move_plane(sends[k], 0, k) for k in (1, 3, 2)]
    sends = [jnp.stack([block[k] for block in line]) for k in range(4)]
    gots = [sends[0]] + [move_plane(sends[k], k, 0) for k in (1, 3, 2)]
    grad_in_w, grad_out_w, table, gain, rounds = finish(gots, swap_plane(weight_sum(shares)), items)

    def another(state):
        turn, total = state
        at = rank - turn * room
        slots = jnp.where((at >= 0) & (at < room), item_ids // items * room + at, -1)
        got = swap_plane(more_slots(slots, item_rows, d_inputs, owners, room))
        return turn + 1, more_table(got, total)

    _, table = lax.while_loop(lambda state: state[0] < rounds[0], another, (jnp.int32(1), table))
    return (grad_in_w, grad_out_w, gain[0], table)


def solution(mesh):
    placed = (
        P("dp", "seq", None),
        P("dp", "seq", None),
        P(),
        P(None, None, "col"),
        P("col", None),
        P("dp", "seq"),
        P("dp"),
        P("dp", None, None),
    )
    return jax.shard_map(
        per_device,
        mesh=mesh,
        in_specs=placed,
        out_specs=(P(None, None, "col"), P("col", None), P("col"), P(("dp", "seq"), "col")),
        check_vma=False,
    )
```

```python
import functools
import math

import jax
import jax.numpy as jnp
from jax import lax
from jax.experimental import pallas as pl
from jax.experimental.pallas import tpu as pltpu
from jax.sharding import PartitionSpec as P

BLOCK = 128
EPSILON = 1e-06
BF16 = jnp.bfloat16
F32 = jnp.float32
MIB = 1024 * 1024
EXTRA = 16
NT = (((1,), (1,)), ((), ()))
TN = (((0,), (0,)), ((), ()))


def kernel_call(body, out_shape, name, flops=1000, bytes_accessed=1000, vmem=24, **kwargs):
    return pl.pallas_call(
        body,
        out_shape=out_shape,
        name=name,
        compiler_params=pltpu.CompilerParams(vmem_limit_bytes=vmem * MIB),
        cost_estimate=pl.CostEstimate(flops=flops, bytes_accessed=bytes_accessed, transcendentals=0),
        **kwargs,
    )


def shape_of(shape, dtype):
    return jax.ShapeDtypeStruct(shape, dtype)


def swap_plane(value):
    return lax.all_to_all(value, ("dp", "seq"), 0, 0, tiled=True)


def plane_rank(z, x):
    return (z % 2) * 8 + (z // 2) * 4 + x


def move_plane(value, dz, dx):
    pairs = []
    for z in range(4):
        for x in range(4):
            pairs.append((plane_rank(z, x), plane_rank((z + dz) % 4, (x + dx) % 4)))
    return lax.ppermute(value, ("dp", "seq"), pairs)


def move_seq(value, dz_hi, dx):
    pairs = [(i, ((i // 4 + dz_hi) % 2) * 4 + (i % 4 + dx) % 4) for i in range(8)]
    return lax.ppermute(value, "seq", pairs)


def move_y(value, dy):
    return lax.ppermute(value, "col", [(i, ((i // 2 + dy) % 4) * 2 + i % 2) for i in range(8)])


def move_core(value):
    return lax.ppermute(value, "col", [(i, i ^ 1) for i in range(8)])


def project_body(length_ref, x_ref, cot_ref, gain_ref, proj_ref, out_ref, mask_ref,
                 own_ref, cross_ref, near1_ref, near2_ref, near3_ref, pre_ref, dmix_ref, upd_ref, inv_cnt_ref, inv_rms_ref, both_ref):
    length, rank = length_ref[0], lax.axis_index("seq")
    step, col = dmix_ref.shape

    @pl.when(pl.program_id(0) == 0)
    def _():
        for c in range(4):
            both_ref[:, pl.ds(c * col, col)] = proj_ref[c]

    x = x_ref[...].astype(F32)
    inv_rms = lax.rsqrt(jnp.mean(x * x, axis=1, keepdims=True) + EPSILON)
    normed = (x * inv_rms * gain_ref[...]).astype(BF16)
    inv_rms_ref[...] = jnp.broadcast_to(inv_rms, inv_rms_ref.shape)
    pre = jnp.dot(normed, both_ref[...], preferred_element_type=F32)
    act = (pre * jax.nn.sigmoid(pre)).astype(BF16)
    for c in range(4):
        pre_ref[c] = pre[:, c * col:(c + 1) * col]
    tile = (rank * pl.num_programs(0) + pl.program_id(0)) * (step // BLOCK)
    local = lax.broadcasted_iota(jnp.int32, (step, 1), 0)
    position = tile * BLOCK + local
    grad = jnp.where(position < length, cot_ref[...].astype(F32), 0.0).astype(BF16)
    d_mixed = lax.dot_general(grad, out_ref[...], NT, preferred_element_type=F32)
    dmix_ref[...] = d_mixed
    update = act[:, :col]
    upd_ref[...] = update
    tiles = mask_ref.shape[0]
    rows = lax.broadcasted_iota(jnp.int32, (tiles, tiles), 0)
    cols = lax.broadcasted_iota(jnp.int32, (tiles, tiles), 1)
    filled = jnp.clip(length - BLOCK * cols, 0, BLOCK)
    counted = jnp.where(cols < rows, mask_ref[...] * filled, 0)
    earlier = jnp.zeros((step, 1), F32)
    for index in range(step // BLOCK):
        picked = jnp.where(rows == tile + index, counted, 0).astype(F32)
        total = jnp.sum(jnp.sum(picked, axis=1, keepdims=True), axis=0, keepdims=True)
        earlier = jnp.where(local // BLOCK == index, total, earlier)
    own_first = tile * BLOCK + local // BLOCK * BLOCK
    diagonal = jnp.minimum(local % BLOCK + 1, jnp.clip(length - own_first, 0, BLOCK)).astype(F32)
    inv_cnt = 1.0 / jnp.maximum(earlier + diagonal, 1.0)
    inv_cnt_ref[...] = jnp.broadcast_to(inv_cnt, inv_cnt_ref.shape)
    qd = (act[:, col:2 * col], (d_mixed * update.astype(F32) * inv_cnt).astype(BF16))
    kv = (act[:, 2 * col:3 * col], act[:, 3 * col:])
    for index in range(2):
        own_ref[0, index], own_ref[1, index] = qd[index], kv[index]
    x_pos = lax.rem(rank, 4)
    later = [rank < 4] + [x_pos + k < 4 for k in (1, 2, 3)]
    for ref, is_later in zip((cross_ref, near1_ref, near2_ref, near3_ref), later):

        @pl.when(is_later)
        def _():
            ref[0], ref[1] = kv

        @pl.when(jnp.logical_not(is_later))
        def _():
            ref[0], ref[1] = qd


def project(lengths, x, cot, gain, proj_in, proj_out, mask):
    tok, width = x.shape
    col = proj_in.shape[2]
    step = 2 * BLOCK
    row = lambda i, w: (i, 0)
    side = lambda i, w: (0, i, 0)
    pair = lambda i, w: (0, 0, i, 0)
    fixed2 = lambda i, w: (0, 0)
    return kernel_call(
        project_body,
        (
            shape_of((2, 2, tok, col), BF16),
            *(shape_of((2, tok, col), BF16) for _ in range(4)),
            shape_of((4, tok, col), F32),
            shape_of((tok, col), F32),
            shape_of((tok, col), BF16),
            shape_of((tok, col), F32),
            shape_of((tok, col), F32),
        ),
        "project",
        vmem=63,
        grid_spec=pltpu.PrefetchScalarGridSpec(
            num_scalar_prefetch=1,
            grid=(tok // step,),
            in_specs=[
                pl.BlockSpec((step, width), row),
                pl.BlockSpec((step, width), row),
                pl.BlockSpec((1, width), fixed2),
                pl.BlockSpec((4, width, col), lambda i, w: (0, 0, 0)),
                pl.BlockSpec((col, width), fixed2),
                pl.BlockSpec(mask.shape, fixed2),
            ],
            out_specs=[
                pl.BlockSpec((2, 2, step, col), pair),
                *(pl.BlockSpec((2, step, col), side) for _ in range(4)),
                pl.BlockSpec((4, step, col), side),
                pl.BlockSpec((step, col), row),
                pl.BlockSpec((step, col), row),
                pl.BlockSpec((step, col), row),
                pl.BlockSpec((step, col), row),
            ],
            scratch_shapes=[pltpu.VMEM((width, 4 * col), BF16)],
        ),
    )(lengths, x, cot, gain.reshape(1, -1), proj_in, proj_out, mask)


def block_terms(a1, a2, b1, b2, keep, scale):
    half = lax.dot_general(a1, b1, NT, preferred_element_type=F32) * (keep * (0.5 * scale))
    other = lax.dot_general(a2, b2, NT, preferred_element_type=F32) * keep
    tanh = jnp.tanh(half)
    twice = 1.0 + tanh
    probs = half * twice
    slope = (other * (twice + probs * (1.0 - tanh))).astype(BF16)
    first = jnp.dot(probs.astype(BF16), b2, preferred_element_type=F32)
    second = jnp.dot(slope, b1, preferred_element_type=F32)
    return first, second


def block_sums(side, own_ref, other, keep_of, scale):
    tok, col = own_ref.shape[2:]
    part = 2 * BLOCK
    first, second = jnp.zeros((tok, col), F32), jnp.zeros((tok, col), F32)
    for start in range(0, tok, part):
        span = pl.ds(start, part)
        terms = block_terms(
            own_ref[side, 0], own_ref[side, 1], other[0][span, :], other[1][span, :], keep_of(start, part), scale
        )
        first, second = first + terms[0], second + terms[1]
    return first, second


def kept_tiles(mask_ref, length_ref, rank, tiles):
    count = mask_ref.shape[0]
    row = lax.broadcasted_iota(jnp.int32, (count, count), 0)
    column = lax.broadcasted_iota(jnp.int32, (count, count), 1)
    kept = jnp.where(column * BLOCK < length_ref[0], mask_ref[...].astype(F32), 0.0).astype(BF16)
    own = jnp.where(row + rank * tiles == column, 1.0, 0.0).astype(BF16)
    as_query = jnp.dot(own, kept, preferred_element_type=F32)
    as_key = lax.dot_general(own, kept, NT, preferred_element_type=F32)
    return as_query.astype(BF16), as_key.astype(BF16)


def keep_rows(kept, other, tiles, tok):
    count = kept.shape[0]
    row = lax.broadcasted_iota(jnp.int32, (count, tok), 0)
    column = lax.broadcasted_iota(jnp.int32, (count, tok), 1)
    spread = jnp.where(row == other * tiles + column // BLOCK, 1.0, 0.0).astype(BF16)
    return jnp.dot(kept, spread, preferred_element_type=F32)[:tiles]


def far_sums(other, rank, kept, own_ref, other_ref, scale):
    tok = own_ref.shape[2]
    tiles = tok // BLOCK
    side = jnp.where(other > rank, 1, 0)
    rows = jnp.where(other > rank, kept[1].astype(F32), kept[0].astype(F32)).astype(BF16)
    keep = keep_rows(rows, other, tiles, tok)

    def keep_of(start, part):
        return by_tile(keep[:, start:start + part], tok)

    return side, block_sums(side, own_ref, (other_ref.at[0], other_ref.at[1]), keep_of, scale)


def rank_at(rank, dz, dx):
    return lax.rem(rank // 4 + dz, 2) * 4 + lax.rem(rank + 4 - dx, 4)


def by_tile(rows, tok):
    tiles, part = rows.shape
    return jnp.broadcast_to(rows[:, None, :], (tiles, tok // tiles, part)).reshape(tok, part)


def near_body(length_ref, own_ref, mask_ref, proj_own_ref, proj_peer_ref, *refs, scale):
    others, (acc_ref, w_own_ref, w_peer_ref, sems) = refs[:-4], refs[-4:]
    tok, col = own_ref.shape[2:]
    place = lax.axis_index("col")
    picks = []
    for proj_ref, w_ref in ((proj_own_ref, w_own_ref), (proj_peer_ref, w_peer_ref)):
        for k in range(4):
            first = (lax.rem(place // 2 + k, 4) * 2 + lax.rem(place, 2)) * col
            rows = pl.ds(pl.multiple_of(first, col), col)
            for c in range(4):
                spot = w_ref.at[pl.ds(k * col, col), pl.ds(c * col, col)]
                picks.append(pltpu.make_async_copy(proj_ref.at[c, rows], spot, sems.at[len(picks)]))
    for pick in picks:
        pick.start()
    tiles = tok // BLOCK
    rank = lax.axis_index("seq")
    kept = kept_tiles(mask_ref, length_ref, rank, tiles)
    for side in range(2):
        other = own_ref.at[1 - side, 0], own_ref.at[1 - side, 1]
        rows = keep_rows(kept[side], rank, tiles, tok)

        def keep_of(start, part):
            row = lax.broadcasted_iota(jnp.int32, (tok, part), 0)
            column = lax.broadcasted_iota(jnp.int32, (tok, part), 1) + start
            ordered = (column <= row) if side == 0 else (row <= column)
            return jnp.where(ordered, by_tile(rows[:, start:start + part], tok), 0.0)

        acc_ref[side, 0], acc_ref[side, 1] = block_sums(side, own_ref, other, keep_of, scale)
    places = [(1, 0), (0, 1), (0, 3), (0, 2)]
    for (dz, dx), other in zip(places, others):
        side, sums = far_sums(rank_at(rank, dz, dx), rank, kept, own_ref, other, scale)
        acc_ref[side, 0] += sums[0]
        acc_ref[side, 1] += sums[1]
    for pick in picks:
        pick.wait()


def near_terms(lengths, own, mask, proj_own, proj_peer, others, scale):
    whole, anywhere = pl.BlockSpec(memory_space=pltpu.VMEM), pl.BlockSpec(memory_space=pl.ANY)
    depth = 4 * proj_own.shape[2]
    return kernel_call(
        functools.partial(near_body, scale=scale),
        (shape_of(own.shape, F32), shape_of((depth, depth), BF16), shape_of((depth, depth), BF16)),
        "near_terms",
        vmem=40,
        in_specs=[pl.BlockSpec(memory_space=pltpu.SMEM)] + [whole] * 2 + [anywhere] * 2 + [whole] * len(others),
        out_specs=[whole] * 3,
        scratch_shapes=[pltpu.SemaphoreType.DMA((32,))],
    )(lengths, own, mask, proj_own, proj_peer, *others)


FAR_INPUTS = 13


def far_body(length_ref, *refs, scale):
    sources, d_out, parts_out = refs[:FAR_INPUTS], refs[FAR_INPUTS], refs[FAR_INPUTS + 1]
    held = refs[FAR_INPUTS + 2:2 * FAR_INPUTS + 2]
    mixed_ref, d_ref, parts_ref, sems, out_sems = refs[2 * FAR_INPUTS + 2:]
    copies = [pltpu.make_async_copy(source, place, sems.at[n]) for n, (source, place) in enumerate(zip(sources, held))]
    for copy in copies:
        copy.start()
    own_ref, mask_ref = held[:2]
    rank = lax.axis_index("seq")
    others, acc_ref = held[2:5], held[5]
    pre_ref, inv_rms_ref, dmix_ref, upd_ref, inv_cnt_ref, normed_t_ref, grad_t_ref = held[6:]
    copies[0].wait()
    copies[1].wait()
    kept = kept_tiles(mask_ref, length_ref, rank, own_ref.shape[2] // BLOCK)
    for index, (dx, other) in enumerate(zip((1, 3, 2), others)):
        copies[2 + index].wait()
        side, sums = far_sums(rank_at(rank, 1, dx), rank, kept, own_ref, other, scale)
        if index == 0:
            copies[5].wait()
        acc_ref[side, 0] += sums[0]
        acc_ref[side, 1] += sums[1]
    for copy in copies[6:11]:
        copy.wait()
    pre_grad_body(acc_ref, pre_ref, inv_rms_ref, dmix_ref, upd_ref, inv_cnt_ref, d_ref, mixed_ref, scale=scale)
    leaving = [pltpu.make_async_copy(d_ref, d_out, out_sems.at[0])]
    leaving[0].start()
    for copy in copies[11:]:
        copy.wait()
    half = parts_ref.shape[0] // 2
    for part in range(2):
        weight_body(part, normed_t_ref, grad_t_ref, d_ref, mixed_ref, parts_ref)
        owners = pl.ds(part * half, half)
        leaving.append(pltpu.make_async_copy(parts_ref.at[owners], parts_out.at[owners], out_sems.at[part + 1]))
        leaving[-1].start()
    for copy in leaving:
        copy.wait()


def far_terms(lengths, own, mask, others, acc, pre, inv_rms, dmix, upd, inv_cnt, normed_t, grad_t, owners, scale):
    _, _, tok, col = own.shape
    width = normed_t.shape[0]
    sources = (own, mask, *others, acc, pre, inv_rms, dmix, upd, inv_cnt, normed_t, grad_t)
    return kernel_call(
        functools.partial(far_body, scale=scale),
        (shape_of((tok + EXTRA, 4 * col), BF16), shape_of((owners, 5 * width // owners, col), BF16)),
        "far_terms",
        vmem=40,
        in_specs=[pl.BlockSpec(memory_space=pltpu.SMEM)] + [pl.BlockSpec(memory_space=pl.ANY)] * len(sources),
        out_specs=[pl.BlockSpec(memory_space=pl.ANY)] * 2,
        scratch_shapes=[
            *(pltpu.VMEM(source.shape, source.dtype) for source in sources),
            pltpu.VMEM((tok, col), BF16),
            pltpu.VMEM((tok + EXTRA, 4 * col), BF16),
            pltpu.VMEM((owners, 5 * width // owners, col), BF16),
            pltpu.SemaphoreType.DMA((len(sources),)),
            pltpu.SemaphoreType.DMA((3,)),
        ],
    )(lengths, *sources)


def pre_grad_body(acc_ref, pre_ref, inv_rms_ref, dmix_ref, upd_ref, inv_cnt_ref, d_ref, mixed_ref, *, scale):
    tok, col = dmix_ref.shape
    stat = jnp.zeros((tok, col), F32)
    attended = acc_ref[0, 0] * inv_cnt_ref[...]
    mixed_ref[...] = (attended * upd_ref[...].astype(F32)).astype(BF16)
    grads = (
        dmix_ref[...] * attended,
        acc_ref[0, 1] * (0.5 * scale),
        acc_ref[1, 1] * (0.5 * scale),
        acc_ref[1, 0],
    )
    for c in range(4):
        pre = pre_ref[c]
        sig = jax.nn.sigmoid(pre)
        d_pre = (grads[c] * (sig * (1.0 + pre * (1.0 - sig)))).astype(BF16)
        d_ref[pl.ds(0, tok), pl.ds(c * col, col)] = d_pre
        stat = stat + d_pre.astype(F32) * pre
    stat = stat / inv_rms_ref[...]
    high = stat.astype(BF16)
    low = (stat - high.astype(F32)).astype(BF16)
    ones = jnp.ones((8, col), BF16)
    sums = lax.dot_general(ones, high, NT, preferred_element_type=F32)
    sums = sums + lax.dot_general(ones, low, NT, preferred_element_type=F32)
    d_ref[pl.ds(tok, EXTRA), :] = two_rows(sums[0:1])


def two_rows(value):
    high = value.astype(BF16).astype(F32)
    low = value - high
    row = lax.broadcasted_iota(jnp.int32, (EXTRA, value.shape[1]), 0)
    both = jnp.where(row == 0, jnp.broadcast_to(high, row.shape), jnp.where(row == 1, jnp.broadcast_to(low, row.shape), 0.0))
    return both.astype(BF16)


def back_body(own_ref, peer_ref, w_own_ref, w_peer_ref, *outs):
    tok = own_ref.shape[0] - EXTRA
    part = lax.dot_general(own_ref[pl.ds(0, tok), :], w_own_ref[...], NT, preferred_element_type=F32)
    part = part + lax.dot_general(peer_ref[pl.ds(0, tok), :], w_peer_ref[...], NT, preferred_element_type=F32)
    sums = jnp.sum(
        own_ref[pl.ds(tok, EXTRA), :].astype(F32) + peer_ref[pl.ds(tok, EXTRA), :].astype(F32), axis=0, keepdims=True
    )
    high = sums.astype(BF16).astype(F32)
    low = sums - high
    col = outs[0].shape[1]
    row = lax.broadcasted_iota(jnp.int32, (EXTRA, col), 0)
    extra = jnp.zeros((EXTRA, col), F32)
    for tile in range(tok // BLOCK):
        span = slice(tile * BLOCK, (tile + 1) * BLOCK)
        extra = jnp.where(row == 4 * tile, jnp.broadcast_to(high[:, span], row.shape), extra)
        extra = jnp.where(row == 4 * tile + 1, jnp.broadcast_to(low[:, span], row.shape), extra)
    extra = extra.astype(BF16)
    for k, out in enumerate(outs):
        out[pl.ds(0, tok), :] = part[:, k * col:(k + 1) * col].astype(BF16)
        out[pl.ds(tok, EXTRA), :] = extra


def back_project(own, peer, w_own, w_peer, col):
    rows, depth = own.shape
    return kernel_call(
        back_body,
        tuple(shape_of((rows, col), BF16) for _ in range(4)),
        "back_project",
    )(own, peer, w_own, w_peer)


def weight_body(part, normed_t_ref, grad_t_ref, d_ref, mixed_ref, out_ref):
    tok, col = mixed_ref.shape
    owners, share = out_ref.shape[0], out_ref.shape[1] // 5
    half = owners // 2
    rows = pl.ds(part * half * share, half * share)
    value = jnp.dot(normed_t_ref[rows, :], d_ref[pl.ds(0, tok), :], preferred_element_type=F32)
    last = jnp.dot(grad_t_ref[rows, :], mixed_ref[...], preferred_element_type=F32)
    for c in range(5):
        piece = value[:, c * col:(c + 1) * col] if c < 4 else last
        out_ref[pl.ds(part * half, half), pl.ds(c * share, share), :] = piece.astype(BF16).reshape(half, share, col)


def weight_sum_body(parts_ref, out_ref):
    total = parts_ref[0].astype(F32)
    for index in range(1, parts_ref.shape[0]):
        total = total + parts_ref[index].astype(F32)
    out_ref[...] = jnp.broadcast_to(total.astype(BF16)[None], out_ref.shape)


def weight_sum(parts):
    return kernel_call(weight_sum_body, shape_of(parts.shape, BF16), "weight_sum")(parts)


def prepare_body(length_ref, x_ref, cot_ref, gain_ref, inv_rms_ref, normed_t_ref, grad_t_ref):
    step = x_ref.shape[0]
    normed = (x_ref[...].astype(F32) * inv_rms_ref[:, :1] * gain_ref[...]).astype(BF16)
    normed_t_ref[...] = normed.T
    first = (lax.axis_index("seq") * pl.num_programs(0) + pl.program_id(0)) * step
    valid = lax.broadcasted_iota(jnp.int32, (step, 1), 0) + first < length_ref[0]
    grad_t_ref[...] = jnp.where(valid, cot_ref[...].astype(F32), 0.0).astype(BF16).T


def prepare(lengths, x, cot, gain, inv_rms):
    tok, width = x.shape
    col = inv_rms.shape[1]
    step = tok // 4
    row = lambda i, n: (i, 0)
    column = lambda i, n: (0, i)
    return kernel_call(
        prepare_body,
        (shape_of((width, tok), BF16), shape_of((width, tok), BF16)),
        "prepare",
        vmem=40,
        grid_spec=pltpu.PrefetchScalarGridSpec(
            num_scalar_prefetch=1,
            grid=(4,),
            in_specs=[
                pl.BlockSpec((step, width), row),
                pl.BlockSpec((step, width), row),
                pl.BlockSpec((1, width), lambda i, n: (0, 0)),
                pl.BlockSpec((step, col), row),
            ],
            out_specs=[pl.BlockSpec((width, step), column), pl.BlockSpec((width, step), column)],
        ),
    )(lengths, x, cot, gain.reshape(1, -1), inv_rms)


def fill_slots(slot_ref, item_ref, value_ref, blocks, owners, extra):
    room = blocks[0].shape[0] - EXTRA
    tok = slot_ref.shape[1]
    group = 4
    local = lax.broadcasted_iota(jnp.int32, (room, tok), 0)
    for first in range(0, len(blocks), group):
        hots = [jnp.where(slot_ref[...] == local + owner * room, 1.0, 0.0) for owner in owners[first:first + group]]
        hot = jnp.concatenate(hots, axis=0).astype(BF16)
        moved = jnp.dot(hot, value_ref[...], preferred_element_type=F32).astype(BF16)
        items = lax.dot_general(item_ref[...], hot, NT, preferred_element_type=F32)
        for index in range(group):
            span = slice(index * room, (index + 1) * room)
            block = blocks[first + index]
            block[pl.ds(0, room), :] = moved[span]
            block[pl.ds(room, EXTRA), :] = (extra + items[:, span]).astype(BF16)


def fill_all(slot_ref, item_ref, value_ref, out_ref, extra):
    owners = list(range(out_ref.shape[0]))
    fill_slots(slot_ref, item_ref, value_ref, [out_ref.at[owner] for owner in owners], owners, extra)


def slots_for(id_ref, rank_ref, slot_ref, item_ref, items, room):
    tok = id_ref.shape[1]
    ids = id_ref[...]
    owner = ids // items
    offset = ids - owner * items
    across = jnp.broadcast_to(owner.astype(F32), (8, tok)).T[:, :1]
    before = lax.broadcasted_iota(jnp.int32, (tok, tok), 0) < lax.broadcasted_iota(jnp.int32, (tok, tok), 1)
    same = jnp.where(before & (across == owner.astype(F32)), 1.0, 0.0)
    rank = jnp.sum(same, axis=0, keepdims=True).astype(jnp.int32)
    rank_ref[...] = rank
    slot_ref[...] = jnp.where(rank < room, owner * room + rank, -1)
    high = offset // 32
    row = lax.broadcasted_iota(jnp.int32, item_ref.shape, 0)
    rows = jnp.zeros(item_ref.shape, F32)
    for index, value in ((2, high + 1), (3, offset - high * 32), (5, rank // room + 1)):
        rows = jnp.where(row == index, jnp.broadcast_to(value.astype(F32), rows.shape), rows)
    item_ref[...] = rows.astype(BF16)


def input_grad_body(length_ref, *refs, items):
    parts = refs[:4]
    x_any, cot_any, gain_any, inv_rms_ref, id_ref, value_ref = refs[4:10]
    outs, (rank_ref, item_ref) = refs[10:14], refs[14:16]
    x_bf_ref, cot_ref, gain_ref, x_ref, slot_ref, sems = refs[16:]
    tok, col = x_ref.shape
    room = outs[0].shape[1] - EXTRA
    mine = pl.ds(pl.multiple_of(lax.axis_index("col") * col, col), col)
    copies = [
        pltpu.make_async_copy(source.at[:, mine], place, sems.at[n])
        for n, (source, place) in enumerate(((x_any, x_bf_ref), (cot_any, cot_ref), (gain_any, gain_ref)))
    ]
    for copy in copies:
        copy.start()
    slots_for(id_ref, rank_ref, slot_ref, item_ref, items, room)
    for copy in copies:
        copy.wait()
    x_ref[...] = x_bf_ref[...].astype(F32) * inv_rms_ref[...]
    first = lax.axis_index("seq") * tok
    d_normed = parts[0][pl.ds(0, tok), :].astype(F32)
    for part in parts[1:]:
        d_normed = d_normed + part[pl.ds(0, tok), :].astype(F32)
    gain_sum = two_rows(jnp.sum(d_normed * x_ref[...], axis=0, keepdims=True)).astype(F32)
    extra = [part[pl.ds(tok, EXTRA), :] for part in parts]
    row = lax.broadcasted_iota(jnp.int32, (EXTRA, col), 0)
    for tile in range(tok // BLOCK):
        rows = pl.ds(tile * BLOCK, BLOCK)
        pick = jnp.where((row >= 4 * tile) & (row < 4 * tile + 4), 1.0, 0.0).astype(BF16)
        mean = jnp.zeros((BLOCK, col), F32)
        for piece in extra:
            mean = mean + lax.dot_general(piece, pick, TN, preferred_element_type=F32)
        inv = inv_rms_ref[rows, :]
        d_t = d_normed[tile * BLOCK:(tile + 1) * BLOCK]
        mean = mean * inv * (1.0 / (8 * col))
        valid = lax.broadcasted_iota(jnp.int32, (BLOCK, 1), 0) + (first + tile * BLOCK) < length_ref[0]
        grad = jnp.where(valid, cot_ref[rows, :].astype(F32), 0.0)
        value = inv * (d_t * gain_ref[...] - x_ref[rows, :] * mean) + grad
        value_ref[rows, :] = value.astype(BF16)
    rounds = jnp.max(item_ref[pl.ds(5, 1), :].astype(F32), axis=1, keepdims=True)
    seq = lax.axis_index("seq")
    z_pos, x_pos = seq // 4 * 2 + lax.axis_index("dp"), lax.rem(seq, 4)
    spots = [(dx, dz) for dx in range(4) for dz in range(4)]
    owners = [plane_rank(lax.rem(z_pos + dz, 4), lax.rem(x_pos + dx, 4)) for dx, dz in spots]
    places = [outs[dx].at[dz] for dx, dz in spots]
    fill_slots(slot_ref, item_ref, value_ref, places, owners, gain_sum + jnp.where(row == 4, rounds, 0.0))


def input_grads(lengths, parts, x, cot, gain, inv_rms, ids, items, room):
    tok, col = inv_rms.shape
    whole, anywhere = pl.BlockSpec(memory_space=pltpu.VMEM), pl.BlockSpec(memory_space=pl.ANY)
    return kernel_call(
        functools.partial(input_grad_body, items=items),
        (
            shape_of((tok, col), BF16),
            *(shape_of((4, room + EXTRA, col), BF16) for _ in range(4)),
            shape_of((1, tok), jnp.int32),
            shape_of((EXTRA, tok), BF16),
        ),
        "input_grads",
        in_specs=[pl.BlockSpec(memory_space=pltpu.SMEM)] + [whole] * 4 + [anywhere] * 3 + [whole] * 2,
        scratch_shapes=[
            pltpu.VMEM((tok, col), BF16),
            pltpu.VMEM((tok, col), BF16),
            pltpu.VMEM((1, col), F32),
            pltpu.VMEM((tok, col), F32),
            pltpu.VMEM((1, tok), jnp.int32),
            pltpu.SemaphoreType.DMA((3,)),
        ],
    )(lengths, *parts, x, cot, gain.reshape(1, -1), inv_rms, ids)


def more_body(slot_ref, item_ref, value_ref, out_ref):
    fill_all(slot_ref, item_ref, value_ref, out_ref, 0.0)


def more_slots(slots, items, values, owners, room):
    col = values.shape[1]
    return kernel_call(more_body, shape_of((owners, room + EXTRA, col), BF16), "more_slots", vmem=63)(slots, items, values)


def rows_total(blocks, first, count):
    room = blocks[0].shape[0] - EXTRA
    total = jnp.zeros((count, blocks[0].shape[1]), F32)
    row = lax.broadcasted_iota(jnp.int32, (count, room), 0) + first
    for pair in range(0, len(blocks), 2):
        hots, data = [], []
        for block in blocks[pair:pair + 2]:
            extra = block[pl.ds(room, EXTRA), :].astype(F32)
            item = ((extra[2:3] - 1.0) * 32.0 + extra[3:4]).astype(jnp.int32)
            hots.append(jnp.where(item == row, 1.0, 0.0).astype(BF16))
            data.append(block[pl.ds(0, room), :])
        total = total + jnp.dot(
            jnp.concatenate(hots, axis=1), jnp.concatenate(data, axis=0), preferred_element_type=F32
        )
    return total


def finish_body(*refs):
    gots, whole_ref, (in_ref, out_ref, table_out, gain_ref, rounds_ref, table_ref, sems) = refs[:4], refs[4], refs[5:]
    step = pl.program_id(0)
    count, (_, rows, col) = table_ref.shape[1], whole_ref.shape
    share = rows // 5
    lasts = []
    for index in range(whole_ref.shape[0]):
        for c in range(4):
            in_ref[c, pl.ds(index * share, share), :] = whole_ref[index, pl.ds(c * share, share), :].astype(F32)
        lasts.append(whole_ref[index, pl.ds(4 * share, share), :].astype(F32))
    out_ref[...] = jnp.concatenate(lasts, axis=0).T
    blocks = [got.at[index] for got in gots for index in range(got.shape[0])]
    table_ref[step] = rows_total(blocks, step * count, count)

    def leaving(index):
        return pltpu.make_async_copy(table_ref.at[index], table_out.at[pl.ds(index * count, count)], sems.at[index])

    leaving(step).start()
    extra = [block[pl.ds(BLOCK, EXTRA), :].astype(F32) for block in blocks]
    total = functools.reduce(lambda a, b: a + b, extra)
    gain_ref[...] = total[0:1] + total[1:2]
    rounds_ref[0] = jnp.max(functools.reduce(jnp.maximum, extra)[4:5]).astype(jnp.int32)

    @pl.when(step == pl.num_programs(0) - 1)
    def _():
        for index in range(table_ref.shape[0]):
            leaving(index).wait()


def finish(gots, whole, items):
    owners, rows, col = whole.shape
    width, steps = 8 * col, 4
    return kernel_call(
        finish_body,
        (
            shape_of((4, width, col), F32),
            shape_of((col, width), F32),
            shape_of((items, col), F32),
            shape_of((1, col), F32),
            shape_of((1,), jnp.int32),
        ),
        "finish",
        grid=(steps,),
        in_specs=[pl.BlockSpec(got.shape, lambda i: (0, 0, 0)) for got in gots]
        + [pl.BlockSpec((owners // steps, rows, col), lambda i: (i, 0, 0))],
        out_specs=[
            pl.BlockSpec((4, width // steps, col), lambda i: (0, i, 0)),
            pl.BlockSpec((col, width // steps), lambda i: (0, i)),
            pl.BlockSpec(memory_space=pltpu.HBM),
            pl.BlockSpec((1, col), lambda i: (0, 0)),
            pl.BlockSpec(memory_space=pltpu.SMEM),
        ],
        scratch_shapes=[pltpu.VMEM((steps, items // steps, col), F32), pltpu.SemaphoreType.DMA((steps,))],
    )(*gots, whole)


def more_table_body(got_ref, table_ref, out_ref):
    count = 2 * BLOCK
    blocks = [got_ref.at[index] for index in range(got_ref.shape[0])]
    for first in range(0, table_ref.shape[0], count):
        rows = pl.ds(first, count)
        out_ref[rows, :] = table_ref[rows, :] + rows_total(blocks, first, count)


def more_table(got, table):
    return kernel_call(more_table_body, shape_of(table.shape, F32), "more_table", vmem=63)(got, table)


def per_device(inputs, cotangent, norm_gain, proj_in, proj_out, item_ids, lengths, tile_mask):
    x_rows, cot_rows = inputs[0], cotangent[0]
    mask = tile_mask[0]
    tok = x_rows.shape[0]
    col = proj_in.shape[2]
    scale = 1.0 / math.sqrt(col)
    owners, items, room = 16, 1024, BLOCK
    seq = lax.axis_index("seq")
    own, cross, near1, near2, near3, pre, dmix, upd, inv_cnt, inv_rms = project(
        lengths, x_rows, cot_rows, norm_gain, proj_in, proj_out, mask
    )

    across = move_seq(cross, 1, 0)
    near = [move_seq(block, 0, k) for block, k in ((near1, 1), (near3, 3), (near2, 2))]
    far = [move_seq(across, 0, k) for k in (1, 3, 2)]

    proj_peer = move_core(proj_in)
    x_now, cot_now, across = lax.optimization_barrier((x_rows, cot_rows, across))
    normed_t, grad_t = prepare(lengths, x_now, cot_now, norm_gain, inv_rms)
    acc, w_own, w_peer = near_terms(lengths, own, mask, proj_in, proj_peer, [across] + near, scale)
    d_own, shares = far_terms(
        lengths, own, mask, far, acc, pre, inv_rms, dmix, upd, inv_cnt, normed_t, grad_t, owners, scale
    )
    d_peer = move_core(d_own)
    shares = swap_plane(shares)
    parts = back_project(d_own, d_peer, w_own, w_peer, col)
    parts = [parts[0]] + [move_y(parts[k], k) for k in (1, 3, 2)]

    d_inputs, *sends, rank, item_rows = input_grads(
        lengths, parts, x_rows, cot_rows, norm_gain, inv_rms, item_ids, items, room
    )
    line = [sends[0]] + [move_plane(sends[k], 0, k) for k in (1, 3, 2)]
    sends = [jnp.stack([block[k] for block in line]) for k in range(4)]
    gots = [sends[0]] + [move_plane(sends[k], k, 0) for k in (1, 3, 2)]
    grad_in_w, grad_out_w, table, gain, rounds = finish(gots, swap_plane(weight_sum(shares)), items)

    def another(state):
        turn, total = state
        at = rank - turn * room
        slots = jnp.where((at >= 0) & (at < room), item_ids // items * room + at, -1)
        got = swap_plane(more_slots(slots, item_rows, d_inputs, owners, room))
        return turn + 1, more_table(got, total)

    _, table = lax.while_loop(lambda state: state[0] < rounds[0], another, (jnp.int32(1), table))
    return (grad_in_w, grad_out_w, gain[0], table)


def solution(mesh):
    placed = (
        P("dp", "seq", None),
        P("dp", "seq", None),
        P(),
        P(None, None, "col"),
        P("col", None),
        P("dp", "seq"),
        P("dp"),
        P("dp", None, None),
    )
    return jax.shard_map(
        per_device,
        mesh=mesh,
        in_specs=placed,
        out_specs=(P(None, None, "col"), P("col", None), P("col"), P(("dp", "seq"), "col")),
        check_vma=False,
    )
```

```python
import functools
import math

import jax
import jax.numpy as jnp
from jax import lax
from jax.experimental import pallas as pl
from jax.experimental.pallas import tpu as pltpu
from jax.sharding import PartitionSpec as P

BLOCK = 128
EPSILON = 1e-06
BF16 = jnp.bfloat16
F32 = jnp.float32
MIB = 1024 * 1024
EXTRA = 16
NT = (((1,), (1,)), ((), ()))
TN = (((0,), (0,)), ((), ()))


def kernel_call(body, out_shape, name, flops=1000, bytes_accessed=1000, vmem=24, **kwargs):
    return pl.pallas_call(
        body,
        out_shape=out_shape,
        name=name,
        compiler_params=pltpu.CompilerParams(vmem_limit_bytes=vmem * MIB),
        cost_estimate=pl.CostEstimate(flops=flops, bytes_accessed=bytes_accessed, transcendentals=0),
        **kwargs,
    )


def shape_of(shape, dtype):
    return jax.ShapeDtypeStruct(shape, dtype)


def swap_plane(value):
    return lax.all_to_all(value, ("dp", "seq"), 0, 0, tiled=True)


def plane_rank(z, x):
    return (z % 2) * 8 + (z // 2) * 4 + x


def move_plane(value, dz, dx):
    pairs = []
    for z in range(4):
        for x in range(4):
            pairs.append((plane_rank(z, x), plane_rank((z + dz) % 4, (x + dx) % 4)))
    return lax.ppermute(value, ("dp", "seq"), pairs)


def move_seq(value, dz_hi, dx):
    pairs = [(i, ((i // 4 + dz_hi) % 2) * 4 + (i % 4 + dx) % 4) for i in range(8)]
    return lax.ppermute(value, "seq", pairs)


def move_y(value, dy):
    return lax.ppermute(value, "col", [(i, ((i // 2 + dy) % 4) * 2 + i % 2) for i in range(8)])


def move_core(value):
    return lax.ppermute(value, "col", [(i, i ^ 1) for i in range(8)])


def project_body(length_ref, x_ref, cot_ref, gain_ref, proj_ref, out_ref, mask_ref,
                 own_ref, cross_ref, near1_ref, near2_ref, near3_ref, pre_ref, dmix_ref, upd_ref, inv_cnt_ref, inv_rms_ref, both_ref):
    length, rank = length_ref[0], lax.axis_index("seq")
    step, col = dmix_ref.shape

    @pl.when(pl.program_id(0) == 0)
    def _():
        for c in range(4):
            both_ref[:, pl.ds(c * col, col)] = proj_ref[c]

    x = x_ref[...].astype(F32)
    inv_rms = lax.rsqrt(jnp.mean(x * x, axis=1, keepdims=True) + EPSILON)
    normed = (x * inv_rms * gain_ref[...]).astype(BF16)
    inv_rms_ref[...] = jnp.broadcast_to(inv_rms, inv_rms_ref.shape)
    pre = jnp.dot(normed, both_ref[...], preferred_element_type=F32)
    act = (pre * jax.nn.sigmoid(pre)).astype(BF16)
    for c in range(4):
        pre_ref[c] = pre[:, c * col:(c + 1) * col]
    tile = (rank * pl.num_programs(0) + pl.program_id(0)) * (step // BLOCK)
    local = lax.broadcasted_iota(jnp.int32, (step, 1), 0)
    position = tile * BLOCK + local
    grad = jnp.where(position < length, cot_ref[...].astype(F32), 0.0).astype(BF16)
    d_mixed = lax.dot_general(grad, out_ref[...], NT, preferred_element_type=F32)
    dmix_ref[...] = d_mixed
    update = act[:, :col]
    upd_ref[...] = update
    tiles = mask_ref.shape[0]
    rows = lax.broadcasted_iota(jnp.int32, (tiles, tiles), 0)
    cols = lax.broadcasted_iota(jnp.int32, (tiles, tiles), 1)
    filled = jnp.clip(length - BLOCK * cols, 0, BLOCK)
    counted = jnp.where(cols < rows, mask_ref[...] * filled, 0)
    earlier = jnp.zeros((step, 1), F32)
    for index in range(step // BLOCK):
        picked = jnp.where(rows == tile + index, counted, 0).astype(F32)
        total = jnp.sum(jnp.sum(picked, axis=1, keepdims=True), axis=0, keepdims=True)
        earlier = jnp.where(local // BLOCK == index, total, earlier)
    own_first = tile * BLOCK + local // BLOCK * BLOCK
    diagonal = jnp.minimum(local % BLOCK + 1, jnp.clip(length - own_first, 0, BLOCK)).astype(F32)
    inv_cnt = 1.0 / jnp.maximum(earlier + diagonal, 1.0)
    inv_cnt_ref[...] = jnp.broadcast_to(inv_cnt, inv_cnt_ref.shape)
    qd = (act[:, col:2 * col], (d_mixed * update.astype(F32) * inv_cnt).astype(BF16))
    kv = (act[:, 2 * col:3 * col], act[:, 3 * col:])
    for index in range(2):
        own_ref[0, index], own_ref[1, index] = qd[index], kv[index]
    x_pos = lax.rem(rank, 4)
    later = [rank < 4] + [x_pos + k < 4 for k in (1, 2, 3)]
    for ref, is_later in zip((cross_ref, near1_ref, near2_ref, near3_ref), later):

        @pl.when(is_later)
        def _():
            ref[0], ref[1] = kv

        @pl.when(jnp.logical_not(is_later))
        def _():
            ref[0], ref[1] = qd


def project(lengths, x, cot, gain, proj_in, proj_out, mask):
    tok, width = x.shape
    col = proj_in.shape[2]
    step = 2 * BLOCK
    row = lambda i, w: (i, 0)
    side = lambda i, w: (0, i, 0)
    pair = lambda i, w: (0, 0, i, 0)
    fixed2 = lambda i, w: (0, 0)
    return kernel_call(
        project_body,
        (
            shape_of((2, 2, tok, col), BF16),
            *(shape_of((2, tok, col), BF16) for _ in range(4)),
            shape_of((4, tok, col), F32),
            shape_of((tok, col), F32),
            shape_of((tok, col), BF16),
            shape_of((tok, col), F32),
            shape_of((tok, col), F32),
        ),
        "project",
        vmem=63,
        grid_spec=pltpu.PrefetchScalarGridSpec(
            num_scalar_prefetch=1,
            grid=(tok // step,),
            in_specs=[
                pl.BlockSpec((step, width), row),
                pl.BlockSpec((step, width), row),
                pl.BlockSpec((1, width), fixed2),
                pl.BlockSpec((4, width, col), lambda i, w: (0, 0, 0)),
                pl.BlockSpec((col, width), fixed2),
                pl.BlockSpec(mask.shape, fixed2),
            ],
            out_specs=[
                pl.BlockSpec((2, 2, step, col), pair),
                *(pl.BlockSpec((2, step, col), side) for _ in range(4)),
                pl.BlockSpec((4, step, col), side),
                pl.BlockSpec((step, col), row),
                pl.BlockSpec((step, col), row),
                pl.BlockSpec((step, col), row),
                pl.BlockSpec((step, col), row),
            ],
            scratch_shapes=[pltpu.VMEM((width, 4 * col), BF16)],
        ),
    )(lengths, x, cot, gain.reshape(1, -1), proj_in, proj_out, mask)


def block_terms(a1, a2, b1, b2, keep, scale):
    half = lax.dot_general(a1, b1, NT, preferred_element_type=F32) * (keep * (0.5 * scale))
    other = lax.dot_general(a2, b2, NT, preferred_element_type=F32) * keep
    tanh = jnp.tanh(half)
    twice = 1.0 + tanh
    probs = half * twice
    slope = (other * (twice + probs * (1.0 - tanh))).astype(BF16)
    first = jnp.dot(probs.astype(BF16), b2, preferred_element_type=F32)
    second = jnp.dot(slope, b1, preferred_element_type=F32)
    return first, second


def block_sums(side, own_ref, other, keep_of, scale):
    tok, col = own_ref.shape[2:]
    part = 2 * BLOCK
    first, second = jnp.zeros((tok, col), F32), jnp.zeros((tok, col), F32)
    for start in range(0, tok, part):
        span = pl.ds(start, part)
        terms = block_terms(
            own_ref[side, 0], own_ref[side, 1], other[0][span, :], other[1][span, :], keep_of(start, part), scale
        )
        first, second = first + terms[0], second + terms[1]
    return first, second


def kept_tiles(mask_ref, length_ref, rank, tiles):
    count = mask_ref.shape[0]
    row = lax.broadcasted_iota(jnp.int32, (count, count), 0)
    column = lax.broadcasted_iota(jnp.int32, (count, count), 1)
    kept = jnp.where(column * BLOCK < length_ref[0], mask_ref[...].astype(F32), 0.0).astype(BF16)
    own = jnp.where(row + rank * tiles == column, 1.0, 0.0).astype(BF16)
    as_query = jnp.dot(own, kept, preferred_element_type=F32)
    as_key = lax.dot_general(own, kept, NT, preferred_element_type=F32)
    return as_query.astype(BF16), as_key.astype(BF16)


def keep_rows(kept, other, tiles, tok):
    count = kept.shape[0]
    row = lax.broadcasted_iota(jnp.int32, (count, tok), 0)
    column = lax.broadcasted_iota(jnp.int32, (count, tok), 1)
    spread = jnp.where(row == other * tiles + column // BLOCK, 1.0, 0.0).astype(BF16)
    return jnp.dot(kept, spread, preferred_element_type=F32)[:tiles]


def far_sums(other, rank, kept, own_ref, other_ref, scale):
    tok = own_ref.shape[2]
    tiles = tok // BLOCK
    side = jnp.where(other > rank, 1, 0)
    rows = jnp.where(other > rank, kept[1].astype(F32), kept[0].astype(F32)).astype(BF16)
    keep = keep_rows(rows, other, tiles, tok)

    def keep_of(start, part):
        return by_tile(keep[:, start:start + part], tok)

    return side, block_sums(side, own_ref, (other_ref.at[0], other_ref.at[1]), keep_of, scale)


def rank_at(rank, dz, dx):
    return lax.rem(rank // 4 + dz, 2) * 4 + lax.rem(rank + 4 - dx, 4)


def by_tile(rows, tok):
    tiles, part = rows.shape
    return jnp.broadcast_to(rows[:, None, :], (tiles, tok // tiles, part)).reshape(tok, part)


def near_body(length_ref, own_ref, mask_ref, proj_own_ref, proj_peer_ref, *refs, scale):
    others, (acc_ref, w_own_ref, w_peer_ref, sems) = refs[:-4], refs[-4:]
    tok, col = own_ref.shape[2:]
    place = lax.axis_index("col")
    picks = []
    for proj_ref, w_ref in ((proj_own_ref, w_own_ref), (proj_peer_ref, w_peer_ref)):
        for k in range(4):
            first = (lax.rem(place // 2 + k, 4) * 2 + lax.rem(place, 2)) * col
            rows = pl.ds(pl.multiple_of(first, col), col)
            for c in range(4):
                spot = w_ref.at[pl.ds(k * col, col), pl.ds(c * col, col)]
                picks.append(pltpu.make_async_copy(proj_ref.at[c, rows], spot, sems.at[len(picks)]))
    for pick in picks:
        pick.start()
    tiles = tok // BLOCK
    rank = lax.axis_index("seq")
    kept = kept_tiles(mask_ref, length_ref, rank, tiles)
    for side in range(2):
        other = own_ref.at[1 - side, 0], own_ref.at[1 - side, 1]
        rows = keep_rows(kept[side], rank, tiles, tok)

        def keep_of(start, part):
            row = lax.broadcasted_iota(jnp.int32, (tok, part), 0)
            column = lax.broadcasted_iota(jnp.int32, (tok, part), 1) + start
            ordered = (column <= row) if side == 0 else (row <= column)
            return jnp.where(ordered, by_tile(rows[:, start:start + part], tok), 0.0)

        acc_ref[side, 0], acc_ref[side, 1] = block_sums(side, own_ref, other, keep_of, scale)
    places = [(1, 0), (0, 1), (0, 3), (0, 2)]
    for (dz, dx), other in zip(places, others):
        side, sums = far_sums(rank_at(rank, dz, dx), rank, kept, own_ref, other, scale)
        acc_ref[side, 0] += sums[0]
        acc_ref[side, 1] += sums[1]
    for pick in picks:
        pick.wait()


def near_terms(lengths, own, mask, proj_own, proj_peer, others, scale):
    whole, anywhere = pl.BlockSpec(memory_space=pltpu.VMEM), pl.BlockSpec(memory_space=pl.ANY)
    depth = 4 * proj_own.shape[2]
    return kernel_call(
        functools.partial(near_body, scale=scale),
        (shape_of(own.shape, F32), shape_of((depth, depth), BF16), shape_of((depth, depth), BF16)),
        "near_terms",
        vmem=40,
        in_specs=[pl.BlockSpec(memory_space=pltpu.SMEM)] + [whole] * 2 + [anywhere] * 2 + [whole] * len(others),
        out_specs=[whole] * 3,
        scratch_shapes=[pltpu.SemaphoreType.DMA((32,))],
    )(lengths, own, mask, proj_own, proj_peer, *others)


FAR_INPUTS = 8


def far_body(length_ref, own_ref, mask_ref, *refs, scale):
    others, refs = refs[:3], refs[3:]
    sources, d_out, parts_out = refs[:FAR_INPUTS], refs[FAR_INPUTS], refs[FAR_INPUTS + 1]
    held = refs[FAR_INPUTS + 2:2 * FAR_INPUTS + 2]
    mixed_ref, d_ref, parts_ref, sems, out_sems = refs[2 * FAR_INPUTS + 2:]
    copies = [pltpu.make_async_copy(source, place, sems.at[n]) for n, (source, place) in enumerate(zip(sources, held))]
    for copy in copies:
        copy.start()
    rank = lax.axis_index("seq")
    acc_ref = held[0]
    pre_ref, inv_rms_ref, dmix_ref, upd_ref, inv_cnt_ref, normed_t_ref, grad_t_ref = held[1:]
    kept = kept_tiles(mask_ref, length_ref, rank, own_ref.shape[2] // BLOCK)
    for index, (dx, other) in enumerate(zip((1, 3, 2), others)):
        side, sums = far_sums(rank_at(rank, 1, dx), rank, kept, own_ref, other, scale)
        if index == 0:
            copies[0].wait()
        acc_ref[side, 0] += sums[0]
        acc_ref[side, 1] += sums[1]
    for copy in copies[1:6]:
        copy.wait()
    pre_grad_body(acc_ref, pre_ref, inv_rms_ref, dmix_ref, upd_ref, inv_cnt_ref, d_ref, mixed_ref, scale=scale)
    leaving = [pltpu.make_async_copy(d_ref, d_out, out_sems.at[0])]
    leaving[0].start()
    for copy in copies[6:]:
        copy.wait()
    half = parts_ref.shape[0] // 2
    for part in range(2):
        weight_body(part, normed_t_ref, grad_t_ref, d_ref, mixed_ref, parts_ref)
        owners = pl.ds(part * half, half)
        leaving.append(pltpu.make_async_copy(parts_ref.at[owners], parts_out.at[owners], out_sems.at[part + 1]))
        leaving[-1].start()
    for copy in leaving:
        copy.wait()


def far_terms(lengths, own, mask, others, acc, pre, inv_rms, dmix, upd, inv_cnt, normed_t, grad_t, owners, scale):
    _, _, tok, col = own.shape
    width = normed_t.shape[0]
    near_by = (own, mask, *others)
    sources = (acc, pre, inv_rms, dmix, upd, inv_cnt, normed_t, grad_t)
    return kernel_call(
        functools.partial(far_body, scale=scale),
        (shape_of((tok + EXTRA, 4 * col), BF16), shape_of((owners, 5 * width // owners, col), BF16)),
        "far_terms",
        vmem=40,
        in_specs=[pl.BlockSpec(memory_space=pltpu.SMEM)]
        + [pl.BlockSpec(memory_space=pltpu.VMEM)] * len(near_by)
        + [pl.BlockSpec(memory_space=pl.ANY)] * len(sources),
        out_specs=[pl.BlockSpec(memory_space=pl.ANY)] * 2,
        scratch_shapes=[
            *(pltpu.VMEM(source.shape, source.dtype) for source in sources),
            pltpu.VMEM((tok, col), BF16),
            pltpu.VMEM((tok + EXTRA, 4 * col), BF16),
            pltpu.VMEM((owners, 5 * width // owners, col), BF16),
            pltpu.SemaphoreType.DMA((len(sources),)),
            pltpu.SemaphoreType.DMA((3,)),
        ],
    )(lengths, *near_by, *sources)


def pre_grad_body(acc_ref, pre_ref, inv_rms_ref, dmix_ref, upd_ref, inv_cnt_ref, d_ref, mixed_ref, *, scale):
    tok, col = dmix_ref.shape
    stat = jnp.zeros((tok, col), F32)
    attended = acc_ref[0, 0] * inv_cnt_ref[...]
    mixed_ref[...] = (attended * upd_ref[...].astype(F32)).astype(BF16)
    grads = (
        dmix_ref[...] * attended,
        acc_ref[0, 1] * (0.5 * scale),
        acc_ref[1, 1] * (0.5 * scale),
        acc_ref[1, 0],
    )
    for c in range(4):
        pre = pre_ref[c]
        sig = jax.nn.sigmoid(pre)
        d_pre = (grads[c] * (sig * (1.0 + pre * (1.0 - sig)))).astype(BF16)
        d_ref[pl.ds(0, tok), pl.ds(c * col, col)] = d_pre
        stat = stat + d_pre.astype(F32) * pre
    stat = stat / inv_rms_ref[...]
    high = stat.astype(BF16)
    low = (stat - high.astype(F32)).astype(BF16)
    ones = jnp.ones((8, col), BF16)
    sums = lax.dot_general(ones, high, NT, preferred_element_type=F32)
    sums = sums + lax.dot_general(ones, low, NT, preferred_element_type=F32)
    d_ref[pl.ds(tok, EXTRA), :] = two_rows(sums[0:1])


def two_rows(value):
    high = value.astype(BF16).astype(F32)
    low = value - high
    row = lax.broadcasted_iota(jnp.int32, (EXTRA, value.shape[1]), 0)
    both = jnp.where(row == 0, jnp.broadcast_to(high, row.shape), jnp.where(row == 1, jnp.broadcast_to(low, row.shape), 0.0))
    return both.astype(BF16)


def back_body(own_ref, peer_ref, w_own_ref, w_peer_ref, *outs):
    tok = own_ref.shape[0] - EXTRA
    part = lax.dot_general(own_ref[pl.ds(0, tok), :], w_own_ref[...], NT, preferred_element_type=F32)
    part = part + lax.dot_general(peer_ref[pl.ds(0, tok), :], w_peer_ref[...], NT, preferred_element_type=F32)
    sums = jnp.sum(
        own_ref[pl.ds(tok, EXTRA), :].astype(F32) + peer_ref[pl.ds(tok, EXTRA), :].astype(F32), axis=0, keepdims=True
    )
    high = sums.astype(BF16).astype(F32)
    low = sums - high
    col = outs[0].shape[1]
    row = lax.broadcasted_iota(jnp.int32, (EXTRA, col), 0)
    extra = jnp.zeros((EXTRA, col), F32)
    for tile in range(tok // BLOCK):
        span = slice(tile * BLOCK, (tile + 1) * BLOCK)
        extra = jnp.where(row == 4 * tile, jnp.broadcast_to(high[:, span], row.shape), extra)
        extra = jnp.where(row == 4 * tile + 1, jnp.broadcast_to(low[:, span], row.shape), extra)
    extra = extra.astype(BF16)
    for k, out in enumerate(outs):
        out[pl.ds(0, tok), :] = part[:, k * col:(k + 1) * col].astype(BF16)
        out[pl.ds(tok, EXTRA), :] = extra


def back_project(own, peer, w_own, w_peer, col):
    rows, depth = own.shape
    return kernel_call(
        back_body,
        tuple(shape_of((rows, col), BF16) for _ in range(4)),
        "back_project",
    )(own, peer, w_own, w_peer)


def weight_body(part, normed_t_ref, grad_t_ref, d_ref, mixed_ref, out_ref):
    tok, col = mixed_ref.shape
    owners, share = out_ref.shape[0], out_ref.shape[1] // 5
    half = owners // 2
    rows = pl.ds(part * half * share, half * share)
    value = jnp.dot(normed_t_ref[rows, :], d_ref[pl.ds(0, tok), :], preferred_element_type=F32)
    last = jnp.dot(grad_t_ref[rows, :], mixed_ref[...], preferred_element_type=F32)
    for c in range(5):
        piece = value[:, c * col:(c + 1) * col] if c < 4 else last
        out_ref[pl.ds(part * half, half), pl.ds(c * share, share), :] = piece.astype(BF16).reshape(half, share, col)


def weight_sum_body(parts_ref, out_ref):
    total = parts_ref[0].astype(F32)
    for index in range(1, parts_ref.shape[0]):
        total = total + parts_ref[index].astype(F32)
    out_ref[...] = jnp.broadcast_to(total.astype(BF16)[None], out_ref.shape)


def weight_sum(parts):
    return kernel_call(weight_sum_body, shape_of(parts.shape, BF16), "weight_sum")(parts)


def prepare_body(length_ref, x_ref, cot_ref, gain_ref, inv_rms_ref, id_ref,
                 normed_t_ref, grad_t_ref, rank_ref, slot_ref, item_ref, *, items, room):
    step = x_ref.shape[0]
    normed = (x_ref[...].astype(F32) * inv_rms_ref[:, :1] * gain_ref[...]).astype(BF16)
    normed_t_ref[...] = normed.T
    first = (lax.axis_index("seq") * pl.num_programs(0) + pl.program_id(0)) * step
    valid = lax.broadcasted_iota(jnp.int32, (step, 1), 0) + first < length_ref[0]
    grad_t_ref[...] = jnp.where(valid, cot_ref[...].astype(F32), 0.0).astype(BF16).T

    @pl.when(pl.program_id(0) == 0)
    def _():
        slots_for(id_ref, rank_ref, slot_ref, item_ref, items, room)


def prepare(lengths, x, cot, gain, inv_rms, ids, items, room):
    tok, width = x.shape
    col = inv_rms.shape[1]
    step = tok // 4
    row = lambda i, n: (i, 0)
    column = lambda i, n: (0, i)
    return kernel_call(
        functools.partial(prepare_body, items=items, room=room),
        (
            shape_of((width, tok), BF16),
            shape_of((width, tok), BF16),
            shape_of((1, tok), jnp.int32),
            shape_of((1, tok), jnp.int32),
            shape_of((EXTRA, tok), BF16),
        ),
        "prepare",
        vmem=40,
        grid_spec=pltpu.PrefetchScalarGridSpec(
            num_scalar_prefetch=1,
            grid=(4,),
            in_specs=[
                pl.BlockSpec((step, width), row),
                pl.BlockSpec((step, width), row),
                pl.BlockSpec((1, width), lambda i, n: (0, 0)),
                pl.BlockSpec((step, col), row),
                pl.BlockSpec((1, tok), lambda i, n: (0, 0)),
            ],
            out_specs=[
                pl.BlockSpec((width, step), column),
                pl.BlockSpec((width, step), column),
                pl.BlockSpec((1, tok), lambda i, n: (0, 0)),
                pl.BlockSpec((1, tok), lambda i, n: (0, 0)),
                pl.BlockSpec((EXTRA, tok), lambda i, n: (0, 0)),
            ],
        ),
    )(lengths, x, cot, gain.reshape(1, -1), inv_rms, ids)


def fill_slots(slot_ref, item_ref, value_ref, blocks, owners, extra):
    room = blocks[0].shape[0] - EXTRA
    tok = slot_ref.shape[1]
    group = 4
    local = lax.broadcasted_iota(jnp.int32, (room, tok), 0)
    for first in range(0, len(blocks), group):
        hots = [jnp.where(slot_ref[...] == local + owner * room, 1.0, 0.0) for owner in owners[first:first + group]]
        hot = jnp.concatenate(hots, axis=0).astype(BF16)
        moved = jnp.dot(hot, value_ref[...], preferred_element_type=F32).astype(BF16)
        items = lax.dot_general(item_ref[...], hot, NT, preferred_element_type=F32)
        for index in range(group):
            span = slice(index * room, (index + 1) * room)
            block = blocks[first + index]
            block[pl.ds(0, room), :] = moved[span]
            block[pl.ds(room, EXTRA), :] = (extra + items[:, span]).astype(BF16)


def fill_all(slot_ref, item_ref, value_ref, out_ref, extra):
    owners = list(range(out_ref.shape[0]))
    fill_slots(slot_ref, item_ref, value_ref, [out_ref.at[owner] for owner in owners], owners, extra)


def slots_for(id_ref, rank_ref, slot_ref, item_ref, items, room):
    tok = id_ref.shape[1]
    ids = id_ref[...]
    owner = ids // items
    offset = ids - owner * items
    across = jnp.broadcast_to(owner.astype(F32), (8, tok)).T[:, :1]
    before = lax.broadcasted_iota(jnp.int32, (tok, tok), 0) < lax.broadcasted_iota(jnp.int32, (tok, tok), 1)
    same = jnp.where(before & (across == owner.astype(F32)), 1.0, 0.0)
    rank = jnp.sum(same, axis=0, keepdims=True).astype(jnp.int32)
    rank_ref[...] = rank
    slot_ref[...] = jnp.where(rank < room, owner * room + rank, -1)
    high = offset // 32
    row = lax.broadcasted_iota(jnp.int32, item_ref.shape, 0)
    rows = jnp.zeros(item_ref.shape, F32)
    for index, value in ((2, high + 1), (3, offset - high * 32), (5, rank // room + 1)):
        rows = jnp.where(row == index, jnp.broadcast_to(value.astype(F32), rows.shape), rows)
    item_ref[...] = rows.astype(BF16)


def input_grad_body(length_ref, *refs):
    parts = refs[:4]
    x_any, cot_any, gain_any, inv_rms_ref, slot_ref, item_ref, value_ref = refs[4:11]
    outs = refs[11:15]
    x_bf_ref, cot_ref, gain_ref, x_ref, sems = refs[15:]
    tok, col = x_ref.shape
    room = outs[0].shape[1] - EXTRA
    mine = pl.ds(pl.multiple_of(lax.axis_index("col") * col, col), col)
    copies = [
        pltpu.make_async_copy(source.at[:, mine], place, sems.at[n])
        for n, (source, place) in enumerate(((x_any, x_bf_ref), (cot_any, cot_ref), (gain_any, gain_ref)))
    ]
    for copy in copies:
        copy.start()
    for copy in copies:
        copy.wait()
    x_ref[...] = x_bf_ref[...].astype(F32) * inv_rms_ref[...]
    first = lax.axis_index("seq") * tok
    d_normed = parts[0][pl.ds(0, tok), :].astype(F32)
    for part in parts[1:]:
        d_normed = d_normed + part[pl.ds(0, tok), :].astype(F32)
    gain_sum = two_rows(jnp.sum(d_normed * x_ref[...], axis=0, keepdims=True)).astype(F32)
    extra = [part[pl.ds(tok, EXTRA), :] for part in parts]
    row = lax.broadcasted_iota(jnp.int32, (EXTRA, col), 0)
    for tile in range(tok // BLOCK):
        rows = pl.ds(tile * BLOCK, BLOCK)
        pick = jnp.where((row >= 4 * tile) & (row < 4 * tile + 4), 1.0, 0.0).astype(BF16)
        mean = jnp.zeros((BLOCK, col), F32)
        for piece in extra:
            mean = mean + lax.dot_general(piece, pick, TN, preferred_element_type=F32)
        inv = inv_rms_ref[rows, :]
        d_t = d_normed[tile * BLOCK:(tile + 1) * BLOCK]
        mean = mean * inv * (1.0 / (8 * col))
        valid = lax.broadcasted_iota(jnp.int32, (BLOCK, 1), 0) + (first + tile * BLOCK) < length_ref[0]
        grad = jnp.where(valid, cot_ref[rows, :].astype(F32), 0.0)
        value = inv * (d_t * gain_ref[...] - x_ref[rows, :] * mean) + grad
        value_ref[rows, :] = value.astype(BF16)
    rounds = jnp.max(item_ref[pl.ds(5, 1), :].astype(F32), axis=1, keepdims=True)
    seq = lax.axis_index("seq")
    z_pos, x_pos = seq // 4 * 2 + lax.axis_index("dp"), lax.rem(seq, 4)
    spots = [(dx, dz) for dx in range(4) for dz in range(4)]
    owners = [plane_rank(lax.rem(z_pos + dz, 4), lax.rem(x_pos + dx, 4)) for dx, dz in spots]
    places = [outs[dx].at[dz] for dx, dz in spots]
    fill_slots(slot_ref, item_ref, value_ref, places, owners, gain_sum + jnp.where(row == 4, rounds, 0.0))


def input_grads(lengths, parts, x, cot, gain, inv_rms, slots, item_rows, room):
    tok, col = inv_rms.shape
    whole, anywhere = pl.BlockSpec(memory_space=pltpu.VMEM), pl.BlockSpec(memory_space=pl.ANY)
    return kernel_call(
        input_grad_body,
        (
            shape_of((tok, col), BF16),
            *(shape_of((4, room + EXTRA, col), BF16) for _ in range(4)),
        ),
        "input_grads",
        in_specs=[pl.BlockSpec(memory_space=pltpu.SMEM)] + [whole] * 4 + [anywhere] * 3 + [whole] * 3,
        scratch_shapes=[
            pltpu.VMEM((tok, col), BF16),
            pltpu.VMEM((tok, col), BF16),
            pltpu.VMEM((1, col), F32),
            pltpu.VMEM((tok, col), F32),
            pltpu.SemaphoreType.DMA((3,)),
        ],
    )(lengths, *parts, x, cot, gain.reshape(1, -1), inv_rms, slots, item_rows)


def more_body(slot_ref, item_ref, value_ref, out_ref):
    fill_all(slot_ref, item_ref, value_ref, out_ref, 0.0)


def more_slots(slots, items, values, owners, room):
    col = values.shape[1]
    return kernel_call(more_body, shape_of((owners, room + EXTRA, col), BF16), "more_slots", vmem=63)(slots, items, values)


def rows_total(blocks, first, count):
    room = blocks[0].shape[0] - EXTRA
    total = jnp.zeros((count, blocks[0].shape[1]), F32)
    row = lax.broadcasted_iota(jnp.int32, (count, room), 0) + first
    for pair in range(0, len(blocks), 2):
        hots, data = [], []
        for block in blocks[pair:pair + 2]:
            extra = block[pl.ds(room, EXTRA), :].astype(F32)
            item = ((extra[2:3] - 1.0) * 32.0 + extra[3:4]).astype(jnp.int32)
            hots.append(jnp.where(item == row, 1.0, 0.0).astype(BF16))
            data.append(block[pl.ds(0, room), :])
        total = total + jnp.dot(
            jnp.concatenate(hots, axis=1), jnp.concatenate(data, axis=0), preferred_element_type=F32
        )
    return total


def finish_body(*refs):
    gots, whole_ref, (in_ref, out_ref, table_out, gain_ref, rounds_ref, table_ref, sems) = refs[:4], refs[4], refs[5:]
    step = pl.program_id(0)
    count, (_, rows, col) = table_ref.shape[1], whole_ref.shape
    share = rows // 5
    lasts = []
    for index in range(whole_ref.shape[0]):
        for c in range(4):
            in_ref[c, pl.ds(index * share, share), :] = whole_ref[index, pl.ds(c * share, share), :].astype(F32)
        lasts.append(whole_ref[index, pl.ds(4 * share, share), :].astype(F32))
    out_ref[...] = jnp.concatenate(lasts, axis=0).T
    blocks = [got.at[index] for got in gots for index in range(got.shape[0])]
    table_ref[step] = rows_total(blocks, step * count, count)

    def leaving(index):
        return pltpu.make_async_copy(table_ref.at[index], table_out.at[pl.ds(index * count, count)], sems.at[index])

    leaving(step).start()
    extra = [block[pl.ds(BLOCK, EXTRA), :].astype(F32) for block in blocks]
    total = functools.reduce(lambda a, b: a + b, extra)
    gain_ref[...] = total[0:1] + total[1:2]
    rounds_ref[0] = jnp.max(functools.reduce(jnp.maximum, extra)[4:5]).astype(jnp.int32)

    @pl.when(step == pl.num_programs(0) - 1)
    def _():
        for index in range(table_ref.shape[0]):
            leaving(index).wait()


def finish(gots, whole, items):
    owners, rows, col = whole.shape
    width, steps = 8 * col, 2
    return kernel_call(
        finish_body,
        (
            shape_of((4, width, col), F32),
            shape_of((col, width), F32),
            shape_of((items, col), F32),
            shape_of((1, col), F32),
            shape_of((1,), jnp.int32),
        ),
        "finish",
        grid=(steps,),
        in_specs=[pl.BlockSpec(got.shape, lambda i: (0, 0, 0)) for got in gots]
        + [pl.BlockSpec((owners // steps, rows, col), lambda i: (i, 0, 0))],
        out_specs=[
            pl.BlockSpec((4, width // steps, col), lambda i: (0, i, 0)),
            pl.BlockSpec((col, width // steps), lambda i: (0, i)),
            pl.BlockSpec(memory_space=pltpu.HBM),
            pl.BlockSpec((1, col), lambda i: (0, 0)),
            pl.BlockSpec(memory_space=pltpu.SMEM),
        ],
        scratch_shapes=[pltpu.VMEM((steps, items // steps, col), F32), pltpu.SemaphoreType.DMA((steps,))],
    )(*gots, whole)


def more_table_body(got_ref, table_ref, out_ref):
    count = 2 * BLOCK
    blocks = [got_ref.at[index] for index in range(got_ref.shape[0])]
    for first in range(0, table_ref.shape[0], count):
        rows = pl.ds(first, count)
        out_ref[rows, :] = table_ref[rows, :] + rows_total(blocks, first, count)


def more_table(got, table):
    return kernel_call(more_table_body, shape_of(table.shape, F32), "more_table", vmem=63)(got, table)


def per_device(inputs, cotangent, norm_gain, proj_in, proj_out, item_ids, lengths, tile_mask):
    x_rows, cot_rows = inputs[0], cotangent[0]
    mask = tile_mask[0]
    tok = x_rows.shape[0]
    col = proj_in.shape[2]
    scale = 1.0 / math.sqrt(col)
    owners, items, room = 16, 1024, BLOCK
    seq = lax.axis_index("seq")
    own, cross, near1, near2, near3, pre, dmix, upd, inv_cnt, inv_rms = project(
        lengths, x_rows, cot_rows, norm_gain, proj_in, proj_out, mask
    )

    across = move_seq(cross, 1, 0)
    near = [move_seq(block, 0, k) for block, k in ((near1, 1), (near3, 3), (near2, 2))]
    far = [move_seq(across, 0, k) for k in (1, 3, 2)]

    proj_peer = move_core(proj_in)
    x_now, cot_now, across = lax.optimization_barrier((x_rows, cot_rows, across))
    normed_t, grad_t, rank, slots, item_rows = prepare(
        lengths, x_now, cot_now, norm_gain, inv_rms, item_ids, items, room
    )
    acc, w_own, w_peer = near_terms(lengths, own, mask, proj_in, proj_peer, [across] + near, scale)
    d_own, shares = far_terms(
        lengths, own, mask, far, acc, pre, inv_rms, dmix, upd, inv_cnt, normed_t, grad_t, owners, scale
    )
    d_peer = move_core(d_own)
    shares = swap_plane(shares)
    parts = back_project(d_own, d_peer, w_own, w_peer, col)
    parts = [parts[0]] + [move_y(parts[k], k) for k in (1, 3, 2)]

    d_inputs, *sends = input_grads(lengths, parts, x_rows, cot_rows, norm_gain, inv_rms, slots, item_rows, room)
    line = [sends[0]] + [move_plane(sends[k], 0, k) for k in (1, 3, 2)]
    sends = [jnp.stack([block[k] for block in line]) for k in range(4)]
    gots = [sends[0]] + [move_plane(sends[k], k, 0) for k in (1, 3, 2)]
    grad_in_w, grad_out_w, table, gain, rounds = finish(gots, swap_plane(weight_sum(shares)), items)

    def another(state):
        turn, total = state
        at = rank - turn * room
        slots = jnp.where((at >= 0) & (at < room), item_ids // items * room + at, -1)
        got = swap_plane(more_slots(slots, item_rows, d_inputs, owners, room))
        return turn + 1, more_table(got, total)

    _, table = lax.while_loop(lambda state: state[0] < rounds[0], another, (jnp.int32(1), table))
    return (grad_in_w, grad_out_w, gain[0], table)


def solution(mesh):
    placed = (
        P("dp", "seq", None),
        P("dp", "seq", None),
        P(),
        P(None, None, "col"),
        P("col", None),
        P("dp", "seq"),
        P("dp"),
        P("dp", None, None),
    )
    return jax.shard_map(
        per_device,
        mesh=mesh,
        in_specs=placed,
        out_specs=(P(None, None, "col"), P("col", None), P("col"), P(("dp", "seq"), "col")),
        check_vma=False,
    )
```

```python
import functools
import math

import jax
import jax.numpy as jnp
from jax import lax
from jax.experimental import pallas as pl
from jax.experimental.pallas import tpu as pltpu
from jax.sharding import PartitionSpec as P

BLOCK = 128
EPSILON = 1e-06
BF16 = jnp.bfloat16
F32 = jnp.float32
MIB = 1024 * 1024
EXTRA = 16
NT = (((1,), (1,)), ((), ()))
TN = (((0,), (0,)), ((), ()))


def kernel_call(body, out_shape, name, flops=1000, bytes_accessed=1000, vmem=24, **kwargs):
    return pl.pallas_call(
        body,
        out_shape=out_shape,
        name=name,
        compiler_params=pltpu.CompilerParams(vmem_limit_bytes=vmem * MIB),
        cost_estimate=pl.CostEstimate(flops=flops, bytes_accessed=bytes_accessed, transcendentals=0),
        **kwargs,
    )


def shape_of(shape, dtype):
    return jax.ShapeDtypeStruct(shape, dtype)


def swap_plane(value):
    return lax.all_to_all(value, ("dp", "seq"), 0, 0, tiled=True)


def plane_rank(z, x):
    return (z % 2) * 8 + (z // 2) * 4 + x


def move_plane(value, dz, dx):
    pairs = []
    for z in range(4):
        for x in range(4):
            pairs.append((plane_rank(z, x), plane_rank((z + dz) % 4, (x + dx) % 4)))
    return lax.ppermute(value, ("dp", "seq"), pairs)


def move_seq(value, dz_hi, dx):
    pairs = [(i, ((i // 4 + dz_hi) % 2) * 4 + (i % 4 + dx) % 4) for i in range(8)]
    return lax.ppermute(value, "seq", pairs)


def move_y(value, dy):
    return lax.ppermute(value, "col", [(i, ((i // 2 + dy) % 4) * 2 + i % 2) for i in range(8)])


def move_core(value):
    return lax.ppermute(value, "col", [(i, i ^ 1) for i in range(8)])


def project_body(length_ref, x_ref, cot_ref, gain_ref, proj_ref, out_ref, mask_ref,
                 own_ref, cross_ref, near1_ref, near2_ref, near3_ref, pre_ref, dmix_ref, upd_ref, inv_cnt_ref, inv_rms_ref, both_ref):
    length, rank = length_ref[0], lax.axis_index("seq")
    step, col = dmix_ref.shape

    @pl.when(pl.program_id(0) == 0)
    def _():
        for c in range(4):
            both_ref[:, pl.ds(c * col, col)] = proj_ref[c]

    x = x_ref[...].astype(F32)
    inv_rms = lax.rsqrt(jnp.mean(x * x, axis=1, keepdims=True) + EPSILON)
    normed = (x * inv_rms * gain_ref[...]).astype(BF16)
    inv_rms_ref[...] = jnp.broadcast_to(inv_rms, inv_rms_ref.shape)
    pre = jnp.dot(normed, both_ref[...], preferred_element_type=F32)
    act = (pre * jax.nn.sigmoid(pre)).astype(BF16)
    for c in range(4):
        pre_ref[c] = pre[:, c * col:(c + 1) * col]
    tile = (rank * pl.num_programs(0) + pl.program_id(0)) * (step // BLOCK)
    local = lax.broadcasted_iota(jnp.int32, (step, 1), 0)
    position = tile * BLOCK + local
    grad = jnp.where(position < length, cot_ref[...].astype(F32), 0.0).astype(BF16)
    d_mixed = lax.dot_general(grad, out_ref[...], NT, preferred_element_type=F32)
    dmix_ref[...] = d_mixed
    update = act[:, :col]
    upd_ref[...] = update
    tiles = mask_ref.shape[0]
    rows = lax.broadcasted_iota(jnp.int32, (tiles, tiles), 0)
    cols = lax.broadcasted_iota(jnp.int32, (tiles, tiles), 1)
    filled = jnp.clip(length - BLOCK * cols, 0, BLOCK)
    counted = jnp.where(cols < rows, mask_ref[...] * filled, 0)
    earlier = jnp.zeros((step, 1), F32)
    for index in range(step // BLOCK):
        picked = jnp.where(rows == tile + index, counted, 0).astype(F32)
        total = jnp.sum(jnp.sum(picked, axis=1, keepdims=True), axis=0, keepdims=True)
        earlier = jnp.where(local // BLOCK == index, total, earlier)
    own_first = tile * BLOCK + local // BLOCK * BLOCK
    diagonal = jnp.minimum(local % BLOCK + 1, jnp.clip(length - own_first, 0, BLOCK)).astype(F32)
    inv_cnt = 1.0 / jnp.maximum(earlier + diagonal, 1.0)
    inv_cnt_ref[...] = jnp.broadcast_to(inv_cnt, inv_cnt_ref.shape)
    qd = (act[:, col:2 * col], (d_mixed * update.astype(F32) * inv_cnt).astype(BF16))
    kv = (act[:, 2 * col:3 * col], act[:, 3 * col:])
    for index in range(2):
        own_ref[0, index], own_ref[1, index] = qd[index], kv[index]
    x_pos = lax.rem(rank, 4)
    later = [rank < 4] + [x_pos + k < 4 for k in (1, 2, 3)]
    for ref, is_later in zip((cross_ref, near1_ref, near2_ref, near3_ref), later):

        @pl.when(is_later)
        def _():
            ref[0], ref[1] = kv

        @pl.when(jnp.logical_not(is_later))
        def _():
            ref[0], ref[1] = qd


def project(lengths, x, cot, gain, proj_in, proj_out, mask):
    tok, width = x.shape
    col = proj_in.shape[2]
    step = 2 * BLOCK
    row = lambda i, w: (i, 0)
    side = lambda i, w: (0, i, 0)
    pair = lambda i, w: (0, 0, i, 0)
    fixed2 = lambda i, w: (0, 0)
    return kernel_call(
        project_body,
        (
            shape_of((2, 2, tok, col), BF16),
            *(shape_of((2, tok, col), BF16) for _ in range(4)),
            shape_of((4, tok, col), F32),
            shape_of((tok, col), F32),
            shape_of((tok, col), BF16),
            shape_of((tok, col), F32),
            shape_of((tok, col), F32),
        ),
        "project",
        vmem=63,
        grid_spec=pltpu.PrefetchScalarGridSpec(
            num_scalar_prefetch=1,
            grid=(tok // step,),
            in_specs=[
                pl.BlockSpec((step, width), row),
                pl.BlockSpec((step, width), row),
                pl.BlockSpec((1, width), fixed2),
                pl.BlockSpec((4, width, col), lambda i, w: (0, 0, 0)),
                pl.BlockSpec((col, width), fixed2),
                pl.BlockSpec(mask.shape, fixed2),
            ],
            out_specs=[
                pl.BlockSpec((2, 2, step, col), pair),
                *(pl.BlockSpec((2, step, col), side) for _ in range(4)),
                pl.BlockSpec((4, step, col), side),
                pl.BlockSpec((step, col), row),
                pl.BlockSpec((step, col), row),
                pl.BlockSpec((step, col), row),
                pl.BlockSpec((step, col), row),
            ],
            scratch_shapes=[pltpu.VMEM((width, 4 * col), BF16)],
        ),
    )(lengths, x, cot, gain.reshape(1, -1), proj_in, proj_out, mask)


def block_terms(a1, a2, b1, b2, keep, scale):
    half = lax.dot_general(a1, b1, NT, preferred_element_type=F32) * (keep * (0.5 * scale))
    other = lax.dot_general(a2, b2, NT, preferred_element_type=F32) * keep
    tanh = jnp.tanh(half)
    twice = 1.0 + tanh
    probs = half * twice
    slope = (other * (twice + probs * (1.0 - tanh))).astype(BF16)
    first = jnp.dot(probs.astype(BF16), b2, preferred_element_type=F32)
    second = jnp.dot(slope, b1, preferred_element_type=F32)
    return first, second


def block_sums(side, own_ref, other, keep_of, scale):
    tok, col = own_ref.shape[2:]
    part = 2 * BLOCK
    first, second = jnp.zeros((tok, col), F32), jnp.zeros((tok, col), F32)
    for start in range(0, tok, part):
        span = pl.ds(start, part)
        terms = block_terms(
            own_ref[side, 0], own_ref[side, 1], other[0][span, :], other[1][span, :], keep_of(start, part), scale
        )
        first, second = first + terms[0], second + terms[1]
    return first, second


def kept_tiles(mask_ref, length_ref, rank, tiles):
    count = mask_ref.shape[0]
    row = lax.broadcasted_iota(jnp.int32, (count, count), 0)
    column = lax.broadcasted_iota(jnp.int32, (count, count), 1)
    kept = jnp.where(column * BLOCK < length_ref[0], mask_ref[...].astype(F32), 0.0).astype(BF16)
    own = jnp.where(row + rank * tiles == column, 1.0, 0.0).astype(BF16)
    as_query = jnp.dot(own, kept, preferred_element_type=F32)
    as_key = lax.dot_general(own, kept, NT, preferred_element_type=F32)
    return as_query.astype(BF16), as_key.astype(BF16)


def keep_rows(kept, other, tiles, tok):
    count = kept.shape[0]
    row = lax.broadcasted_iota(jnp.int32, (count, tok), 0)
    column = lax.broadcasted_iota(jnp.int32, (count, tok), 1)
    spread = jnp.where(row == other * tiles + column // BLOCK, 1.0, 0.0).astype(BF16)
    return jnp.dot(kept, spread, preferred_element_type=F32)[:tiles]


def far_sums(other, rank, kept, own_ref, other_ref, scale):
    tok = own_ref.shape[2]
    tiles = tok // BLOCK
    side = jnp.where(other > rank, 1, 0)
    rows = jnp.where(other > rank, kept[1].astype(F32), kept[0].astype(F32)).astype(BF16)
    keep = keep_rows(rows, other, tiles, tok)

    def keep_of(start, part):
        return by_tile(keep[:, start:start + part], tok)

    return side, block_sums(side, own_ref, (other_ref.at[0], other_ref.at[1]), keep_of, scale)


def rank_at(rank, dz, dx):
    return lax.rem(rank // 4 + dz, 2) * 4 + lax.rem(rank + 4 - dx, 4)


def by_tile(rows, tok):
    tiles, part = rows.shape
    return jnp.broadcast_to(rows[:, None, :], (tiles, tok // tiles, part)).reshape(tok, part)


def near_body(length_ref, own_ref, mask_ref, proj_own_ref, proj_peer_ref, *refs, scale):
    others, (acc_ref, w_own_ref, w_peer_ref, sems) = refs[:-4], refs[-4:]
    tok, col = own_ref.shape[2:]
    place = lax.axis_index("col")
    picks = []
    for proj_ref, w_ref in ((proj_own_ref, w_own_ref), (proj_peer_ref, w_peer_ref)):
        for k in range(4):
            first = (lax.rem(place // 2 + k, 4) * 2 + lax.rem(place, 2)) * col
            rows = pl.ds(pl.multiple_of(first, col), col)
            for c in range(4):
                spot = w_ref.at[pl.ds(k * col, col), pl.ds(c * col, col)]
                picks.append(pltpu.make_async_copy(proj_ref.at[c, rows], spot, sems.at[len(picks)]))
    for pick in picks:
        pick.start()
    tiles = tok // BLOCK
    rank = lax.axis_index("seq")
    kept = kept_tiles(mask_ref, length_ref, rank, tiles)
    for side in range(2):
        other = own_ref.at[1 - side, 0], own_ref.at[1 - side, 1]
        rows = keep_rows(kept[side], rank, tiles, tok)

        def keep_of(start, part):
            row = lax.broadcasted_iota(jnp.int32, (tok, part), 0)
            column = lax.broadcasted_iota(jnp.int32, (tok, part), 1) + start
            ordered = (column <= row) if side == 0 else (row <= column)
            return jnp.where(ordered, by_tile(rows[:, start:start + part], tok), 0.0)

        acc_ref[side, 0], acc_ref[side, 1] = block_sums(side, own_ref, other, keep_of, scale)
    places = [(1, 0), (0, 1), (0, 3), (0, 2)]
    for (dz, dx), other in zip(places, others):
        side, sums = far_sums(rank_at(rank, dz, dx), rank, kept, own_ref, other, scale)
        acc_ref[side, 0] += sums[0]
        acc_ref[side, 1] += sums[1]
    for pick in picks:
        pick.wait()


def near_terms(lengths, own, mask, proj_own, proj_peer, others, scale):
    whole, anywhere = pl.BlockSpec(memory_space=pltpu.VMEM), pl.BlockSpec(memory_space=pl.ANY)
    depth = 4 * proj_own.shape[2]
    return kernel_call(
        functools.partial(near_body, scale=scale),
        (shape_of(own.shape, F32), shape_of((depth, depth), BF16), shape_of((depth, depth), BF16)),
        "near_terms",
        vmem=40,
        in_specs=[pl.BlockSpec(memory_space=pltpu.SMEM)] + [whole] * 2 + [anywhere] * 2 + [whole] * len(others),
        out_specs=[whole] * 3,
        scratch_shapes=[pltpu.SemaphoreType.DMA((32,))],
    )(lengths, own, mask, proj_own, proj_peer, *others)


FAR_INPUTS = 8


def far_body(length_ref, own_ref, mask_ref, *refs, scale):
    others, refs = refs[:3], refs[3:]
    sources, d_out, parts_out = refs[:FAR_INPUTS], refs[FAR_INPUTS], refs[FAR_INPUTS + 1]
    held = refs[FAR_INPUTS + 2:2 * FAR_INPUTS + 2]
    mixed_ref, d_ref, parts_ref, sems, out_sems = refs[2 * FAR_INPUTS + 2:]
    copies = [pltpu.make_async_copy(source, place, sems.at[n]) for n, (source, place) in enumerate(zip(sources, held))]
    for copy in copies:
        copy.start()
    rank = lax.axis_index("seq")
    acc_ref = held[0]
    pre_ref, inv_rms_ref, dmix_ref, upd_ref, inv_cnt_ref, normed_t_ref, grad_t_ref = held[1:]
    kept = kept_tiles(mask_ref, length_ref, rank, own_ref.shape[2] // BLOCK)
    for index, (dx, other) in enumerate(zip((1, 3, 2), others)):
        side, sums = far_sums(rank_at(rank, 1, dx), rank, kept, own_ref, other, scale)
        if index == 0:
            copies[0].wait()
        acc_ref[side, 0] += sums[0]
        acc_ref[side, 1] += sums[1]
    for copy in copies[1:6]:
        copy.wait()
    pre_grad_body(acc_ref, pre_ref, inv_rms_ref, dmix_ref, upd_ref, inv_cnt_ref, d_ref, mixed_ref, scale=scale)
    leaving = [pltpu.make_async_copy(d_ref, d_out, out_sems.at[0])]
    leaving[0].start()
    for copy in copies[6:]:
        copy.wait()
    half = parts_ref.shape[0] // 2
    for part in range(2):
        weight_body(part, normed_t_ref, grad_t_ref, d_ref, mixed_ref, parts_ref)
        owners = pl.ds(part * half, half)
        leaving.append(pltpu.make_async_copy(parts_ref.at[owners], parts_out.at[owners], out_sems.at[part + 1]))
        leaving[-1].start()
    for copy in leaving:
        copy.wait()


def far_terms(lengths, own, mask, others, acc, pre, inv_rms, dmix, upd, inv_cnt, normed_t, grad_t, owners, scale):
    _, _, tok, col = own.shape
    width = normed_t.shape[0]
    near_by = (own, mask, *others)
    sources = (acc, pre, inv_rms, dmix, upd, inv_cnt, normed_t, grad_t)
    return kernel_call(
        functools.partial(far_body, scale=scale),
        (shape_of((tok + EXTRA, 4 * col), BF16), shape_of((owners, 5 * width // owners, col), BF16)),
        "far_terms",
        vmem=40,
        in_specs=[pl.BlockSpec(memory_space=pltpu.SMEM)]
        + [pl.BlockSpec(memory_space=pltpu.VMEM)] * len(near_by)
        + [pl.BlockSpec(memory_space=pl.ANY)] * len(sources),
        out_specs=[pl.BlockSpec(memory_space=pl.ANY)] * 2,
        scratch_shapes=[
            *(pltpu.VMEM(source.shape, source.dtype) for source in sources),
            pltpu.VMEM((tok, col), BF16),
            pltpu.VMEM((tok + EXTRA, 4 * col), BF16),
            pltpu.VMEM((owners, 5 * width // owners, col), BF16),
            pltpu.SemaphoreType.DMA((len(sources),)),
            pltpu.SemaphoreType.DMA((3,)),
        ],
    )(lengths, *near_by, *sources)


def pre_grad_body(acc_ref, pre_ref, inv_rms_ref, dmix_ref, upd_ref, inv_cnt_ref, d_ref, mixed_ref, *, scale):
    tok, col = dmix_ref.shape
    stat = jnp.zeros((tok, col), F32)
    attended = acc_ref[0, 0] * inv_cnt_ref[...]
    mixed_ref[...] = (attended * upd_ref[...].astype(F32)).astype(BF16)
    grads = (
        dmix_ref[...] * attended,
        acc_ref[0, 1] * (0.5 * scale),
        acc_ref[1, 1] * (0.5 * scale),
        acc_ref[1, 0],
    )
    for c in range(4):
        pre = pre_ref[c]
        sig = jax.nn.sigmoid(pre)
        d_pre = (grads[c] * (sig * (1.0 + pre * (1.0 - sig)))).astype(BF16)
        d_ref[pl.ds(0, tok), pl.ds(c * col, col)] = d_pre
        stat = stat + d_pre.astype(F32) * pre
    stat = stat / inv_rms_ref[...]
    high = stat.astype(BF16)
    low = (stat - high.astype(F32)).astype(BF16)
    ones = jnp.ones((8, col), BF16)
    sums = lax.dot_general(ones, high, NT, preferred_element_type=F32)
    sums = sums + lax.dot_general(ones, low, NT, preferred_element_type=F32)
    d_ref[pl.ds(tok, EXTRA), :] = two_rows(sums[0:1])


def two_rows(value):
    high = value.astype(BF16).astype(F32)
    low = value - high
    row = lax.broadcasted_iota(jnp.int32, (EXTRA, value.shape[1]), 0)
    both = jnp.where(row == 0, jnp.broadcast_to(high, row.shape), jnp.where(row == 1, jnp.broadcast_to(low, row.shape), 0.0))
    return both.astype(BF16)


def back_body(own_ref, peer_ref, w_own_ref, w_peer_ref, *outs):
    tok = own_ref.shape[0] - EXTRA
    part = lax.dot_general(own_ref[pl.ds(0, tok), :], w_own_ref[...], NT, preferred_element_type=F32)
    part = part + lax.dot_general(peer_ref[pl.ds(0, tok), :], w_peer_ref[...], NT, preferred_element_type=F32)
    sums = jnp.sum(
        own_ref[pl.ds(tok, EXTRA), :].astype(F32) + peer_ref[pl.ds(tok, EXTRA), :].astype(F32), axis=0, keepdims=True
    )
    high = sums.astype(BF16).astype(F32)
    low = sums - high
    col = outs[0].shape[1]
    row = lax.broadcasted_iota(jnp.int32, (EXTRA, col), 0)
    extra = jnp.zeros((EXTRA, col), F32)
    for tile in range(tok // BLOCK):
        span = slice(tile * BLOCK, (tile + 1) * BLOCK)
        extra = jnp.where(row == 4 * tile, jnp.broadcast_to(high[:, span], row.shape), extra)
        extra = jnp.where(row == 4 * tile + 1, jnp.broadcast_to(low[:, span], row.shape), extra)
    extra = extra.astype(BF16)
    for k, out in enumerate(outs):
        out[pl.ds(0, tok), :] = part[:, k * col:(k + 1) * col].astype(BF16)
        out[pl.ds(tok, EXTRA), :] = extra


def back_project(own, peer, w_own, w_peer, col):
    rows, depth = own.shape
    return kernel_call(
        back_body,
        tuple(shape_of((rows, col), BF16) for _ in range(4)),
        "back_project",
    )(own, peer, w_own, w_peer)


def weight_body(part, normed_t_ref, grad_t_ref, d_ref, mixed_ref, out_ref):
    tok, col = mixed_ref.shape
    owners, share = out_ref.shape[0], out_ref.shape[1] // 5
    half = owners // 2
    rows = pl.ds(part * half * share, half * share)
    value = jnp.dot(normed_t_ref[rows, :], d_ref[pl.ds(0, tok), :], preferred_element_type=F32)
    last = jnp.dot(grad_t_ref[rows, :], mixed_ref[...], preferred_element_type=F32)
    for c in range(5):
        piece = value[:, c * col:(c + 1) * col] if c < 4 else last
        out_ref[pl.ds(part * half, half), pl.ds(c * share, share), :] = piece.astype(BF16).reshape(half, share, col)


def weight_sum_body(parts_ref, out_ref):
    total = parts_ref[0].astype(F32)
    for index in range(1, parts_ref.shape[0]):
        total = total + parts_ref[index].astype(F32)
    out_ref[...] = jnp.broadcast_to(total.astype(BF16)[None], out_ref.shape)


def weight_sum(parts):
    return kernel_call(weight_sum_body, shape_of(parts.shape, BF16), "weight_sum")(parts)


def prepare_body(length_ref, x_ref, cot_ref, gain_ref, inv_rms_ref, id_ref,
                 normed_t_ref, grad_t_ref, rank_ref, slot_ref, item_ref, *, items, room):
    step = x_ref.shape[0]
    normed = (x_ref[...].astype(F32) * inv_rms_ref[:, :1] * gain_ref[...]).astype(BF16)
    normed_t_ref[...] = normed.T
    first = (lax.axis_index("seq") * pl.num_programs(0) + pl.program_id(0)) * step
    valid = lax.broadcasted_iota(jnp.int32, (step, 1), 0) + first < length_ref[0]
    grad_t_ref[...] = jnp.where(valid, cot_ref[...].astype(F32), 0.0).astype(BF16).T

    @pl.when(pl.program_id(0) == 0)
    def _():
        slots_for(id_ref, rank_ref, slot_ref, item_ref, items, room)


def prepare(lengths, x, cot, gain, inv_rms, ids, items, room):
    tok, width = x.shape
    col = inv_rms.shape[1]
    step = tok // 4
    row = lambda i, n: (i, 0)
    column = lambda i, n: (0, i)
    return kernel_call(
        functools.partial(prepare_body, items=items, room=room),
        (
            shape_of((width, tok), BF16),
            shape_of((width, tok), BF16),
            shape_of((1, tok), jnp.int32),
            shape_of((1, tok), jnp.int32),
            shape_of((EXTRA, tok), BF16),
        ),
        "prepare",
        vmem=40,
        grid_spec=pltpu.PrefetchScalarGridSpec(
            num_scalar_prefetch=1,
            grid=(4,),
            in_specs=[
                pl.BlockSpec((step, width), row),
                pl.BlockSpec((step, width), row),
                pl.BlockSpec((1, width), lambda i, n: (0, 0)),
                pl.BlockSpec((step, col), row),
                pl.BlockSpec((1, tok), lambda i, n: (0, 0)),
            ],
            out_specs=[
                pl.BlockSpec((width, step), column),
                pl.BlockSpec((width, step), column),
                pl.BlockSpec((1, tok), lambda i, n: (0, 0)),
                pl.BlockSpec((1, tok), lambda i, n: (0, 0)),
                pl.BlockSpec((EXTRA, tok), lambda i, n: (0, 0)),
            ],
        ),
    )(lengths, x, cot, gain.reshape(1, -1), inv_rms, ids)


def fill_slots(slot_ref, item_ref, value_ref, blocks, owners, extra):
    room = blocks[0].shape[0] - EXTRA
    tok = slot_ref.shape[1]
    group = 4
    local = lax.broadcasted_iota(jnp.int32, (room, tok), 0)
    for first in range(0, len(blocks), group):
        hots = [jnp.where(slot_ref[...] == local + owner * room, 1.0, 0.0) for owner in owners[first:first + group]]
        hot = jnp.concatenate(hots, axis=0).astype(BF16)
        moved = jnp.dot(hot, value_ref[...], preferred_element_type=F32).astype(BF16)
        items = lax.dot_general(item_ref[...], hot, NT, preferred_element_type=F32)
        for index in range(group):
            span = slice(index * room, (index + 1) * room)
            block = blocks[first + index]
            block[pl.ds(0, room), :] = moved[span]
            block[pl.ds(room, EXTRA), :] = (extra + items[:, span]).astype(BF16)


def fill_all(slot_ref, item_ref, value_ref, out_ref, extra):
    owners = list(range(out_ref.shape[0]))
    fill_slots(slot_ref, item_ref, value_ref, [out_ref.at[owner] for owner in owners], owners, extra)


def slots_for(id_ref, rank_ref, slot_ref, item_ref, items, room):
    tok = id_ref.shape[1]
    ids = id_ref[...]
    owner = ids // items
    offset = ids - owner * items
    across = jnp.broadcast_to(owner.astype(F32), (8, tok)).T[:, :1]
    before = lax.broadcasted_iota(jnp.int32, (tok, tok), 0) < lax.broadcasted_iota(jnp.int32, (tok, tok), 1)
    same = jnp.where(before & (across == owner.astype(F32)), 1.0, 0.0)
    rank = jnp.sum(same, axis=0, keepdims=True).astype(jnp.int32)
    rank_ref[...] = rank
    slot_ref[...] = jnp.where(rank < room, owner * room + rank, -1)
    high = offset // 32
    row = lax.broadcasted_iota(jnp.int32, item_ref.shape, 0)
    rows = jnp.zeros(item_ref.shape, F32)
    for index, value in ((2, high + 1), (3, offset - high * 32), (5, rank // room + 1)):
        rows = jnp.where(row == index, jnp.broadcast_to(value.astype(F32), rows.shape), rows)
    item_ref[...] = rows.astype(BF16)


def input_grad_body(length_ref, *refs):
    parts = refs[:4]
    x_any, cot_any, gain_any, inv_rms_ref, slot_ref, item_ref, value_ref = refs[4:11]
    outs = refs[11:15]
    x_bf_ref, cot_ref, gain_ref, x_ref, sems = refs[15:]
    tok, col = x_ref.shape
    room = outs[0].shape[1] - EXTRA
    mine = pl.ds(pl.multiple_of(lax.axis_index("col") * col, col), col)
    copies = [
        pltpu.make_async_copy(source.at[:, mine], place, sems.at[n])
        for n, (source, place) in enumerate(((x_any, x_bf_ref), (cot_any, cot_ref), (gain_any, gain_ref)))
    ]
    for copy in copies:
        copy.start()
    for copy in copies:
        copy.wait()
    x_ref[...] = x_bf_ref[...].astype(F32) * inv_rms_ref[...]
    first = lax.axis_index("seq") * tok
    d_normed = parts[0][pl.ds(0, tok), :].astype(F32)
    for part in parts[1:]:
        d_normed = d_normed + part[pl.ds(0, tok), :].astype(F32)
    gain_sum = two_rows(jnp.sum(d_normed * x_ref[...], axis=0, keepdims=True)).astype(F32)
    extra = [part[pl.ds(tok, EXTRA), :] for part in parts]
    row = lax.broadcasted_iota(jnp.int32, (EXTRA, col), 0)
    for tile in range(tok // BLOCK):
        rows = pl.ds(tile * BLOCK, BLOCK)
        pick = jnp.where((row >= 4 * tile) & (row < 4 * tile + 4), 1.0, 0.0).astype(BF16)
        mean = jnp.zeros((BLOCK, col), F32)
        for piece in extra:
            mean = mean + lax.dot_general(piece, pick, TN, preferred_element_type=F32)
        inv = inv_rms_ref[rows, :]
        d_t = d_normed[tile * BLOCK:(tile + 1) * BLOCK]
        mean = mean * inv * (1.0 / (8 * col))
        valid = lax.broadcasted_iota(jnp.int32, (BLOCK, 1), 0) + (first + tile * BLOCK) < length_ref[0]
        grad = jnp.where(valid, cot_ref[rows, :].astype(F32), 0.0)
        value = inv * (d_t * gain_ref[...] - x_ref[rows, :] * mean) + grad
        value_ref[rows, :] = value.astype(BF16)
    rounds = jnp.max(item_ref[pl.ds(5, 1), :].astype(F32), axis=1, keepdims=True)
    seq = lax.axis_index("seq")
    z_pos, x_pos = seq // 4 * 2 + lax.axis_index("dp"), lax.rem(seq, 4)
    spots = [(dx, dz) for dx in range(4) for dz in range(4)]
    owners = [plane_rank(lax.rem(z_pos + dz, 4), lax.rem(x_pos + dx, 4)) for dx, dz in spots]
    places = [outs[dx].at[dz] for dx, dz in spots]
    fill_slots(slot_ref, item_ref, value_ref, places, owners, gain_sum + jnp.where(row == 4, rounds, 0.0))


def input_grads(lengths, parts, x, cot, gain, inv_rms, slots, item_rows, room):
    tok, col = inv_rms.shape
    whole, anywhere = pl.BlockSpec(memory_space=pltpu.VMEM), pl.BlockSpec(memory_space=pl.ANY)
    return kernel_call(
        input_grad_body,
        (
            shape_of((tok, col), BF16),
            *(shape_of((4, room + EXTRA, col), BF16) for _ in range(4)),
        ),
        "input_grads",
        in_specs=[pl.BlockSpec(memory_space=pltpu.SMEM)] + [whole] * 4 + [anywhere] * 3 + [whole] * 3,
        scratch_shapes=[
            pltpu.VMEM((tok, col), BF16),
            pltpu.VMEM((tok, col), BF16),
            pltpu.VMEM((1, col), F32),
            pltpu.VMEM((tok, col), F32),
            pltpu.SemaphoreType.DMA((3,)),
        ],
    )(lengths, *parts, x, cot, gain.reshape(1, -1), inv_rms, slots, item_rows)


def more_body(slot_ref, item_ref, value_ref, out_ref):
    fill_all(slot_ref, item_ref, value_ref, out_ref, 0.0)


def more_slots(slots, items, values, owners, room):
    col = values.shape[1]
    return kernel_call(more_body, shape_of((owners, room + EXTRA, col), BF16), "more_slots", vmem=63)(slots, items, values)


def rows_total(blocks, first, count):
    room = blocks[0].shape[0] - EXTRA
    total = jnp.zeros((count, blocks[0].shape[1]), F32)
    row = lax.broadcasted_iota(jnp.int32, (count, room), 0) + first
    for pair in range(0, len(blocks), 2):
        hots, data = [], []
        for block in blocks[pair:pair + 2]:
            extra = block[pl.ds(room, EXTRA), :].astype(F32)
            item = ((extra[2:3] - 1.0) * 32.0 + extra[3:4]).astype(jnp.int32)
            hots.append(jnp.where(item == row, 1.0, 0.0).astype(BF16))
            data.append(block[pl.ds(0, room), :])
        total = total + jnp.dot(
            jnp.concatenate(hots, axis=1), jnp.concatenate(data, axis=0), preferred_element_type=F32
        )
    return total


def place_body(whole_ref, in_ref, out_ref):
    count, rows, col = whole_ref.shape
    share = rows // 5
    lasts = []
    for index in range(count):
        for c in range(4):
            in_ref[c, pl.ds(index * share, share), :] = whole_ref[index, pl.ds(c * share, share), :].astype(F32)
        lasts.append(whole_ref[index, pl.ds(4 * share, share), :].astype(F32))
    out_ref[...] = jnp.concatenate(lasts, axis=0).T


def place_weights(whole):
    owners, rows, col = whole.shape
    width, steps = 8 * col, 2
    return kernel_call(
        place_body,
        (shape_of((4, width, col), F32), shape_of((col, width), F32)),
        "place_weights",
        grid=(steps,),
        in_specs=[pl.BlockSpec((owners // steps, rows, col), lambda i: (i, 0, 0))],
        out_specs=[
            pl.BlockSpec((4, width // steps, col), lambda i: (0, i, 0)),
            pl.BlockSpec((col, width // steps), lambda i: (0, i)),
        ],
    )(whole)


def table_body(*refs):
    gots, (table_ref, gain_ref, rounds_ref) = refs[:4], refs[4:]
    count = 2 * BLOCK
    blocks = [got.at[index] for got in gots for index in range(got.shape[0])]
    for first in range(0, table_ref.shape[0], count):
        table_ref[pl.ds(first, count), :] = rows_total(blocks, first, count)
    extra = [block[pl.ds(BLOCK, EXTRA), :].astype(F32) for block in blocks]
    total = functools.reduce(lambda a, b: a + b, extra)
    gain_ref[...] = total[0:1] + total[1:2]
    rounds_ref[0] = jnp.max(functools.reduce(jnp.maximum, extra)[4:5]).astype(jnp.int32)


def table_grads(gots, items):
    col = gots[0].shape[2]
    whole = pl.BlockSpec(memory_space=pltpu.VMEM)
    return kernel_call(
        table_body,
        (shape_of((items, col), F32), shape_of((1, col), F32), shape_of((1,), jnp.int32)),
        "table_grads",
        out_specs=[whole, whole, pl.BlockSpec(memory_space=pltpu.SMEM)],
    )(*gots)


def more_table_body(got_ref, table_ref, out_ref):
    count = 2 * BLOCK
    blocks = [got_ref.at[index] for index in range(got_ref.shape[0])]
    for first in range(0, table_ref.shape[0], count):
        rows = pl.ds(first, count)
        out_ref[rows, :] = table_ref[rows, :] + rows_total(blocks, first, count)


def more_table(got, table):
    return kernel_call(more_table_body, shape_of(table.shape, F32), "more_table", vmem=63)(got, table)


def per_device(inputs, cotangent, norm_gain, proj_in, proj_out, item_ids, lengths, tile_mask):
    x_rows, cot_rows = inputs[0], cotangent[0]
    mask = tile_mask[0]
    tok = x_rows.shape[0]
    col = proj_in.shape[2]
    scale = 1.0 / math.sqrt(col)
    owners, items, room = 16, 1024, BLOCK
    seq = lax.axis_index("seq")
    own, cross, near1, near2, near3, pre, dmix, upd, inv_cnt, inv_rms = project(
        lengths, x_rows, cot_rows, norm_gain, proj_in, proj_out, mask
    )

    across = move_seq(cross, 1, 0)
    near = [move_seq(block, 0, k) for block, k in ((near1, 1), (near3, 3), (near2, 2))]
    far = [move_seq(across, 0, k) for k in (1, 3, 2)]

    proj_peer = move_core(proj_in)
    x_now, cot_now, across = lax.optimization_barrier((x_rows, cot_rows, across))
    normed_t, grad_t, rank, slots, item_rows = prepare(
        lengths, x_now, cot_now, norm_gain, inv_rms, item_ids, items, room
    )
    acc, w_own, w_peer = near_terms(lengths, own, mask, proj_in, proj_peer, [across] + near, scale)
    d_own, shares = far_terms(
        lengths, own, mask, far, acc, pre, inv_rms, dmix, upd, inv_cnt, normed_t, grad_t, owners, scale
    )
    d_peer = move_core(d_own)
    shares = swap_plane(shares)
    parts = back_project(d_own, d_peer, w_own, w_peer, col)
    parts = [parts[0]] + [move_y(parts[k], k) for k in (1, 3, 2)]

    d_inputs, *sends = input_grads(lengths, parts, x_rows, cot_rows, norm_gain, inv_rms, slots, item_rows, room)
    line = [sends[0]] + [move_plane(sends[k], 0, k) for k in (1, 3, 2)]
    sends = [jnp.stack([block[k] for block in line]) for k in range(4)]
    gots = [sends[0]] + [move_plane(sends[k], k, 0) for k in (1, 3, 2)]
    grad_in_w, grad_out_w = place_weights(swap_plane(weight_sum(shares)))
    grad_out_w, *gots = lax.optimization_barrier((grad_out_w, *gots))
    table, gain, rounds = table_grads(gots, items)

    def another(state):
        turn, total = state
        at = rank - turn * room
        slots = jnp.where((at >= 0) & (at < room), item_ids // items * room + at, -1)
        got = swap_plane(more_slots(slots, item_rows, d_inputs, owners, room))
        return turn + 1, more_table(got, total)

    _, table = lax.while_loop(lambda state: state[0] < rounds[0], another, (jnp.int32(1), table))
    return (grad_in_w, grad_out_w, gain[0], table)


def solution(mesh):
    placed = (
        P("dp", "seq", None),
        P("dp", "seq", None),
        P(),
        P(None, None, "col"),
        P("col", None),
        P("dp", "seq"),
        P("dp"),
        P("dp", None, None),
    )
    return jax.shard_map(
        per_device,
        mesh=mesh,
        in_specs=placed,
        out_specs=(P(None, None, "col"), P("col", None), P("col"), P(("dp", "seq"), "col")),
        check_vma=False,
    )
```

```python
import functools
import math

import jax
import jax.numpy as jnp
from jax import lax
from jax.experimental import pallas as pl
from jax.experimental.pallas import tpu as pltpu
from jax.sharding import PartitionSpec as P

BLOCK = 128
EPSILON = 1e-06
BF16 = jnp.bfloat16
F32 = jnp.float32
MIB = 1024 * 1024
EXTRA = 16
NT = (((1,), (1,)), ((), ()))
TN = (((0,), (0,)), ((), ()))


def kernel_call(body, out_shape, name, flops=1000, bytes_accessed=1000, vmem=24, **kwargs):
    return pl.pallas_call(
        body,
        out_shape=out_shape,
        name=name,
        compiler_params=pltpu.CompilerParams(vmem_limit_bytes=vmem * MIB),
        cost_estimate=pl.CostEstimate(flops=flops, bytes_accessed=bytes_accessed, transcendentals=0),
        **kwargs,
    )


def shape_of(shape, dtype):
    return jax.ShapeDtypeStruct(shape, dtype)


def swap_plane(value):
    return lax.all_to_all(value, ("dp", "seq"), 0, 0, tiled=True)


def plane_rank(z, x):
    return (z % 2) * 8 + (z // 2) * 4 + x


def move_plane(value, dz, dx):
    pairs = []
    for z in range(4):
        for x in range(4):
            pairs.append((plane_rank(z, x), plane_rank((z + dz) % 4, (x + dx) % 4)))
    return lax.ppermute(value, ("dp", "seq"), pairs)


def move_seq(value, dz_hi, dx):
    pairs = [(i, ((i // 4 + dz_hi) % 2) * 4 + (i % 4 + dx) % 4) for i in range(8)]
    return lax.ppermute(value, "seq", pairs)


def move_y(value, dy):
    return lax.ppermute(value, "col", [(i, ((i // 2 + dy) % 4) * 2 + i % 2) for i in range(8)])


def move_core(value):
    return lax.ppermute(value, "col", [(i, i ^ 1) for i in range(8)])


def project_body(length_ref, x_ref, cot_ref, gain_ref, proj_ref, out_ref, mask_ref,
                 own_ref, cross_ref, near1_ref, near2_ref, near3_ref, pre_ref, dmix_ref, upd_ref, inv_cnt_ref, inv_rms_ref, both_ref):
    length, rank = length_ref[0], lax.axis_index("seq")
    step, col = dmix_ref.shape

    @pl.when(pl.program_id(0) == 0)
    def _():
        for c in range(4):
            both_ref[:, pl.ds(c * col, col)] = proj_ref[c]

    x = x_ref[...].astype(F32)
    inv_rms = lax.rsqrt(jnp.mean(x * x, axis=1, keepdims=True) + EPSILON)
    normed = (x * inv_rms * gain_ref[...]).astype(BF16)
    inv_rms_ref[...] = jnp.broadcast_to(inv_rms, inv_rms_ref.shape)
    pre = jnp.dot(normed, both_ref[...], preferred_element_type=F32)
    act = (pre * jax.nn.sigmoid(pre)).astype(BF16)
    for c in range(4):
        pre_ref[c] = pre[:, c * col:(c + 1) * col]
    tile = (rank * pl.num_programs(0) + pl.program_id(0)) * (step // BLOCK)
    local = lax.broadcasted_iota(jnp.int32, (step, 1), 0)
    position = tile * BLOCK + local
    grad = jnp.where(position < length, cot_ref[...].astype(F32), 0.0).astype(BF16)
    d_mixed = lax.dot_general(grad, out_ref[...], NT, preferred_element_type=F32)
    dmix_ref[...] = d_mixed
    update = act[:, :col]
    upd_ref[...] = update
    tiles = mask_ref.shape[0]
    rows = lax.broadcasted_iota(jnp.int32, (tiles, tiles), 0)
    cols = lax.broadcasted_iota(jnp.int32, (tiles, tiles), 1)
    filled = jnp.clip(length - BLOCK * cols, 0, BLOCK)
    counted = jnp.where(cols < rows, mask_ref[...] * filled, 0)
    earlier = jnp.zeros((step, 1), F32)
    for index in range(step // BLOCK):
        picked = jnp.where(rows == tile + index, counted, 0).astype(F32)
        total = jnp.sum(jnp.sum(picked, axis=1, keepdims=True), axis=0, keepdims=True)
        earlier = jnp.where(local // BLOCK == index, total, earlier)
    own_first = tile * BLOCK + local // BLOCK * BLOCK
    diagonal = jnp.minimum(local % BLOCK + 1, jnp.clip(length - own_first, 0, BLOCK)).astype(F32)
    inv_cnt = 1.0 / jnp.maximum(earlier + diagonal, 1.0)
    inv_cnt_ref[...] = jnp.broadcast_to(inv_cnt, inv_cnt_ref.shape)
    qd = (act[:, col:2 * col], (d_mixed * update.astype(F32) * inv_cnt).astype(BF16))
    kv = (act[:, 2 * col:3 * col], act[:, 3 * col:])
    for index in range(2):
        own_ref[0, index], own_ref[1, index] = qd[index], kv[index]
    x_pos = lax.rem(rank, 4)
    later = [rank < 4] + [x_pos + k < 4 for k in (1, 2, 3)]
    for ref, is_later in zip((cross_ref, near1_ref, near2_ref, near3_ref), later):

        @pl.when(is_later)
        def _():
            ref[0], ref[1] = kv

        @pl.when(jnp.logical_not(is_later))
        def _():
            ref[0], ref[1] = qd


def project(lengths, x, cot, gain, proj_in, proj_out, mask):
    tok, width = x.shape
    col = proj_in.shape[2]
    step = 2 * BLOCK
    row = lambda i, w: (i, 0)
    side = lambda i, w: (0, i, 0)
    pair = lambda i, w: (0, 0, i, 0)
    fixed2 = lambda i, w: (0, 0)
    return kernel_call(
        project_body,
        (
            shape_of((2, 2, tok, col), BF16),
            *(shape_of((2, tok, col), BF16) for _ in range(4)),
            shape_of((4, tok, col), F32),
            shape_of((tok, col), F32),
            shape_of((tok, col), BF16),
            shape_of((tok, col), F32),
            shape_of((tok, col), F32),
        ),
        "project",
        vmem=63,
        grid_spec=pltpu.PrefetchScalarGridSpec(
            num_scalar_prefetch=1,
            grid=(tok // step,),
            in_specs=[
                pl.BlockSpec((step, width), row),
                pl.BlockSpec((step, width), row),
                pl.BlockSpec((1, width), fixed2),
                pl.BlockSpec((4, width, col), lambda i, w: (0, 0, 0)),
                pl.BlockSpec((col, width), fixed2),
                pl.BlockSpec(mask.shape, fixed2),
            ],
            out_specs=[
                pl.BlockSpec((2, 2, step, col), pair),
                *(pl.BlockSpec((2, step, col), side) for _ in range(4)),
                pl.BlockSpec((4, step, col), side),
                pl.BlockSpec((step, col), row),
                pl.BlockSpec((step, col), row),
                pl.BlockSpec((step, col), row),
                pl.BlockSpec((step, col), row),
            ],
            scratch_shapes=[pltpu.VMEM((width, 4 * col), BF16)],
        ),
    )(lengths, x, cot, gain.reshape(1, -1), proj_in, proj_out, mask)


def block_terms(a1, a2, b1, b2, keep, scale):
    half = lax.dot_general(a1, b1, NT, preferred_element_type=F32) * (keep * (0.5 * scale))
    other = lax.dot_general(a2, b2, NT, preferred_element_type=F32) * keep
    tanh = jnp.tanh(half)
    twice = 1.0 + tanh
    probs = half * twice
    slope = (other * (twice + probs * (1.0 - tanh))).astype(BF16)
    first = jnp.dot(probs.astype(BF16), b2, preferred_element_type=F32)
    second = jnp.dot(slope, b1, preferred_element_type=F32)
    return first, second


def block_sums(side, own_ref, other, keep_of, scale):
    tok, col = own_ref.shape[2:]
    part = 2 * BLOCK
    first, second = jnp.zeros((tok, col), F32), jnp.zeros((tok, col), F32)
    for start in range(0, tok, part):
        span = pl.ds(start, part)
        terms = block_terms(
            own_ref[side, 0], own_ref[side, 1], other[0][span, :], other[1][span, :], keep_of(start, part), scale
        )
        first, second = first + terms[0], second + terms[1]
    return first, second


def kept_tiles(mask_ref, length_ref, rank, tiles):
    count = mask_ref.shape[0]
    row = lax.broadcasted_iota(jnp.int32, (count, count), 0)
    column = lax.broadcasted_iota(jnp.int32, (count, count), 1)
    kept = jnp.where(column * BLOCK < length_ref[0], mask_ref[...].astype(F32), 0.0).astype(BF16)
    own = jnp.where(row + rank * tiles == column, 1.0, 0.0).astype(BF16)
    as_query = jnp.dot(own, kept, preferred_element_type=F32)
    as_key = lax.dot_general(own, kept, NT, preferred_element_type=F32)
    return as_query.astype(BF16), as_key.astype(BF16)


def keep_rows(kept, other, tiles, tok):
    count = kept.shape[0]
    row = lax.broadcasted_iota(jnp.int32, (count, tok), 0)
    column = lax.broadcasted_iota(jnp.int32, (count, tok), 1)
    spread = jnp.where(row == other * tiles + column // BLOCK, 1.0, 0.0).astype(BF16)
    return jnp.dot(kept, spread, preferred_element_type=F32)[:tiles]


def far_sums(other, rank, kept, own_ref, other_ref, scale):
    tok = own_ref.shape[2]
    tiles = tok // BLOCK
    side = jnp.where(other > rank, 1, 0)
    rows = jnp.where(other > rank, kept[1].astype(F32), kept[0].astype(F32)).astype(BF16)
    keep = keep_rows(rows, other, tiles, tok)

    def keep_of(start, part):
        return by_tile(keep[:, start:start + part], tok)

    return side, block_sums(side, own_ref, (other_ref.at[0], other_ref.at[1]), keep_of, scale)


def rank_at(rank, dz, dx):
    return lax.rem(rank // 4 + dz, 2) * 4 + lax.rem(rank + 4 - dx, 4)


def by_tile(rows, tok):
    tiles, part = rows.shape
    return jnp.broadcast_to(rows[:, None, :], (tiles, tok // tiles, part)).reshape(tok, part)


def near_body(length_ref, own_ref, mask_ref, proj_own_ref, proj_peer_ref, *refs, scale):
    others, (acc_ref, w_own_ref, w_peer_ref, sems) = refs[:-4], refs[-4:]
    tok, col = own_ref.shape[2:]
    place = lax.axis_index("col")
    picks = []
    for proj_ref, w_ref in ((proj_own_ref, w_own_ref), (proj_peer_ref, w_peer_ref)):
        for k in range(4):
            first = (lax.rem(place // 2 + k, 4) * 2 + lax.rem(place, 2)) * col
            rows = pl.ds(pl.multiple_of(first, col), col)
            for c in range(4):
                spot = w_ref.at[pl.ds(k * col, col), pl.ds(c * col, col)]
                picks.append(pltpu.make_async_copy(proj_ref.at[c, rows], spot, sems.at[len(picks)]))
    for pick in picks:
        pick.start()
    tiles = tok // BLOCK
    rank = lax.axis_index("seq")
    kept = kept_tiles(mask_ref, length_ref, rank, tiles)
    for side in range(2):
        other = own_ref.at[1 - side, 0], own_ref.at[1 - side, 1]
        rows = keep_rows(kept[side], rank, tiles, tok)

        def keep_of(start, part):
            row = lax.broadcasted_iota(jnp.int32, (tok, part), 0)
            column = lax.broadcasted_iota(jnp.int32, (tok, part), 1) + start
            ordered = (column <= row) if side == 0 else (row <= column)
            return jnp.where(ordered, by_tile(rows[:, start:start + part], tok), 0.0)

        acc_ref[side, 0], acc_ref[side, 1] = block_sums(side, own_ref, other, keep_of, scale)
    places = [(1, 0), (0, 1), (0, 3), (0, 2)]
    for (dz, dx), other in zip(places, others):
        side, sums = far_sums(rank_at(rank, dz, dx), rank, kept, own_ref, other, scale)
        acc_ref[side, 0] += sums[0]
        acc_ref[side, 1] += sums[1]
    for pick in picks:
        pick.wait()


def near_terms(lengths, own, mask, proj_own, proj_peer, others, scale):
    whole, anywhere = pl.BlockSpec(memory_space=pltpu.VMEM), pl.BlockSpec(memory_space=pl.ANY)
    depth = 4 * proj_own.shape[2]
    return kernel_call(
        functools.partial(near_body, scale=scale),
        (shape_of(own.shape, F32), shape_of((depth, depth), BF16), shape_of((depth, depth), BF16)),
        "near_terms",
        vmem=40,
        in_specs=[pl.BlockSpec(memory_space=pltpu.SMEM)] + [whole] * 2 + [anywhere] * 2 + [whole] * len(others),
        out_specs=[whole] * 3,
        scratch_shapes=[pltpu.SemaphoreType.DMA((32,))],
    )(lengths, own, mask, proj_own, proj_peer, *others)


FAR_INPUTS = 8


def far_body(length_ref, own_ref, mask_ref, *refs, scale):
    others, refs = refs[:3], refs[3:]
    sources, d_out, parts_out = refs[:FAR_INPUTS], refs[FAR_INPUTS], refs[FAR_INPUTS + 1]
    held = refs[FAR_INPUTS + 2:2 * FAR_INPUTS + 2]
    mixed_ref, d_ref, parts_ref, sems, out_sems = refs[2 * FAR_INPUTS + 2:]
    copies = [pltpu.make_async_copy(source, place, sems.at[n]) for n, (source, place) in enumerate(zip(sources, held))]
    for copy in copies:
        copy.start()
    rank = lax.axis_index("seq")
    acc_ref = held[0]
    pre_ref, inv_rms_ref, dmix_ref, upd_ref, inv_cnt_ref, normed_t_ref, grad_t_ref = held[1:]
    kept = kept_tiles(mask_ref, length_ref, rank, own_ref.shape[2] // BLOCK)
    for index, (dx, other) in enumerate(zip((1, 3, 2), others)):
        side, sums = far_sums(rank_at(rank, 1, dx), rank, kept, own_ref, other, scale)
        if index == 0:
            copies[0].wait()
        acc_ref[side, 0] += sums[0]
        acc_ref[side, 1] += sums[1]
    for copy in copies[1:6]:
        copy.wait()
    pre_grad_body(acc_ref, pre_ref, inv_rms_ref, dmix_ref, upd_ref, inv_cnt_ref, d_ref, mixed_ref, scale=scale)
    leaving = [pltpu.make_async_copy(d_ref, d_out, out_sems.at[0])]
    leaving[0].start()
    for copy in copies[6:]:
        copy.wait()
    half = parts_ref.shape[0] // 2
    for part in range(2):
        weight_body(part, normed_t_ref, grad_t_ref, d_ref, mixed_ref, parts_ref)
        owners = pl.ds(part * half, half)
        leaving.append(pltpu.make_async_copy(parts_ref.at[owners], parts_out.at[owners], out_sems.at[part + 1]))
        leaving[-1].start()
    for copy in leaving:
        copy.wait()


def far_terms(lengths, own, mask, others, acc, pre, inv_rms, dmix, upd, inv_cnt, normed_t, grad_t, owners, scale):
    _, _, tok, col = own.shape
    width = normed_t.shape[0]
    near_by = (own, mask, *others)
    sources = (acc, pre, inv_rms, dmix, upd, inv_cnt, normed_t, grad_t)
    return kernel_call(
        functools.partial(far_body, scale=scale),
        (shape_of((tok + EXTRA, 4 * col), BF16), shape_of((owners, 5 * width // owners, col), BF16)),
        "far_terms",
        vmem=40,
        in_specs=[pl.BlockSpec(memory_space=pltpu.SMEM)]
        + [pl.BlockSpec(memory_space=pltpu.VMEM)] * len(near_by)
        + [pl.BlockSpec(memory_space=pl.ANY)] * len(sources),
        out_specs=[pl.BlockSpec(memory_space=pl.ANY)] * 2,
        scratch_shapes=[
            *(pltpu.VMEM(source.shape, source.dtype) for source in sources),
            pltpu.VMEM((tok, col), BF16),
            pltpu.VMEM((tok + EXTRA, 4 * col), BF16),
            pltpu.VMEM((owners, 5 * width // owners, col), BF16),
            pltpu.SemaphoreType.DMA((len(sources),)),
            pltpu.SemaphoreType.DMA((3,)),
        ],
    )(lengths, *near_by, *sources)


def pre_grad_body(acc_ref, pre_ref, inv_rms_ref, dmix_ref, upd_ref, inv_cnt_ref, d_ref, mixed_ref, *, scale):
    tok, col = dmix_ref.shape
    stat = jnp.zeros((tok, col), F32)
    attended = acc_ref[0, 0] * inv_cnt_ref[...]
    mixed_ref[...] = (attended * upd_ref[...].astype(F32)).astype(BF16)
    grads = (
        dmix_ref[...] * attended,
        acc_ref[0, 1] * (0.5 * scale),
        acc_ref[1, 1] * (0.5 * scale),
        acc_ref[1, 0],
    )
    for c in range(4):
        pre = pre_ref[c]
        sig = jax.nn.sigmoid(pre)
        d_pre = (grads[c] * (sig * (1.0 + pre * (1.0 - sig)))).astype(BF16)
        d_ref[pl.ds(0, tok), pl.ds(c * col, col)] = d_pre
        stat = stat + d_pre.astype(F32) * pre
    stat = stat / inv_rms_ref[...]
    high = stat.astype(BF16)
    low = (stat - high.astype(F32)).astype(BF16)
    ones = jnp.ones((8, col), BF16)
    sums = lax.dot_general(ones, high, NT, preferred_element_type=F32)
    sums = sums + lax.dot_general(ones, low, NT, preferred_element_type=F32)
    d_ref[pl.ds(tok, EXTRA), :] = two_rows(sums[0:1])


def two_rows(value):
    high = value.astype(BF16).astype(F32)
    low = value - high
    row = lax.broadcasted_iota(jnp.int32, (EXTRA, value.shape[1]), 0)
    both = jnp.where(row == 0, jnp.broadcast_to(high, row.shape), jnp.where(row == 1, jnp.broadcast_to(low, row.shape), 0.0))
    return both.astype(BF16)


def back_body(own_ref, peer_ref, w_own_ref, w_peer_ref, *outs):
    tok = own_ref.shape[0] - EXTRA
    part = lax.dot_general(own_ref[pl.ds(0, tok), :], w_own_ref[...], NT, preferred_element_type=F32)
    part = part + lax.dot_general(peer_ref[pl.ds(0, tok), :], w_peer_ref[...], NT, preferred_element_type=F32)
    sums = jnp.sum(
        own_ref[pl.ds(tok, EXTRA), :].astype(F32) + peer_ref[pl.ds(tok, EXTRA), :].astype(F32), axis=0, keepdims=True
    )
    high = sums.astype(BF16).astype(F32)
    low = sums - high
    col = outs[0].shape[1]
    row = lax.broadcasted_iota(jnp.int32, (EXTRA, col), 0)
    extra = jnp.zeros((EXTRA, col), F32)
    for tile in range(tok // BLOCK):
        span = slice(tile * BLOCK, (tile + 1) * BLOCK)
        extra = jnp.where(row == 4 * tile, jnp.broadcast_to(high[:, span], row.shape), extra)
        extra = jnp.where(row == 4 * tile + 1, jnp.broadcast_to(low[:, span], row.shape), extra)
    extra = extra.astype(BF16)
    for k, out in enumerate(outs):
        out[pl.ds(0, tok), :] = part[:, k * col:(k + 1) * col].astype(BF16)
        out[pl.ds(tok, EXTRA), :] = extra


def back_project(own, peer, w_own, w_peer, col):
    rows, depth = own.shape
    return kernel_call(
        back_body,
        tuple(shape_of((rows, col), BF16) for _ in range(4)),
        "back_project",
    )(own, peer, w_own, w_peer)


def weight_body(part, normed_t_ref, grad_t_ref, d_ref, mixed_ref, out_ref):
    tok, col = mixed_ref.shape
    owners, share = out_ref.shape[0], out_ref.shape[1] // 5
    half = owners // 2
    rows = pl.ds(part * half * share, half * share)
    value = jnp.dot(normed_t_ref[rows, :], d_ref[pl.ds(0, tok), :], preferred_element_type=F32)
    last = jnp.dot(grad_t_ref[rows, :], mixed_ref[...], preferred_element_type=F32)
    for c in range(5):
        piece = value[:, c * col:(c + 1) * col] if c < 4 else last
        out_ref[pl.ds(part * half, half), pl.ds(c * share, share), :] = piece.astype(BF16).reshape(half, share, col)


def weight_sum_body(parts_ref, out_ref):
    total = parts_ref[0].astype(F32)
    for index in range(1, parts_ref.shape[0]):
        total = total + parts_ref[index].astype(F32)
    out_ref[...] = jnp.broadcast_to(total.astype(BF16)[None], out_ref.shape)


def weight_sum(parts):
    return kernel_call(weight_sum_body, shape_of(parts.shape, BF16), "weight_sum")(parts)


def prepare_body(length_ref, x_ref, cot_ref, gain_ref, inv_rms_ref, id_ref,
                 normed_t_ref, grad_t_ref, rank_ref, slot_ref, item_ref, *, items, room):
    step = x_ref.shape[0]
    normed = (x_ref[...].astype(F32) * inv_rms_ref[:, :1] * gain_ref[...]).astype(BF16)
    normed_t_ref[...] = normed.T
    first = (lax.axis_index("seq") * pl.num_programs(0) + pl.program_id(0)) * step
    valid = lax.broadcasted_iota(jnp.int32, (step, 1), 0) + first < length_ref[0]
    grad_t_ref[...] = jnp.where(valid, cot_ref[...].astype(F32), 0.0).astype(BF16).T

    @pl.when(pl.program_id(0) == 0)
    def _():
        slots_for(id_ref, rank_ref, slot_ref, item_ref, items, room)


def prepare(lengths, x, cot, gain, inv_rms, ids, items, room):
    tok, width = x.shape
    col = inv_rms.shape[1]
    step = tok // 4
    row = lambda i, n: (i, 0)
    column = lambda i, n: (0, i)
    return kernel_call(
        functools.partial(prepare_body, items=items, room=room),
        (
            shape_of((width, tok), BF16),
            shape_of((width, tok), BF16),
            shape_of((1, tok), jnp.int32),
            shape_of((1, tok), jnp.int32),
            shape_of((EXTRA, tok), BF16),
        ),
        "prepare",
        vmem=40,
        grid_spec=pltpu.PrefetchScalarGridSpec(
            num_scalar_prefetch=1,
            grid=(4,),
            in_specs=[
                pl.BlockSpec((step, width), row),
                pl.BlockSpec((step, width), row),
                pl.BlockSpec((1, width), lambda i, n: (0, 0)),
                pl.BlockSpec((step, col), row),
                pl.BlockSpec((1, tok), lambda i, n: (0, 0)),
            ],
            out_specs=[
                pl.BlockSpec((width, step), column),
                pl.BlockSpec((width, step), column),
                pl.BlockSpec((1, tok), lambda i, n: (0, 0)),
                pl.BlockSpec((1, tok), lambda i, n: (0, 0)),
                pl.BlockSpec((EXTRA, tok), lambda i, n: (0, 0)),
            ],
        ),
    )(lengths, x, cot, gain.reshape(1, -1), inv_rms, ids)


def fill_slots(slot_ref, item_ref, value_ref, blocks, owners, extra):
    room = blocks[0].shape[0] - EXTRA
    tok = slot_ref.shape[1]
    group = 4
    local = lax.broadcasted_iota(jnp.int32, (room, tok), 0)
    for first in range(0, len(blocks), group):
        hots = [jnp.where(slot_ref[...] == local + owner * room, 1.0, 0.0) for owner in owners[first:first + group]]
        hot = jnp.concatenate(hots, axis=0).astype(BF16)
        moved = jnp.dot(hot, value_ref[...], preferred_element_type=F32).astype(BF16)
        items = lax.dot_general(item_ref[...], hot, NT, preferred_element_type=F32)
        for index in range(group):
            span = slice(index * room, (index + 1) * room)
            block = blocks[first + index]
            block[pl.ds(0, room), :] = moved[span]
            block[pl.ds(room, EXTRA), :] = (extra + items[:, span]).astype(BF16)


def fill_all(slot_ref, item_ref, value_ref, out_ref, extra):
    owners = list(range(out_ref.shape[0]))
    fill_slots(slot_ref, item_ref, value_ref, [out_ref.at[owner] for owner in owners], owners, extra)


def slots_for(id_ref, rank_ref, slot_ref, item_ref, items, room):
    tok = id_ref.shape[1]
    ids = id_ref[...]
    owner = ids // items
    offset = ids - owner * items
    across = jnp.broadcast_to(owner.astype(F32), (8, tok)).T[:, :1]
    before = lax.broadcasted_iota(jnp.int32, (tok, tok), 0) < lax.broadcasted_iota(jnp.int32, (tok, tok), 1)
    same = jnp.where(before & (across == owner.astype(F32)), 1.0, 0.0)
    rank = jnp.sum(same, axis=0, keepdims=True).astype(jnp.int32)
    rank_ref[...] = rank
    slot_ref[...] = jnp.where(rank < room, owner * room + rank, -1)
    high = offset // 32
    row = lax.broadcasted_iota(jnp.int32, item_ref.shape, 0)
    rows = jnp.zeros(item_ref.shape, F32)
    for index, value in ((2, high + 1), (3, offset - high * 32), (5, rank // room + 1)):
        rows = jnp.where(row == index, jnp.broadcast_to(value.astype(F32), rows.shape), rows)
    item_ref[...] = rows.astype(BF16)


def input_grad_body(length_ref, *refs):
    parts = refs[:4]
    x_any, cot_any, gain_any, inv_rms_ref, slot_ref, item_ref, value_ref = refs[4:11]
    outs = refs[11:15]
    x_bf_ref, cot_ref, gain_ref, x_ref, sems = refs[15:]
    tok, col = x_ref.shape
    room = outs[0].shape[1] - EXTRA
    mine = pl.ds(pl.multiple_of(lax.axis_index("col") * col, col), col)
    copies = [
        pltpu.make_async_copy(source.at[:, mine], place, sems.at[n])
        for n, (source, place) in enumerate(((x_any, x_bf_ref), (cot_any, cot_ref), (gain_any, gain_ref)))
    ]
    for copy in copies:
        copy.start()
    for copy in copies:
        copy.wait()
    x_ref[...] = x_bf_ref[...].astype(F32) * inv_rms_ref[...]
    first = lax.axis_index("seq") * tok
    d_normed = parts[0][pl.ds(0, tok), :].astype(F32)
    for part in parts[1:]:
        d_normed = d_normed + part[pl.ds(0, tok), :].astype(F32)
    gain_sum = two_rows(jnp.sum(d_normed * x_ref[...], axis=0, keepdims=True)).astype(F32)
    extra = [part[pl.ds(tok, EXTRA), :] for part in parts]
    row = lax.broadcasted_iota(jnp.int32, (EXTRA, col), 0)
    for tile in range(tok // BLOCK):
        rows = pl.ds(tile * BLOCK, BLOCK)
        pick = jnp.where((row >= 4 * tile) & (row < 4 * tile + 4), 1.0, 0.0).astype(BF16)
        mean = jnp.zeros((BLOCK, col), F32)
        for piece in extra:
            mean = mean + lax.dot_general(piece, pick, TN, preferred_element_type=F32)
        inv = inv_rms_ref[rows, :]
        d_t = d_normed[tile * BLOCK:(tile + 1) * BLOCK]
        mean = mean * inv * (1.0 / (8 * col))
        valid = lax.broadcasted_iota(jnp.int32, (BLOCK, 1), 0) + (first + tile * BLOCK) < length_ref[0]
        grad = jnp.where(valid, cot_ref[rows, :].astype(F32), 0.0)
        value = inv * (d_t * gain_ref[...] - x_ref[rows, :] * mean) + grad
        value_ref[rows, :] = value.astype(BF16)
    rounds = jnp.max(item_ref[pl.ds(5, 1), :].astype(F32), axis=1, keepdims=True)
    seq = lax.axis_index("seq")
    z_pos, x_pos = seq // 4 * 2 + lax.axis_index("dp"), lax.rem(seq, 4)
    spots = [(dx, dz) for dx in range(4) for dz in range(4)]
    owners = [plane_rank(lax.rem(z_pos + dz, 4), lax.rem(x_pos + dx, 4)) for dx, dz in spots]
    places = [outs[dx].at[dz] for dx, dz in spots]
    fill_slots(slot_ref, item_ref, value_ref, places, owners, gain_sum + jnp.where(row == 4, rounds, 0.0))


def input_grads(lengths, parts, x, cot, gain, inv_rms, slots, item_rows, room):
    tok, col = inv_rms.shape
    whole, anywhere = pl.BlockSpec(memory_space=pltpu.VMEM), pl.BlockSpec(memory_space=pl.ANY)
    return kernel_call(
        input_grad_body,
        (
            shape_of((tok, col), BF16),
            *(shape_of((4, room + EXTRA, col), BF16) for _ in range(4)),
        ),
        "input_grads",
        in_specs=[pl.BlockSpec(memory_space=pltpu.SMEM)] + [whole] * 4 + [anywhere] * 3 + [whole] * 3,
        scratch_shapes=[
            pltpu.VMEM((tok, col), BF16),
            pltpu.VMEM((tok, col), BF16),
            pltpu.VMEM((1, col), F32),
            pltpu.VMEM((tok, col), F32),
            pltpu.SemaphoreType.DMA((3,)),
        ],
    )(lengths, *parts, x, cot, gain.reshape(1, -1), inv_rms, slots, item_rows)


def more_body(slot_ref, item_ref, value_ref, out_ref):
    fill_all(slot_ref, item_ref, value_ref, out_ref, 0.0)


def more_slots(slots, items, values, owners, room):
    col = values.shape[1]
    return kernel_call(more_body, shape_of((owners, room + EXTRA, col), BF16), "more_slots", vmem=63)(slots, items, values)


def rows_total(blocks, first, count):
    room = blocks[0].shape[0] - EXTRA
    total = jnp.zeros((count, blocks[0].shape[1]), F32)
    row = lax.broadcasted_iota(jnp.int32, (count, room), 0) + first
    for pair in range(0, len(blocks), 2):
        hots, data = [], []
        for block in blocks[pair:pair + 2]:
            extra = block[pl.ds(room, EXTRA), :].astype(F32)
            item = ((extra[2:3] - 1.0) * 32.0 + extra[3:4]).astype(jnp.int32)
            hots.append(jnp.where(item == row, 1.0, 0.0).astype(BF16))
            data.append(block[pl.ds(0, room), :])
        total = total + jnp.dot(
            jnp.concatenate(hots, axis=1), jnp.concatenate(data, axis=0), preferred_element_type=F32
        )
    return total


def place_body(whole_ref, in_ref, out_ref):
    count, rows, col = whole_ref.shape
    share = rows // 5
    lasts = []
    for index in range(count):
        for c in range(4):
            in_ref[c, pl.ds(index * share, share), :] = whole_ref[index, pl.ds(c * share, share), :].astype(F32)
        lasts.append(whole_ref[index, pl.ds(4 * share, share), :].astype(F32))
    out_ref[...] = jnp.concatenate(lasts, axis=0).T


def place_weights(whole):
    owners, rows, col = whole.shape
    width, steps = 8 * col, 2
    return kernel_call(
        place_body,
        (shape_of((4, width, col), F32), shape_of((col, width), F32)),
        "place_weights",
        grid=(steps,),
        in_specs=[pl.BlockSpec((owners // steps, rows, col), lambda i: (i, 0, 0))],
        out_specs=[
            pl.BlockSpec((4, width // steps, col), lambda i: (0, i, 0)),
            pl.BlockSpec((col, width // steps), lambda i: (0, i)),
        ],
    )(whole)


def table_body(*refs):
    gots, (table_ref, gain_ref, rounds_ref) = refs[:4], refs[4:]
    count = 2 * BLOCK
    blocks = [got.at[index] for got in gots for index in range(got.shape[0])]
    for first in range(0, table_ref.shape[0], count):
        table_ref[pl.ds(first, count), :] = rows_total(blocks, first, count)
    extra = [block[pl.ds(BLOCK, EXTRA), :].astype(F32) for block in blocks]
    total = functools.reduce(lambda a, b: a + b, extra)
    gain_ref[...] = total[0:1] + total[1:2]
    rounds_ref[0] = jnp.max(functools.reduce(jnp.maximum, extra)[4:5]).astype(jnp.int32)


def table_grads(gots, items):
    col = gots[0].shape[2]
    whole = pl.BlockSpec(memory_space=pltpu.VMEM)
    return kernel_call(
        table_body,
        (shape_of((items, col), F32), shape_of((1, col), F32), shape_of((1,), jnp.int32)),
        "table_grads",
        out_specs=[whole, whole, pl.BlockSpec(memory_space=pltpu.SMEM)],
    )(*gots)


def more_table_body(got_ref, table_ref, out_ref):
    count = 2 * BLOCK
    blocks = [got_ref.at[index] for index in range(got_ref.shape[0])]
    for first in range(0, table_ref.shape[0], count):
        rows = pl.ds(first, count)
        out_ref[rows, :] = table_ref[rows, :] + rows_total(blocks, first, count)


def more_table(got, table):
    return kernel_call(more_table_body, shape_of(table.shape, F32), "more_table", vmem=63)(got, table)


def per_device(inputs, cotangent, norm_gain, proj_in, proj_out, item_ids, lengths, tile_mask):
    x_rows, cot_rows = inputs[0], cotangent[0]
    mask = tile_mask[0]
    tok = x_rows.shape[0]
    col = proj_in.shape[2]
    scale = 1.0 / math.sqrt(col)
    owners, items, room = 16, 1024, BLOCK
    seq = lax.axis_index("seq")
    own, cross, near1, near2, near3, pre, dmix, upd, inv_cnt, inv_rms = project(
        lengths, x_rows, cot_rows, norm_gain, proj_in, proj_out, mask
    )

    across = move_seq(cross, 1, 0)
    near = [move_seq(block, 0, k) for block, k in ((near1, 1), (near3, 3), (near2, 2))]
    far = [move_seq(across, 0, k) for k in (1, 3, 2)]

    proj_peer = move_core(proj_in)
    x_now, cot_now, across = lax.optimization_barrier((x_rows, cot_rows, across))
    normed_t, grad_t, rank, slots, item_rows = prepare(
        lengths, x_now, cot_now, norm_gain, inv_rms, item_ids, items, room
    )
    acc, w_own, w_peer = near_terms(lengths, own, mask, proj_in, proj_peer, [across] + near, scale)
    d_own, shares = far_terms(
        lengths, own, mask, far, acc, pre, inv_rms, dmix, upd, inv_cnt, normed_t, grad_t, owners, scale
    )
    d_peer = move_core(d_own)
    shares = swap_plane(shares)
    parts = back_project(d_own, d_peer, w_own, w_peer, col)
    parts = [parts[0]] + [move_y(parts[k], k) for k in (2, 1, 3)]

    d_inputs, *sends = input_grads(lengths, parts, x_rows, cot_rows, norm_gain, inv_rms, slots, item_rows, room)
    line = [sends[0]] + [move_plane(sends[k], 0, k) for k in (2, 1, 3)]
    sends = [jnp.stack([block[k] for block in line]) for k in range(4)]
    gots = [sends[0]] + [move_plane(sends[k], k, 0) for k in (1, 3, 2)]
    grad_in_w, grad_out_w = place_weights(swap_plane(weight_sum(shares)))
    grad_out_w, *gots = lax.optimization_barrier((grad_out_w, *gots))
    table, gain, rounds = table_grads(gots, items)

    def another(state):
        turn, total = state
        at = rank - turn * room
        slots = jnp.where((at >= 0) & (at < room), item_ids // items * room + at, -1)
        got = swap_plane(more_slots(slots, item_rows, d_inputs, owners, room))
        return turn + 1, more_table(got, total)

    _, table = lax.while_loop(lambda state: state[0] < rounds[0], another, (jnp.int32(1), table))
    return (grad_in_w, grad_out_w, gain[0], table)


def solution(mesh):
    placed = (
        P("dp", "seq", None),
        P("dp", "seq", None),
        P(),
        P(None, None, "col"),
        P("col", None),
        P("dp", "seq"),
        P("dp"),
        P("dp", None, None),
    )
    return jax.shard_map(
        per_device,
        mesh=mesh,
        in_specs=placed,
        out_specs=(P(None, None, "col"), P("col", None), P("col"), P(("dp", "seq"), "col")),
        check_vma=False,
    )
```
